512 devices in a mesh: ctx: 16 (over x, y_hi), fsdp: 32 (over z, y_lo, core).
Axes of the slice: x: 4, y: 8 (y_hi: 4, y_lo: 2; y = y_hi * 2 + y_lo), z: 8, core: 2. Of those that a mesh axis runs over, the one named last changes fastest.
Arguments:
- queries: bfloat16 [2048, 12288], P('ctx', 'fsdp'), may hold values from -200 to 200, as said below
- keys: bfloat16 [2048, 12288], P('ctx', 'fsdp'), may hold values from -200 to 200, as said below
- values: bfloat16 [2048, 12288], P('ctx', 'fsdp'), may hold values from -6 to 6
- query_tangent: bfloat16 [2048, 12288], P('ctx', 'fsdp'), may hold values from -6 to 6
- key_tangent: bfloat16 [2048, 12288], P('ctx', 'fsdp'), may hold values from -6 to 6
- value_tangent: bfloat16 [2048, 12288], P('ctx', 'fsdp'), may hold values from -6 to 6
- query_gain: float32 [3072], P('fsdp'), may hold values from 0.5 to 1.5
- key_gain: float32 [3072], P('fsdp'), may hold values from 0.5 to 1.5
- time_index: int32 [4], replicated, may hold values from 0 to 999
- shard_order: int32 [16], P('ctx'), may hold values from 0 to 15, each once
Outputs:
- query_grad: bfloat16 [2048, 12288], P('ctx', 'fsdp')
- key_grad: bfloat16 [2048, 12288], P('ctx', 'fsdp')
- value_grad: bfloat16 [2048, 12288], P('ctx', 'fsdp')
- query_gain_grad: float32 [3072], P('fsdp')
- key_gain_grad: float32 [3072], P('fsdp')
The draws below stay inside these ranges and needn't reach their ends.
Inputs may be any that keep to these rules, and one draw needn't show every extreme that they name: `queries`: each sample's channels hold 24 heads of 128 channels in order. `keys`: laid out as the queries. `shard_order`: each block index appears once.
All inputs are finite; a program needn't handle non-finite values.
Results may differ from the reference program's by a relative error of at most 0.024.
Values may be sent and summed in bfloat16 or wider, within the bound.
A program may use at most 64 MiB of HBM per device.

```python
import math
import jax
import jax.numpy as jnp
from jax import lax

TOK_DEV = 128
HD = 128
STEPS = 1000
HEADS = 24
CHANNELS = 3072
SAMPLES = 4
SEQ = 2048
N_CTX = 16


def drawn_pair(key):
    width_all = SAMPLES * CHANNELS
    query_base = jax.random.truncated_normal(jax.random.fold_in(key, 101), -6.0, 6.0, (SEQ, width_all), jnp.float32)
    key_base = jax.random.truncated_normal(jax.random.fold_in(key, 102), -6.0, 6.0, (SEQ, width_all), jnp.float32)
    return (query_base, key_base)


def draw_queries(key, part):
    return drawn_pair(key)[0].astype(jnp.bfloat16)


def draw_keys(key, part):
    return drawn_pair(key)[1].astype(jnp.bfloat16)


def set_ends(result, key, least, high):
    shape = result.shape
    place = [jax.random.randint(jax.random.fold_in(key, axis), (), 0, shape[axis]) for axis in range(len(shape))]
    result = result.at[tuple(place)].set(least)
    longest = shape.index(max(shape))
    place[longest] = (place[longest] + 1) % shape[longest]
    return result.at[tuple(place)].set(high)


def block_levels(rng, dims, split, least, largest):
    def one(dim, parts):
        draws = jax.random.uniform(jax.random.fold_in(jax.random.fold_in(rng, 6), dim), (parts,), jnp.float32, least / len(split), largest / len(split))
        return jnp.repeat(jnp.exp(draws), dims[dim] // parts).reshape((-1,) + (1,) * (len(dims) - dim - 1))

    factor_of = one(*split[0])
    for cut in split[1:]:
        factor_of = factor_of * one(*cut)
    return factor_of


def bell_draw(key, extent, width, limit, cuts=(), kind=jnp.bfloat16):
    drawn = jax.random.normal(key, extent, jnp.float32) * width
    if len(cuts) > 0:
        drawn = block_levels(key, extent, cuts, -0.22, 0.18) * drawn
    return jnp.clip(drawn, min=-limit, max=limit).astype(kind)


def setup_inputs(seed: int = 0) -> dict:
    splits = jax.random.split(jax.random.key(seed), 11)
    queries = draw_queries(jax.random.fold_in(splits[10], 71), 0)
    keys = draw_keys(jax.random.fold_in(splits[10], 71), 0)
    values = bell_draw(splits[2], (SEQ, SAMPLES * CHANNELS), 1.0, 6.0, ((0, 16), (1, 32)))
    query_tangent = bell_draw(splits[3], (SEQ, SAMPLES * CHANNELS), 1.0, 6.0, ((0, 16), (1, 32)))
    key_tangent = bell_draw(splits[4], (SEQ, SAMPLES * CHANNELS), 1.0, 6.0, ((0, 16), (1, 32)))
    value_tangent = bell_draw(splits[5], (SEQ, SAMPLES * CHANNELS), 1.0, 6.0, ((0, 16), (1, 32)))
    query_gain = jnp.clip(1.0 + 0.1 * jax.random.normal(splits[6], (CHANNELS,), jnp.float32), 0.5, 1.5)
    key_gain = jnp.clip(1.0 + 0.1 * jax.random.normal(splits[7], (CHANNELS,), jnp.float32), 0.5, 1.5)
    time_index = set_ends(jax.random.randint(splits[8], (SAMPLES,), 0, STEPS), jax.random.fold_in(splits[8], 1), 0, STEPS - 1).astype(jnp.int32)
    shard_order = jax.random.permutation(splits[9], N_CTX).astype(jnp.int32)
    return dict(queries=queries, keys=keys, values=values, query_tangent=query_tangent, key_tangent=key_tangent, value_tangent=value_tangent, query_gain=query_gain, key_gain=key_gain, time_index=time_index, shard_order=shard_order)


eps_norm = 1e-06
loss_scale = 256.0
rope_base = 10000.0
floor_term = 0.1

def rope_tables(shard_order):
    row_ids = jnp.arange(SEQ, dtype=jnp.int32)
    block_ids = row_ids // TOK_DEV
    onehot = (block_ids[:, None] == jnp.arange(N_CTX, dtype=jnp.int32)[None, :]).astype(jnp.int32)
    starts = lax.optimization_barrier(jnp.sum(onehot * shard_order[None, :].astype(jnp.int32), axis=1)) * TOK_DEV
    places = (starts + row_ids % TOK_DEV).astype(jnp.float32)
    freqs = rope_base ** (-jnp.arange(HD // 2, dtype=jnp.float32) / (HD // 2))
    angles = places[:, None] * freqs[None, :]
    return (jnp.cos(angles), jnp.sin(angles))

def rotate(field, cos_table, sin_table, turn_sign):
    half_width = field.shape[-1] // 2
    first_half = field[..., :half_width]
    second_half = field[..., half_width:]
    return jnp.concatenate([first_half * cos_table - turn_sign * second_half * sin_table, turn_sign * first_half * sin_table + second_half * cos_table], axis=-1)

def normalize(field, field_tan, gain_vec):
    inv_rms = lax.rsqrt(lax.optimization_barrier(jnp.mean(field * field, axis=-1, keepdims=True)) + eps_norm)
    cross = lax.optimization_barrier(jnp.mean(field * field_tan, axis=-1, keepdims=True))
    normed = field * inv_rms * gain_vec
    normed_tan = (field_tan * inv_rms - field * inv_rms ** 3 * cross) * gain_vec
    return (normed, normed_tan, inv_rms)

def denormalize(field, inv_rms, gain_vec, grad_y):
    scaled = gain_vec * grad_y
    cross = lax.optimization_barrier(jnp.mean(field * scaled, axis=-1, keepdims=True))
    backed = inv_rms * scaled - field * inv_rms ** 3 * cross
    gain_grad = lax.optimization_barrier(jnp.sum(grad_y * field * inv_rms, axis=(0, 1)))
    return (backed, gain_grad)

def forward_pair(group):
    query_blk, key_blk, value_blk, qtan_blk, ktan_blk, vtan_blk = group
    inv_root = HD ** (-0.5)
    scores = jnp.dot(query_blk, key_blk.T, preferred_element_type=jnp.float32) * inv_root
    slopes = (jnp.dot(qtan_blk, key_blk.T, preferred_element_type=jnp.float32) + jnp.dot(query_blk, ktan_blk.T, preferred_element_type=jnp.float32)) * inv_root
    peak = lax.optimization_barrier(jnp.max(scores, axis=1, keepdims=True))
    weights = jnp.exp(scores - peak)
    totals = lax.optimization_barrier(jnp.sum(weights, axis=1, keepdims=True))
    tilted = weights * slopes
    weights_b = weights.astype(jnp.bfloat16)
    tilted_b = tilted.astype(jnp.bfloat16)
    numer = jnp.dot(weights_b, value_blk, preferred_element_type=jnp.float32)
    numer_tan = jnp.dot(weights_b, vtan_blk, preferred_element_type=jnp.float32) + jnp.dot(tilted_b, value_blk, preferred_element_type=jnp.float32)
    tilt = lax.optimization_barrier(jnp.sum(tilted, axis=1, keepdims=True))
    output = numer / totals
    output_tan = numer_tan / totals - tilt / totals * output
    return (output, output_tan, peak + jnp.log(totals))

def backward_pair(group):
    query_blk, key_blk, value_blk, cot_blk, logsum, drift = group
    inv_root = HD ** (-0.5)
    scores = jnp.dot(query_blk, key_blk.T, preferred_element_type=jnp.float32) * inv_root
    probs = jnp.exp(scores - logsum)
    probs_b = probs.astype(jnp.bfloat16)
    dvalue = jnp.dot(probs_b.T, cot_blk, preferred_element_type=jnp.float32)
    dprobs = jnp.dot(cot_blk, value_blk.T, preferred_element_type=jnp.float32)
    dscore = (probs * (dprobs - drift) * inv_root).astype(jnp.bfloat16)
    dquery = jnp.dot(dscore, key_blk, preferred_element_type=jnp.float32)
    dkey = jnp.dot(dscore.T, query_blk, preferred_element_type=jnp.float32)
    return (dquery, dkey, dvalue)

def reference(queries, keys, values, query_tangent, key_tangent, value_tangent, query_gain, key_gain, time_index, shard_order):
    cos_table, sin_table = rope_tables(shard_order)
    cos_four = cos_table[:, None, None, :]
    sin_four = sin_table[:, None, None, :]

    def spread(array):
        return array.astype(jnp.float32).reshape(SEQ, SAMPLES, CHANNELS)

    def heads_of(array):
        return array.reshape(SEQ, SAMPLES, HEADS, HD)

    def to_pairs(array):
        return jnp.transpose(array, (1, 2, 0, 3)).reshape(SAMPLES * HEADS, SEQ, array.shape[-1])

    def from_pairs(array):
        return jnp.transpose(array.reshape(SAMPLES, HEADS, SEQ, array.shape[-1]), (2, 0, 1, 3))
    query_x = spread(queries)
    key_x = spread(keys)
    query_y, query_yt, query_r = normalize(query_x, spread(query_tangent), query_gain.astype(jnp.float32))
    key_y, key_yt, key_r = normalize(key_x, spread(key_tangent), key_gain.astype(jnp.float32))
    query_n = rotate(heads_of(query_y), cos_four, sin_four, 1.0).astype(jnp.bfloat16)
    query_nt = rotate(heads_of(query_yt), cos_four, sin_four, 1.0).astype(jnp.bfloat16)
    key_n = rotate(heads_of(key_y), cos_four, sin_four, 1.0).astype(jnp.bfloat16)
    key_nt = rotate(heads_of(key_yt), cos_four, sin_four, 1.0).astype(jnp.bfloat16)
    value_h = heads_of(values)
    value_ht = heads_of(value_tangent)
    outputs, output_tan, logsum = lax.map(forward_pair, (to_pairs(query_n), to_pairs(key_n), to_pairs(value_h), to_pairs(query_nt), to_pairs(key_nt), to_pairs(value_ht)))
    outputs = from_pairs(outputs)
    output_tan = from_pairs(output_tan)
    logsum = from_pairs(logsum)
    angle_t = 0.5 * math.pi * (time_index.astype(jnp.float32) + 0.5) / STEPS
    coef_out = (jnp.sin(angle_t) * jnp.cos(angle_t))[None, :, None, None]
    coef_tan = (jnp.cos(angle_t) ** 2)[None, :, None, None]
    raw_target = coef_out * outputs + coef_tan * output_tan
    level = jnp.sqrt(lax.optimization_barrier(jnp.mean(raw_target * raw_target, axis=(2, 3), keepdims=True)))
    cotangent = (loss_scale * raw_target / (level + floor_term)).astype(jnp.bfloat16)
    drift = lax.optimization_barrier(jnp.sum(cotangent.astype(jnp.float32) * outputs, axis=-1, keepdims=True))
    dquery, dkey, dvalue = lax.map(backward_pair, (to_pairs(query_n), to_pairs(key_n), to_pairs(value_h), to_pairs(cotangent), to_pairs(logsum), to_pairs(drift)))
    query_dy = rotate(from_pairs(dquery), cos_four, sin_four, -1.0).reshape(SEQ, SAMPLES, CHANNELS)
    key_dy = rotate(from_pairs(dkey), cos_four, sin_four, -1.0).reshape(SEQ, SAMPLES, CHANNELS)
    query_back, query_gain_grad = denormalize(query_x, query_r, query_gain.astype(jnp.float32), query_dy)
    key_back, key_gain_grad = denormalize(key_x, key_r, key_gain.astype(jnp.float32), key_dy)
    query_grad = query_back.reshape(SEQ, SAMPLES * CHANNELS).astype(jnp.bfloat16)
    key_grad = key_back.reshape(SEQ, SAMPLES * CHANNELS).astype(jnp.bfloat16)
    value_grad = from_pairs(dvalue).reshape(SEQ, SAMPLES * CHANNELS).astype(jnp.bfloat16)
    return (query_grad, key_grad, value_grad, query_gain_grad, key_gain_grad)
```

```python
import math

import jax
import jax.numpy as jnp
from jax import lax
from jax.experimental import pallas as pl
from jax.experimental.pallas import tpu as pltpu
from jax.sharding import PartitionSpec as P

MESH = pl.DeviceIdType.MESH
F32 = jnp.float32
BF16 = jnp.bfloat16

HD = 128
TOK = 128
STEPS = 1000
CHANNELS = 3072
HEADS_DEV = 3
N_CTX = 16
N_FSDP = 32
RANKS = 8
SAMPLES = 4
SLOTS = 8
ROWS = SLOTS * TOK
SEQ = 2 * ROWS
GSH = 96
CHUNK = 256
N_CHUNK = ROWS // CHUNK
KTILE = 512

eps_norm = 1e-06
loss_scale = 256.0
floor_term = 0.1
ROOT = math.sqrt(HD)
EXP2C = math.log2(math.e) / ROOT

LOC = ((0, 2, 9, 11, 4, 14), (5, 7, 14, 12, 9, 3))

NT = (((1,), (1,)), ((), ()))


def dot(a, b):
    return jnp.dot(a, b, preferred_element_type=F32)


def cols_to_rows(cols):
    lane = lax.broadcasted_iota(jnp.int32, (TOK, 128), 1)
    tile = jnp.zeros((TOK, 128), F32)
    for i, col in enumerate(cols):
        tile = jnp.where(lane == i, col, tile)
    return tile.T[0:8, :]


def rows_to_cols(rows):
    return jnp.concatenate([rows] * 16, axis=0).T


def kernel(
    so_ref,
    ti_ref,
    q_ref,
    k_ref,
    v_ref,
    qt_ref,
    kt_ref,
    vt_ref,
    qg_ref,
    kg_ref,
    dq_out,
    dk_out,
    dv_out,
    qgg_out,
    kgg_out,
    cosw,
    sinw,
    gsend,
    grecv,
    strecv,
    statc,
    gains,
    qs,
    ks,
    qq,
    kk,
    vv,
    vT,
    kT,
    s_buf,
    t_buf,
    e_buf,
    ds_buf,
    cn_buf,
    oT,
    gT,
    lrow,
    erecv,
    lev,
    resq,
    resk,
    resv,
    xsend,
    xrecv,
    retq,
    retk,
    retv,
    crecv,
    ggsend,
    ggrecv,
    ffrecv,
    g_ss,
    g_rs,
    st_ss,
    st_rs,
    v_ss,
    v_rs,
    q_ss,
    q_rs,
    k_ss,
    k_rs,
    fk_ss,
    fk_rs,
    fv_ss,
    fv_rs,
    e_ss,
    e_rs,
    r_ss,
    r_rs,
    x_ss,
    x_rs,
    c_ss,
    c_rs,
    gg_ss,
    gg_rs,
    ff_ss,
    ff_rs,
):
    c = lax.axis_index("ctx")
    f = lax.axis_index("fsdp")
    samp = f // 8
    rank = f % 8
    ylo = (f // 2) % 2
    core = f % 2
    base = f - core
    sib = base + (1 - core)
    half = c % 2
    slot = c // 2

    dests = []
    for h in range(HEADS_DEV):
        a, b = LOC[0][h], LOC[0][3 + h]
        d, e = LOC[1][h], LOC[1][3 + h]
        cd = a + core * (b - a) + ylo * (d - a) + core * ylo * (e - d - b + a)
        fd = base + half
        dests.append((cd, fd, jnp.logical_and(cd == c, fd == f)))

    act = 0
    jj = 0
    for j in range(6):
        hit = jnp.where(c == LOC[0][j] + ylo * (LOC[1][j] - LOC[0][j]), 1, 0)
        act = act + hit
        jj = jj + j * hit
    active = act == 1
    hcore = jj // 3
    hl = jj % 3
    src_f = base + hcore

    def source(t):
        cs = 2 * t + core
        return cs, src_f, jnp.logical_and(cs == c, src_f == f)

    def remote(src, dst, ss, rs, dev):
        return pltpu.make_async_remote_copy(
            src_ref=src, dst_ref=dst, send_sem=ss, recv_sem=rs, device_id=dev, device_id_type=MESH
        )

    def push(src, dst, ss, rs, dev, own):
        @pl.when(own)
        def _():
            pltpu.make_async_copy(src, dst, rs).start()

        @pl.when(jnp.logical_not(own))
        def _():
            remote(src, dst, ss, rs, dev).start()

    def sent(src, dst, ss, rs, dev, own):
        @pl.when(jnp.logical_not(own))
        def _():
            remote(src, dst, ss, rs, dev).wait_send()

    def arrived(dst, rs):
        pltpu.make_async_copy(dst, dst, rs).wait()

    barrier = pltpu.get_barrier_semaphore()
    for i in range(1, N_FSDP):
        pl.semaphore_signal(barrier, inc=1, device_id=(c, (f + i) % N_FSDP), device_id_type=MESH)
    own_heads = 0
    for cd, fd, own in dests:
        own_heads = own_heads + jnp.where(own, 1, 0)

        @pl.when(jnp.logical_not(own))
        def _(cd=cd, fd=fd):
            pl.semaphore_signal(barrier, inc=1, device_id=(cd, fd), device_id_type=MESH)

    @pl.when(active)
    def _():
        for t in range(SLOTS):
            cs, fs, own = source(t)

            @pl.when(jnp.logical_not(own))
            def _(cs=cs, fs=fs):
                pl.semaphore_signal(barrier, inc=1, device_id=(cs, fs), device_id_type=MESH)

    m_id = lax.broadcasted_iota(jnp.int32, (8, 128), 1) % 64
    freq = jnp.full((8, 128), 1.0, F32)
    for bit in range(6):
        factor = 10000.0 ** (-(2.0**bit) / 64.0)
        freq = freq * jnp.where((m_id // (2**bit)) % 2 == 1, factor, 1.0)
    row_id = lax.broadcasted_iota(jnp.int32, (TOK, 128), 0)
    place = (row_id + so_ref[0] * TOK).astype(F32)
    angle = place * freq[0:1, :]
    lane_id = lax.broadcasted_iota(jnp.int32, (TOK, 128), 1)
    cosw[...] = jnp.cos(angle)
    sin_t = jnp.sin(angle)
    sinw[...] = jnp.where(lane_id < 64, -sin_t, sin_t)

    qx = q_ref[...].astype(F32)
    kx = k_ref[...].astype(F32)
    qdx = qt_ref[...].astype(F32)
    kdx = kt_ref[...].astype(F32)

    def rsum(x):
        return jnp.sum(x, axis=1, keepdims=True)

    strecv[rank] = cols_to_rows([rsum(qx * qx), rsum(kx * kx), rsum(qx * qdx), rsum(kx * kdx)])
    gsend[...] = jnp.zeros((8, 128), F32)
    gsend[0:1, 0:GSH] = qg_ref[...]
    gsend[1:2, 0:GSH] = kg_ref[...]

    own_src = jnp.where(jnp.logical_and(half == core, hcore == core), 1, 0)
    pl.semaphore_wait(
        barrier, (N_FSDP - 1) + (HEADS_DEV - own_heads) + act * (SLOTS - own_src)
    )

    gain_copies = []
    for s in range(SAMPLES):
        fu = 8 * s + f // 4
        gain_copies.append(
            (gsend, grecv.at[f % 4], g_ss.at[s], g_rs.at[f % 4], (c, fu), fu == f)
        )
    for args in gain_copies:
        push(*args)
    stat_copies = []
    for i in range(1, RANKS):
        peer = samp * 8 + (rank + i) % 8
        stat_copies.append(
            remote(strecv.at[rank], strecv.at[rank], st_ss.at[i], st_rs.at[rank], (c, peer))
        )
    for copy in stat_copies:
        copy.start()
    val_copies = []
    for h, (cd, fd, own) in enumerate(dests):
        for n, ref in enumerate((v_ref, vt_ref)):
            val_copies.append(
                (
                    ref.at[:, h * HD : (h + 1) * HD],
                    vv.at[slot, :, n * HD : (n + 1) * HD],
                    v_ss.at[h, n],
                    v_rs.at[slot, n],
                    (cd, fd),
                    own,
                )
            )
    for args in val_copies:
        push(*args)

    for i in range(1, RANKS):
        peer = (rank + i) % 8
        arrived(strecv.at[peer], st_rs.at[peer])
    for i in range(4):
        arrived(grecv.at[i], g_rs.at[i])

    total = strecv[0]
    for i in range(1, RANKS):
        total = total + strecv[i]
    stat = rows_to_cols(total) / CHANNELS
    statc[...] = stat
    qr = lax.rsqrt(stat[:, 0:1] + eps_norm)
    kr = lax.rsqrt(stat[:, 1:2] + eps_norm)
    qc = stat[:, 2:3]
    kc = stat[:, 3:4]
    both = jnp.concatenate([grecv[i][:, 0:GSH] for i in range(4)], axis=1)
    gains[...] = both
    cos_w = cosw[...]
    sin_w = sinw[...]

    def turn(x, sign):
        return x * cos_w + sign * pltpu.roll(x, 64, 1) * sin_w

    def normed(x, dx, inv, cross, gain):
        y = x * inv * gain
        yt = (dx * inv - x * (inv * inv * inv) * cross) * gain
        return turn(y, 1.0).astype(BF16), turn(yt, 1.0).astype(BF16)

    qk_copies = []
    for h, (cd, fd, own) in enumerate(dests):
        cols = slice(h * HD, (h + 1) * HD)
        y, yt = normed(k_ref[:, cols].astype(F32), kt_ref[:, cols].astype(F32), kr, kc, both[1:2, cols])
        ks[h, :, 0:HD] = y
        ks[h, :, HD : 2 * HD] = yt
        args = (ks.at[h], kk.at[slot], k_ss.at[h], k_rs.at[slot], (cd, fd), own)
        push(*args)
        qk_copies.append(args)
    for h, (cd, fd, own) in enumerate(dests):
        cols = slice(h * HD, (h + 1) * HD)
        y, yt = normed(q_ref[:, cols].astype(F32), qt_ref[:, cols].astype(F32), qr, qc, both[0:1, cols])
        qs[h, :, 0:HD] = yt
        qs[h, :, HD : 2 * HD] = y
        args = (qs.at[h], qq.at[slot], q_ss.at[h], q_rs.at[slot], (cd, fd), own)
        push(*args)
        qk_copies.append(args)

    for args in gain_copies + val_copies + qk_copies:
        sent(*args)
    for copy in stat_copies:
        copy.wait_send()

    @pl.when(active)
    def _():
        for t in range(SLOTS):
            arrived(vv.at[t, :, 0:HD], v_rs.at[t, 0])
            arrived(vv.at[t, :, HD : 2 * HD], v_rs.at[t, 1])
            remote(vv.at[t], vv.at[SLOTS + t], fv_ss.at[t], fv_rs.at[t], (c, sib)).start()
        for t in range(SLOTS):
            arrived(kk.at[t], k_rs.at[t])
            remote(kk.at[t], kk.at[SLOTS + t], fk_ss.at[t], fk_rs.at[t], (c, sib)).start()
        for t in range(SLOTS):
            arrived(qq.at[t], q_rs.at[t])
        for t in range(SLOTS):
            remote(vv.at[t], vv.at[SLOTS + t], fv_ss.at[t], fv_rs.at[t], (c, sib)).wait()
            remote(kk.at[t], kk.at[SLOTS + t], fk_ss.at[t], fk_rs.at[t], (c, sib)).wait()
        for t in range(2 * SLOTS):
            rows = slice(t * TOK, (t + 1) * TOK)
            vT[:, rows] = vv[t].T
            kT[:, rows] = kk[t, :, 0:HD].T

        t_val = jnp.full((8, 128), ti_ref[samp], jnp.int32).astype(F32)
        t_ang = (0.5 * math.pi) * (t_val + 0.5) / STEPS
        sin_a = jnp.sin(t_ang)[0:1, :]
        cos_a = jnp.cos(t_ang)[0:1, :]
        c_out = jnp.concatenate([sin_a * cos_a] * 2, axis=1)
        c_tan = jnp.concatenate([cos_a * cos_a] * 2, axis=1)

        per = KTILE // TOK

        def forward(rc, carry):
            qb = qq[pl.ds(rc * 2, 2)].reshape(CHUNK, 2 * HD)
            peak = jnp.full((1, CHUNK), -jnp.inf, F32)
            for kt in range(SEQ // KTILE):
                kb = kk[kt * per : (kt + 1) * per, :, 0:HD].reshape(KTILE, HD)
                sc = lax.dot_general(kb, qb[:, HD : 2 * HD], NT, preferred_element_type=F32)
                s_buf[kt * KTILE : (kt + 1) * KTILE, :] = sc
                peak = jnp.maximum(peak, jnp.max(sc, axis=0, keepdims=True))
            shift = peak * EXP2C
            lsum = jnp.zeros((1, CHUNK), F32)
            tilt = jnp.zeros((1, CHUNK), F32)
            cols = pl.ds(pl.multiple_of(rc * CHUNK, CHUNK), CHUNK)
            for kt in range(SEQ // KTILE):
                rows = slice(kt * KTILE, (kt + 1) * KTILE)
                kb = kk[kt * per : (kt + 1) * per].reshape(KTILE, 2 * HD)
                up = lax.dot_general(kb, qb, NT, preferred_element_type=F32)
                ex = jnp.exp2(s_buf[rows, :] * EXP2C - shift)
                ti = ex * up
                lsum = lsum + jnp.sum(ex, axis=0, keepdims=True)
                tilt = tilt + jnp.sum(ti, axis=0, keepdims=True)
                e_buf[rows, cols] = ex.astype(BF16)
                t_buf[rows, :] = ti.astype(BF16)
            ov = dot(vT[...], e_buf[:, cols])
            tv = dot(vT[0:HD, :], t_buf[...])
            linv = 1.0 / lsum
            out = ov[0:HD, :] * linv
            out_t = (ov[HD : 2 * HD, :] + tv * (1.0 / ROOT)) * linv - (tilt * (1.0 / ROOT)) * linv * out
            oT[rc] = out
            gT[rc] = c_out * out + c_tan * out_t
            lrow[rc] = jnp.broadcast_to(linv, (8, CHUNK))
            return carry

        lax.fori_loop(0, N_CHUNK, forward, 0)

        energy = []
        for rc in range(N_CHUNK):
            g = gT[rc]
            e = jnp.sum(g * g, axis=0, keepdims=True)
            energy += [e[:, 0:128], e[:, 128:256]]
        mine = (rank // 2) * 6 + jj
        erecv[mine] = jnp.concatenate(energy, axis=0)
        for plane in range(4):
            for j in range(6):
                idx = plane * 6 + j
                fp = 8 * samp + plane * 2 + core

                @pl.when(mine != idx)
                def _(idx=idx, cp=LOC[plane % 2][j], fp=fp):
                    remote(
                        erecv.at[mine], erecv.at[mine], e_ss.at[idx], e_rs.at[mine], (cp, fp)
                    ).start()

        for idx in range(24):

            @pl.when(mine != idx)
            def _(idx=idx):
                arrived(erecv.at[idx], e_rs.at[idx])

        esum = erecv[0]
        for idx in range(1, 24):
            esum = esum + erecv[idx]
        scale = loss_scale / (jnp.sqrt(esum / CHANNELS) + floor_term)
        for rc in range(N_CHUNK):
            row = jnp.concatenate([scale[2 * rc : 2 * rc + 1], scale[2 * rc + 1 : 2 * rc + 2]], axis=1)
            lev[rc] = jnp.broadcast_to(row, (8, CHUNK))

        def back(rc, carry):
            cols = pl.ds(pl.multiple_of(rc * CHUNK, CHUNK), CHUNK)
            cot = (gT[rc] * lev[rc][0:1, :]).astype(BF16).astype(F32)
            cn = cot * (lrow[rc][0:1, :] * (1.0 / ROOT))
            cnT = cn.astype(BF16)
            drift = jnp.sum(cnT.astype(F32) * oT[rc], axis=0, keepdims=True)
            cn_buf[pl.ds(rc * 2, 2)] = cn.T.astype(BF16).reshape(2, TOK, HD)
            for kt in range(SEQ // KTILE):
                rows = slice(kt * KTILE, (kt + 1) * KTILE)
                vb = vv[kt * per : (kt + 1) * per, :, 0:HD].reshape(KTILE, HD)
                dp = dot(vb, cnT)
                ds_buf[rows, cols] = (e_buf[rows, cols].astype(F32) * (dp - drift)).astype(BF16)
            dqT = dot(kT[...], ds_buf[:, cols])
            resq[pl.ds(rc * 2, 2)] = dqT.T.astype(BF16).reshape(2, TOK, HD)
            for u in range(2):
                t = rc * 2 + u
                cs, fs, own = source(t)
                push(resq.at[t], retq.at[hl], r_ss.at[0, t], r_rs.at[0, hl], (cs, fs), own)
            return carry

        lax.fori_loop(0, N_CHUNK, back, 0)

        qn = qq[:, :, HD : 2 * HD].reshape(ROWS, HD)
        cn_all = cn_buf[...].reshape(ROWS, HD)
        xsend[0] = dot(ds_buf[ROWS:SEQ, :], qn).astype(BF16)
        xk = remote(xsend.at[0], xrecv.at[0], x_ss.at[0], x_rs.at[0], (c, sib))
        xk.start()
        xsend[1] = dot(e_buf[ROWS:SEQ, :], cn_all).astype(BF16)
        xv = remote(xsend.at[1], xrecv.at[1], x_ss.at[1], x_rs.at[1], (c, sib))
        xv.start()
        dk = dot(ds_buf[0:ROWS, :], qn)
        xk.wait_recv()
        resk[...] = (dk + xrecv[0].astype(F32)).astype(BF16).reshape(SLOTS, TOK, HD)
        for t in range(SLOTS):
            cs, fs, own = source(t)
            push(resk.at[t], retk.at[hl], r_ss.at[1, t], r_rs.at[1, hl], (cs, fs), own)
        dv = dot(e_buf[0:ROWS, :], cn_all)
        xv.wait_recv()
        resv[...] = ((dv + xrecv[1].astype(F32)) * ROOT).astype(BF16).reshape(SLOTS, TOK, HD)
        for t in range(SLOTS):
            cs, fs, own = source(t)
            push(resv.at[t], retv.at[hl], r_ss.at[2, t], r_rs.at[2, hl], (cs, fs), own)

        xk.wait_send()
        xv.wait_send()
        for t in range(SLOTS):
            cs, fs, own = source(t)
            sent(resq.at[t], retq.at[hl], r_ss.at[0, t], r_rs.at[0, hl], (cs, fs), own)
            sent(resk.at[t], retk.at[hl], r_ss.at[1, t], r_rs.at[1, hl], (cs, fs), own)
            sent(resv.at[t], retv.at[hl], r_ss.at[2, t], r_rs.at[2, hl], (cs, fs), own)
        for plane in range(4):
            for j in range(6):
                idx = plane * 6 + j
                fp = 8 * samp + plane * 2 + core

                @pl.when(mine != idx)
                def _(idx=idx, cp=LOC[plane % 2][j], fp=fp):
                    remote(
                        erecv.at[mine], erecv.at[mine], e_ss.at[idx], e_rs.at[mine], (cp, fp)
                    ).wait_send()

    def inverse_turn(ret):
        x = ret.astype(F32)
        return x * cosw[...] - pltpu.roll(x, 64, 1) * sinw[...]

    def inv_of(i):
        return lax.rsqrt(statc[:, i : i + 1] + eps_norm)

    crosses = []
    sums = []
    for i, (x_ref, ret, tensor) in enumerate(((q_ref, retq, 0), (k_ref, retk, 1))):
        inv = inv_of(i)
        part = jnp.zeros((TOK, HD), F32)
        rows = []
        for h in range(HEADS_DEV):
            cols = slice(h * HD, (h + 1) * HD)
            arrived(ret.at[h], r_rs.at[tensor, h])
            dyx = inverse_turn(ret[h]) * x_ref[:, cols].astype(F32)
            part = part + dyx * gains[i : i + 1, cols]
            rows.append(jnp.sum(dyx * inv, axis=0, keepdims=True))
        crosses.append(rsum(part))
        sums.append(jnp.concatenate(rows, axis=1))
    crecv[rank] = cols_to_rows(crosses)
    cross_copies = []
    for i in range(1, RANKS):
        peer = samp * 8 + (rank + i) % 8
        cross_copies.append(
            remote(crecv.at[rank], crecv.at[rank], c_ss.at[i], c_rs.at[rank], (c, peer))
        )
    for copy in cross_copies:
        copy.start()
    gg_copies = []
    ggsend[...] = jnp.zeros((4, 8, 128), F32)
    for i in range(4):
        for n in range(2):
            ggsend[i, n : n + 1, 0:GSH] = sums[n][:, i * GSH : (i + 1) * GSH]
        fo = 4 * rank + i
        gg_copies.append(
            (ggsend.at[i], ggrecv.at[samp], gg_ss.at[i], gg_rs.at[samp], (c, fo), fo == f)
        )
    for args in gg_copies:
        push(*args)

    for h in range(HEADS_DEV):
        arrived(retv.at[h], r_rs.at[2, h])
        dv_out[:, h * HD : (h + 1) * HD] = retv[h]

    for s in range(SAMPLES):
        arrived(ggrecv.at[s], gg_rs.at[s])
    ffrecv[c] = ggrecv[0] + ggrecv[1] + ggrecv[2] + ggrecv[3]
    ff_copies = []
    for i in range(1, N_CTX):
        ff_copies.append(
            remote(ffrecv.at[c], ffrecv.at[c], ff_ss.at[i], ff_rs.at[c], ((c + i) % N_CTX, f))
        )
    for copy in ff_copies:
        copy.start()

    for i in range(1, RANKS):
        peer = (rank + i) % 8
        arrived(crecv.at[peer], c_rs.at[peer])
    ctot = crecv[0]
    for i in range(1, RANKS):
        ctot = ctot + crecv[i]
    cmean = rows_to_cols(ctot) / CHANNELS
    for i, (x_ref, ret, out) in enumerate(((q_ref, retq, dq_out), (k_ref, retk, dk_out))):
        inv = inv_of(i)
        pull = inv * inv * inv * cmean[:, i : i + 1]
        for h in range(HEADS_DEV):
            cols = slice(h * HD, (h + 1) * HD)
            hh = inverse_turn(ret[h]) * gains[i : i + 1, cols]
            out[:, cols] = (inv * hh - x_ref[:, cols].astype(F32) * pull).astype(BF16)

    for i in range(1, N_CTX):
        peer = (c + i) % N_CTX
        arrived(ffrecv.at[peer], ff_rs.at[peer])
    ftot = ffrecv[0]
    for i in range(1, N_CTX):
        ftot = ftot + ffrecv[i]
    qgg_out[...] = ftot[0:1, 0:GSH]
    kgg_out[...] = ftot[1:2, 0:GSH]
    for copy in cross_copies + ff_copies:
        copy.wait_send()
    for args in gg_copies:
        sent(*args)


def per_device(
    queries,
    keys,
    values,
    query_tangent,
    key_tangent,
    value_tangent,
    query_gain,
    key_gain,
    time_index,
    shard_order,
):
    width = HEADS_DEV * HD
    vm = pl.BlockSpec(memory_space=pltpu.VMEM)
    sm = pl.BlockSpec(memory_space=pltpu.SMEM)
    dma = pltpu.SemaphoreType.DMA
    big = jax.ShapeDtypeStruct((TOK, width), BF16)
    small = jax.ShapeDtypeStruct((1, GSH), F32)
    scratch = [
        pltpu.VMEM((TOK, 128), F32),
        pltpu.VMEM((TOK, 128), F32),
        pltpu.VMEM((8, 128), F32),
        pltpu.VMEM((4, 8, 128), F32),
        pltpu.VMEM((8, 8, 128), F32),
        pltpu.VMEM((TOK, 128), F32),
        pltpu.VMEM((8, width), F32),
        pltpu.VMEM((3, TOK, 256), BF16),
        pltpu.VMEM((3, TOK, 256), BF16),
        pltpu.VMEM((SLOTS, TOK, 256), BF16),
        pltpu.VMEM((2 * SLOTS, TOK, 256), BF16),
        pltpu.VMEM((2 * SLOTS, TOK, 256), BF16),
        pltpu.VMEM((256, SEQ), BF16),
        pltpu.VMEM((128, SEQ), BF16),
        pltpu.VMEM((SEQ, CHUNK), F32),
        pltpu.VMEM((SEQ, CHUNK), BF16),
        pltpu.VMEM((SEQ, ROWS), BF16),
        pltpu.VMEM((SEQ, ROWS), BF16),
        pltpu.VMEM((SLOTS, TOK, HD), BF16),
        pltpu.VMEM((N_CHUNK, HD, CHUNK), F32),
        pltpu.VMEM((N_CHUNK, HD, CHUNK), F32),
        pltpu.VMEM((N_CHUNK, 8, CHUNK), F32),
        pltpu.VMEM((24, 8, 128), F32),
        pltpu.VMEM((N_CHUNK, 8, CHUNK), F32),
        pltpu.VMEM((SLOTS, TOK, HD), BF16),
        pltpu.VMEM((SLOTS, TOK, HD), BF16),
        pltpu.VMEM((SLOTS, TOK, HD), BF16),
        pltpu.VMEM((2, ROWS, HD), BF16),
        pltpu.VMEM((2, ROWS, HD), BF16),
        pltpu.VMEM((3, TOK, HD), BF16),
        pltpu.VMEM((3, TOK, HD), BF16),
        pltpu.VMEM((3, TOK, HD), BF16),
        pltpu.VMEM((8, 8, 128), F32),
        pltpu.VMEM((4, 8, 128), F32),
        pltpu.VMEM((4, 8, 128), F32),
        pltpu.VMEM((16, 8, 128), F32),
        dma((4,)),
        dma((4,)),
        dma((8,)),
        dma((8,)),
        dma((3, 2)),
        dma((8, 2)),
        dma((3,)),
        dma((8,)),
        dma((3,)),
        dma((8,)),
        dma((8,)),
        dma((8,)),
        dma((8,)),
        dma((8,)),
        dma((24,)),
        dma((24,)),
        dma((3, 8)),
        dma((3, 3)),
        dma((2,)),
        dma((2,)),
        dma((8,)),
        dma((8,)),
        dma((4,)),
        dma((4,)),
        dma((16,)),
        dma((16,)),
    ]
    outs = pl.pallas_call(
        kernel,
        out_shape=(big, big, big, small, small),
        in_specs=[sm, sm] + [vm] * 8,
        out_specs=(vm,) * 5,
        scratch_shapes=scratch,
        compiler_params=pltpu.CompilerParams(
            collective_id=0, has_side_effects=True, vmem_limit_bytes=48 * 1024 * 1024
        ),
        name="tangent_attention",
    )(
        shard_order,
        time_index,
        queries,
        keys,
        values,
        query_tangent,
        key_tangent,
        value_tangent,
        query_gain.reshape(1, GSH),
        key_gain.reshape(1, GSH),
    )
    return (outs[0], outs[1], outs[2], outs[3].reshape(GSH), outs[4].reshape(GSH))


def solution(mesh):
    placed = (
        P("ctx", "fsdp"),
        P("ctx", "fsdp"),
        P("ctx", "fsdp"),
        P("ctx", "fsdp"),
        P("ctx", "fsdp"),
        P("ctx", "fsdp"),
        P("fsdp"),
        P("fsdp"),
        P(),
        P("ctx"),
    )
    return jax.shard_map(
        per_device,
        mesh=mesh,
        in_specs=placed,
        out_specs=(P("ctx", "fsdp"), P("ctx", "fsdp"), P("ctx", "fsdp"), P("fsdp"), P("fsdp")),
        check_vma=False,
    )
```

```python
import math

import jax
import jax.numpy as jnp
from jax import lax
from jax.experimental import pallas as pl
from jax.experimental.pallas import tpu as pltpu
from jax.sharding import PartitionSpec as P

MESH = pl.DeviceIdType.MESH
F32 = jnp.float32
BF16 = jnp.bfloat16

HD = 128
TOK = 128
STEPS = 1000
CHANNELS = 3072
HEADS_DEV = 3
N_CTX = 16
N_FSDP = 32
RANKS = 8
SAMPLES = 4
SLOTS = 8
ROWS = SLOTS * TOK
SEQ = 2 * ROWS
GSH = 96
CHUNK = 256
N_CHUNK = ROWS // CHUNK
KTILE = 512
VMEM_LIMIT = 63 * 1024 * 1024

eps_norm = 1e-06
loss_scale = 256.0
floor_term = 0.1
ROOT = math.sqrt(HD)
EXP2C = math.log2(math.e) / ROOT

LOC = ((0, 2, 9, 11, 4, 14), (5, 7, 14, 12, 9, 3))

NT = (((1,), (1,)), ((), ()))


def dot(a, b):
    return jnp.dot(a, b, preferred_element_type=F32)


def cols_to_rows(cols):
    lane = lax.broadcasted_iota(jnp.int32, (TOK, 128), 1)
    tile = jnp.zeros((TOK, 128), F32)
    for i, col in enumerate(cols):
        tile = jnp.where(lane == i, col, tile)
    return tile.T[0:8, :]


def rows_to_cols(rows):
    return jnp.concatenate([rows] * 16, axis=0).T


def kernel(
    so_ref,
    ti_ref,
    q_hbm,
    k_hbm,
    v_hbm,
    qt_hbm,
    kt_hbm,
    vt_hbm,
    qg_ref,
    kg_ref,
    dq_hbm,
    dk_hbm,
    dv_hbm,
    qgg_hbm,
    kgg_hbm,
    loaded,
    dq_out,
    dk_out,
    dv_out,
    qgg_out,
    kgg_out,
    cosw,
    sinw,
    gsend,
    grecv,
    strecv,
    statc,
    gains,
    qs,
    ks,
    qq,
    kk,
    vv,
    vT,
    kT,
    s_buf,
    t_buf,
    e_buf,
    ds_buf,
    cn_buf,
    oT,
    gT,
    lrow,
    erecv,
    qn_buf,
    resq,
    resk,
    resv,
    xsend,
    xrecv,
    retq,
    retk,
    retv,
    crecv,
    ggsend,
    ggrecv,
    ffrecv,
    g_ss,
    g_rs,
    st_ss,
    st_rs,
    v_ss,
    v_rs,
    q_ss,
    q_rs,
    k_ss,
    k_rs,
    fk_ss,
    fk_rs,
    fv_ss,
    fv_rs,
    e_ss,
    e_rs,
    r_ss,
    r_rs,
    x_ss,
    x_rs,
    c_ss,
    c_rs,
    gg_ss,
    gg_rs,
    ff_ss,
    ff_rs,
    in_sem,
    out_sem,
):
    q_ref, k_ref, v_ref, qt_ref, kt_ref, vt_ref = (loaded.at[n] for n in range(6))
    c = lax.axis_index("ctx")
    f = lax.axis_index("fsdp")
    samp = f // 8
    rank = f % 8
    ylo = (f // 2) % 2
    core = f % 2
    base = f - core
    sib = base + (1 - core)
    half = c % 2
    slot = c // 2

    dests = []
    for h in range(HEADS_DEV):
        a, b = LOC[0][h], LOC[0][3 + h]
        d, e = LOC[1][h], LOC[1][3 + h]
        cd = a + core * (b - a) + ylo * (d - a) + core * ylo * (e - d - b + a)
        fd = base + half
        dests.append((cd, fd, jnp.logical_and(cd == c, fd == f)))

    act = 0
    jj = 0
    for j in range(6):
        hit = jnp.where(c == LOC[0][j] + ylo * (LOC[1][j] - LOC[0][j]), 1, 0)
        act = act + hit
        jj = jj + j * hit
    active = act == 1
    hcore = jj // 3
    hl = jj % 3
    src_f = base + hcore

    def source(t):
        cs = 2 * t + core
        return cs, src_f, jnp.logical_and(cs == c, src_f == f)

    def remote(src, dst, ss, rs, dev):
        return pltpu.make_async_remote_copy(
            src_ref=src, dst_ref=dst, send_sem=ss, recv_sem=rs, device_id=dev, device_id_type=MESH
        )

    def push(src, dst, ss, rs, dev, own):
        @pl.when(own)
        def _():
            pltpu.make_async_copy(src, dst, rs).start()

        @pl.when(jnp.logical_not(own))
        def _():
            remote(src, dst, ss, rs, dev).start()

    def sent(src, dst, ss, rs, dev, own):
        @pl.when(jnp.logical_not(own))
        def _():
            remote(src, dst, ss, rs, dev).wait_send()

    def arrived(dst, rs):
        pltpu.make_async_copy(dst, dst, rs).wait()

    barrier = pltpu.get_barrier_semaphore()
    for i in range(1, N_FSDP):
        pl.semaphore_signal(barrier, inc=1, device_id=(c, (f + i) % N_FSDP), device_id_type=MESH)
    own_heads = 0
    for cd, fd, own in dests:
        own_heads = own_heads + jnp.where(own, 1, 0)

        @pl.when(jnp.logical_not(own))
        def _(cd=cd, fd=fd):
            pl.semaphore_signal(barrier, inc=1, device_id=(cd, fd), device_id_type=MESH)

    @pl.when(active)
    def _():
        for t in range(SLOTS):
            cs, fs, own = source(t)

            @pl.when(jnp.logical_not(own))
            def _(cs=cs, fs=fs):
                pl.semaphore_signal(barrier, inc=1, device_id=(cs, fs), device_id_type=MESH)

    loads = [
        pltpu.make_async_copy(src, loaded.at[n], in_sem.at[n])
        for n, src in enumerate((q_hbm, k_hbm, v_hbm, qt_hbm, kt_hbm, vt_hbm))
    ]
    for load in loads:
        load.start()

    m_id = lax.broadcasted_iota(jnp.int32, (8, 128), 1) % 64
    freq = jnp.full((8, 128), 1.0, F32)
    for bit in range(6):
        factor = 10000.0 ** (-(2.0**bit) / 64.0)
        freq = freq * jnp.where((m_id // (2**bit)) % 2 == 1, factor, 1.0)
    row_id = lax.broadcasted_iota(jnp.int32, (TOK, 128), 0)
    place = (row_id + so_ref[0] * TOK).astype(F32)
    angle = place * freq[0:1, :]
    lane_id = lax.broadcasted_iota(jnp.int32, (TOK, 128), 1)
    cosw[...] = jnp.cos(angle)
    sin_t = jnp.sin(angle)
    sinw[...] = jnp.where(lane_id < 64, -sin_t, sin_t)

    for load in loads:
        load.wait()
    qx = q_ref[...].astype(F32)
    kx = k_ref[...].astype(F32)
    qdx = qt_ref[...].astype(F32)
    kdx = kt_ref[...].astype(F32)

    def rsum(x):
        return jnp.sum(x, axis=1, keepdims=True)

    strecv[rank] = cols_to_rows([rsum(qx * qx), rsum(kx * kx), rsum(qx * qdx), rsum(kx * kdx)])
    gsend[...] = jnp.zeros((8, 128), F32)
    gsend[0:1, 0:GSH] = qg_ref[...]
    gsend[1:2, 0:GSH] = kg_ref[...]

    own_src = jnp.where(jnp.logical_and(half == core, hcore == core), 1, 0)
    pl.semaphore_wait(
        barrier, (N_FSDP - 1) + (HEADS_DEV - own_heads) + act * (SLOTS - own_src)
    )

    gain_copies = []
    for s in range(SAMPLES):
        fu = 8 * s + f // 4
        gain_copies.append(
            (gsend, grecv.at[f % 4], g_ss.at[s], g_rs.at[f % 4], (c, fu), fu == f)
        )
    for args in gain_copies:
        push(*args)
    stat_copies = []
    for i in range(1, RANKS):
        peer = samp * 8 + (rank + i) % 8
        stat_copies.append(
            remote(strecv.at[rank], strecv.at[rank], st_ss.at[i], st_rs.at[rank], (c, peer))
        )
    for copy in stat_copies:
        copy.start()
    val_copies = []
    for h, (cd, fd, own) in enumerate(dests):
        for n, ref in enumerate((v_ref, vt_ref)):
            val_copies.append(
                (
                    ref.at[:, h * HD : (h + 1) * HD],
                    vv.at[slot, :, n * HD : (n + 1) * HD],
                    v_ss.at[h, n],
                    v_rs.at[slot, n],
                    (cd, fd),
                    own,
                )
            )
    for args in val_copies:
        push(*args)

    for i in range(1, RANKS):
        peer = (rank + i) % 8
        arrived(strecv.at[peer], st_rs.at[peer])
    for i in range(4):
        arrived(grecv.at[i], g_rs.at[i])

    total = strecv[0]
    for i in range(1, RANKS):
        total = total + strecv[i]
    stat = rows_to_cols(total) / CHANNELS
    statc[...] = stat
    qr = lax.rsqrt(stat[:, 0:1] + eps_norm)
    kr = lax.rsqrt(stat[:, 1:2] + eps_norm)
    qc = stat[:, 2:3]
    kc = stat[:, 3:4]
    both = jnp.concatenate([grecv[i][:, 0:GSH] for i in range(4)], axis=1)
    gains[...] = both
    cos_w = cosw[...]
    sin_w = sinw[...]

    def turn(x, sign):
        return x * cos_w + sign * pltpu.roll(x, 64, 1) * sin_w

    def normed(x, dx, inv, cross, gain):
        y = x * inv * gain
        yt = (dx * inv - x * (inv * inv * inv) * cross) * gain
        return turn(y, 1.0).astype(BF16), turn(yt, 1.0).astype(BF16)

    qk_copies = []
    for h, (cd, fd, own) in enumerate(dests):
        cols = slice(h * HD, (h + 1) * HD)
        y, yt = normed(k_ref[:, cols].astype(F32), kt_ref[:, cols].astype(F32), kr, kc, both[1:2, cols])
        ks[h, :, 0:HD] = y
        ks[h, :, HD : 2 * HD] = yt
        args = (ks.at[h], kk.at[slot], k_ss.at[h], k_rs.at[slot], (cd, fd), own)
        push(*args)
        qk_copies.append(args)
    for h, (cd, fd, own) in enumerate(dests):
        cols = slice(h * HD, (h + 1) * HD)
        y, yt = normed(q_ref[:, cols].astype(F32), qt_ref[:, cols].astype(F32), qr, qc, both[0:1, cols])
        qs[h, :, 0:HD] = yt
        qs[h, :, HD : 2 * HD] = y
        args = (qs.at[h], qq.at[slot], q_ss.at[h], q_rs.at[slot], (cd, fd), own)
        push(*args)
        qk_copies.append(args)

    for args in gain_copies + val_copies + qk_copies:
        sent(*args)
    for copy in stat_copies:
        copy.wait_send()

    @pl.when(active)
    def _():
        for t in range(SLOTS):
            arrived(vv.at[t, :, 0:HD], v_rs.at[t, 0])
            arrived(vv.at[t, :, HD : 2 * HD], v_rs.at[t, 1])
            remote(vv.at[t], vv.at[SLOTS + t], fv_ss.at[t], fv_rs.at[t], (c, sib)).start()
        for t in range(SLOTS):
            arrived(kk.at[t], k_rs.at[t])
            remote(kk.at[t], kk.at[SLOTS + t], fk_ss.at[t], fk_rs.at[t], (c, sib)).start()
        for t in range(SLOTS):
            arrived(qq.at[t], q_rs.at[t])
        for t in range(SLOTS):
            remote(vv.at[t], vv.at[SLOTS + t], fv_ss.at[t], fv_rs.at[t], (c, sib)).wait()
            remote(kk.at[t], kk.at[SLOTS + t], fk_ss.at[t], fk_rs.at[t], (c, sib)).wait()
        for t in range(2 * SLOTS):
            rows = slice(t * TOK, (t + 1) * TOK)
            vT[:, rows] = vv[t].T
            kT[:, rows] = kk[t, :, 0:HD].T

        t_val = jnp.full((8, 128), ti_ref[samp], jnp.int32).astype(F32)
        t_ang = (0.5 * math.pi) * (t_val + 0.5) / STEPS
        sin_a = jnp.sin(t_ang)[0:1, :]
        cos_a = jnp.cos(t_ang)[0:1, :]
        c_out = jnp.concatenate([sin_a * cos_a] * 2, axis=1)
        c_tan = jnp.concatenate([cos_a * cos_a] * 2, axis=1)

        per = KTILE // TOK

        def forward(rc, carry):
            qb = qq[pl.ds(rc * 2, 2)].reshape(CHUNK, 2 * HD)
            peak = jnp.full((1, CHUNK), -jnp.inf, F32)
            for kt in range(SEQ // KTILE):
                kb = kk[kt * per : (kt + 1) * per, :, 0:HD].reshape(KTILE, HD)
                sc = lax.dot_general(kb, qb[:, HD : 2 * HD], NT, preferred_element_type=F32)
                s_buf[kt * KTILE : (kt + 1) * KTILE, :] = sc
                peak = jnp.maximum(peak, jnp.max(sc, axis=0, keepdims=True))
            shift = peak * EXP2C
            lsum = jnp.zeros((1, CHUNK), F32)
            tilt = jnp.zeros((1, CHUNK), F32)
            cols = pl.ds(pl.multiple_of(rc * CHUNK, CHUNK), CHUNK)
            for kt in range(SEQ // KTILE):
                rows = slice(kt * KTILE, (kt + 1) * KTILE)
                kb = kk[kt * per : (kt + 1) * per].reshape(KTILE, 2 * HD)
                up = lax.dot_general(kb, qb, NT, preferred_element_type=F32)
                ex = jnp.exp2(s_buf[rows, :] * EXP2C - shift)
                ti = ex * up
                lsum = lsum + jnp.sum(ex, axis=0, keepdims=True)
                tilt = tilt + jnp.sum(ti, axis=0, keepdims=True)
                e_buf[rows, cols] = ex.astype(BF16)
                t_buf[rows, :] = ti.astype(BF16)
            ov = dot(vT[...], e_buf[:, cols])
            tv = dot(vT[0:HD, :], t_buf[...])
            linv = 1.0 / lsum
            out = ov[0:HD, :] * linv
            out_t = (ov[HD : 2 * HD, :] + tv * (1.0 / ROOT)) * linv - (tilt * (1.0 / ROOT)) * linv * out
            oT[rc] = out
            gT[rc] = c_out * out + c_tan * out_t
            lrow[rc] = jnp.broadcast_to(linv, (8, CHUNK))
            return carry

        lax.fori_loop(0, N_CHUNK, forward, 0)

        energy = []
        for rc in range(N_CHUNK):
            g = gT[rc]
            e = jnp.sum(g * g, axis=0, keepdims=True)
            energy += [e[:, 0:128], e[:, 128:256]]
        mine = (rank // 2) * 6 + jj
        erecv[mine] = jnp.concatenate(energy, axis=0)
        for plane in range(4):
            for j in range(6):
                idx = plane * 6 + j
                fp = 8 * samp + plane * 2 + core

                @pl.when(mine != idx)
                def _(idx=idx, cp=LOC[plane % 2][j], fp=fp):
                    remote(
                        erecv.at[mine], erecv.at[mine], e_ss.at[idx], e_rs.at[mine], (cp, fp)
                    ).start()

        def back(rc, carry):
            cols = pl.ds(pl.multiple_of(rc * CHUNK, CHUNK), CHUNK)
            cnT = (gT[rc] * (lrow[rc][0:1, :] * (1.0 / ROOT))).astype(BF16)
            drift = jnp.sum(cnT.astype(F32) * oT[rc], axis=0, keepdims=True)
            for kt in range(SEQ // KTILE):
                rows = slice(kt * KTILE, (kt + 1) * KTILE)
                vb = vv[kt * per : (kt + 1) * per, :, 0:HD].reshape(KTILE, HD)
                dp = dot(vb, cnT)
                ds_buf[rows, cols] = (e_buf[rows, cols].astype(F32) * (dp - drift)).astype(BF16)
            oT[rc] = dot(kT[...], ds_buf[:, cols])
            return carry

        lax.fori_loop(0, N_CHUNK, back, 0)

        for idx in range(24):

            @pl.when(mine != idx)
            def _(idx=idx):
                arrived(erecv.at[idx], e_rs.at[idx])

        esum = erecv[0]
        for idx in range(1, 24):
            esum = esum + erecv[idx]
        scale = loss_scale / (jnp.sqrt(esum / CHANNELS) + floor_term)
        for rc in range(N_CHUNK):
            row = jnp.concatenate([scale[2 * rc : 2 * rc + 1], scale[2 * rc + 1 : 2 * rc + 2]], axis=1)
            resq[2 * rc : 2 * rc + 2] = (oT[rc] * row).T.astype(BF16).reshape(2, TOK, HD)
            cn = gT[rc] * (lrow[rc][0:1, :] * row * (1.0 / ROOT))
            cn_buf[2 * rc : 2 * rc + 2] = cn.T.astype(BF16).reshape(2, TOK, HD)
            for t in (2 * rc, 2 * rc + 1):
                cs, fs, own = source(t)
                push(resq.at[t], retq.at[hl], r_ss.at[0, t], r_rs.at[0, hl], (cs, fs), own)
        scale_c = rows_to_cols(scale)
        for t in range(SLOTS):
            qn_buf[t * TOK : (t + 1) * TOK, :] = (
                qq[t, :, HD : 2 * HD].astype(F32) * scale_c[:, t : t + 1]
            ).astype(BF16)

        qn = qn_buf[...]
        cn_all = cn_buf[...].reshape(ROWS, HD)
        xsend[0] = dot(ds_buf[ROWS:SEQ, :], qn).astype(BF16)
        xk = remote(xsend.at[0], xrecv.at[0], x_ss.at[0], x_rs.at[0], (c, sib))
        xk.start()
        xsend[1] = dot(e_buf[ROWS:SEQ, :], cn_all).astype(BF16)
        xv = remote(xsend.at[1], xrecv.at[1], x_ss.at[1], x_rs.at[1], (c, sib))
        xv.start()
        dk = dot(ds_buf[0:ROWS, :], qn)
        xk.wait_recv()
        resk[...] = (dk + xrecv[0].astype(F32)).astype(BF16).reshape(SLOTS, TOK, HD)
        for t in range(SLOTS):
            cs, fs, own = source(t)
            push(resk.at[t], retk.at[hl], r_ss.at[1, t], r_rs.at[1, hl], (cs, fs), own)
        dv = dot(e_buf[0:ROWS, :], cn_all)
        xv.wait_recv()
        resv[...] = ((dv + xrecv[1].astype(F32)) * ROOT).astype(BF16).reshape(SLOTS, TOK, HD)
        for t in range(SLOTS):
            cs, fs, own = source(t)
            push(resv.at[t], retv.at[hl], r_ss.at[2, t], r_rs.at[2, hl], (cs, fs), own)

        xk.wait_send()
        xv.wait_send()
        for t in range(SLOTS):
            cs, fs, own = source(t)
            sent(resq.at[t], retq.at[hl], r_ss.at[0, t], r_rs.at[0, hl], (cs, fs), own)
            sent(resk.at[t], retk.at[hl], r_ss.at[1, t], r_rs.at[1, hl], (cs, fs), own)
            sent(resv.at[t], retv.at[hl], r_ss.at[2, t], r_rs.at[2, hl], (cs, fs), own)
        for plane in range(4):
            for j in range(6):
                idx = plane * 6 + j
                fp = 8 * samp + plane * 2 + core

                @pl.when(mine != idx)
                def _(idx=idx, cp=LOC[plane % 2][j], fp=fp):
                    remote(
                        erecv.at[mine], erecv.at[mine], e_ss.at[idx], e_rs.at[mine], (cp, fp)
                    ).wait_send()

    def inverse_turn(ret):
        x = ret.astype(F32)
        return x * cosw[...] - pltpu.roll(x, 64, 1) * sinw[...]

    def inv_of(i):
        return lax.rsqrt(statc[:, i : i + 1] + eps_norm)

    crosses = []
    sums = []
    for i, (x_ref, ret, tensor) in enumerate(((q_ref, retq, 0), (k_ref, retk, 1))):
        inv = inv_of(i)
        part = jnp.zeros((TOK, HD), F32)
        rows = []
        for h in range(HEADS_DEV):
            cols = slice(h * HD, (h + 1) * HD)
            arrived(ret.at[h], r_rs.at[tensor, h])
            dyx = inverse_turn(ret[h]) * x_ref[:, cols].astype(F32)
            part = part + dyx * gains[i : i + 1, cols]
            rows.append(jnp.sum(dyx * inv, axis=0, keepdims=True))
        crosses.append(rsum(part))
        sums.append(jnp.concatenate(rows, axis=1))
    crecv[rank] = cols_to_rows(crosses)
    cross_copies = []
    for i in range(1, RANKS):
        peer = samp * 8 + (rank + i) % 8
        cross_copies.append(
            remote(crecv.at[rank], crecv.at[rank], c_ss.at[i], c_rs.at[rank], (c, peer))
        )
    for copy in cross_copies:
        copy.start()
    gg_copies = []
    ggsend[...] = jnp.zeros((4, 8, 128), F32)
    for i in range(4):
        for n in range(2):
            ggsend[i, n : n + 1, 0:GSH] = sums[n][:, i * GSH : (i + 1) * GSH]
        fo = 4 * rank + i
        gg_copies.append(
            (ggsend.at[i], ggrecv.at[samp], gg_ss.at[i], gg_rs.at[samp], (c, fo), fo == f)
        )
    for args in gg_copies:
        push(*args)

    for h in range(HEADS_DEV):
        arrived(retv.at[h], r_rs.at[2, h])
        dv_out[:, h * HD : (h + 1) * HD] = retv[h]
    stores = [
        pltpu.make_async_copy(src, dst, out_sem.at[n])
        for n, (src, dst) in enumerate(
            (
                (dq_out, dq_hbm),
                (dk_out, dk_hbm),
                (dv_out, dv_hbm),
                (qgg_out, qgg_hbm),
                (kgg_out, kgg_hbm),
            )
        )
    ]
    stores[2].start()

    for s in range(SAMPLES):
        arrived(ggrecv.at[s], gg_rs.at[s])
    ffrecv[c] = ggrecv[0] + ggrecv[1] + ggrecv[2] + ggrecv[3]
    ff_copies = []
    for i in range(1, N_CTX):
        ff_copies.append(
            remote(ffrecv.at[c], ffrecv.at[c], ff_ss.at[i], ff_rs.at[c], ((c + i) % N_CTX, f))
        )
    for copy in ff_copies:
        copy.start()

    for i in range(1, RANKS):
        peer = (rank + i) % 8
        arrived(crecv.at[peer], c_rs.at[peer])
    ctot = crecv[0]
    for i in range(1, RANKS):
        ctot = ctot + crecv[i]
    cmean = rows_to_cols(ctot) / CHANNELS
    for i, (x_ref, ret, out) in enumerate(((q_ref, retq, dq_out), (k_ref, retk, dk_out))):
        inv = inv_of(i)
        pull = inv * inv * inv * cmean[:, i : i + 1]
        for h in range(HEADS_DEV):
            cols = slice(h * HD, (h + 1) * HD)
            hh = inverse_turn(ret[h]) * gains[i : i + 1, cols]
            out[:, cols] = (inv * hh - x_ref[:, cols].astype(F32) * pull).astype(BF16)
        stores[i].start()

    for i in range(1, N_CTX):
        peer = (c + i) % N_CTX
        arrived(ffrecv.at[peer], ff_rs.at[peer])
    ftot = ffrecv[0]
    for i in range(1, N_CTX):
        ftot = ftot + ffrecv[i]
    qgg_out[...] = ftot[0:1, 0:GSH]
    kgg_out[...] = ftot[1:2, 0:GSH]
    stores[3].start()
    stores[4].start()
    for copy in cross_copies + ff_copies:
        copy.wait_send()
    for args in gg_copies:
        sent(*args)
    for store in stores:
        store.wait()


def finish(*refs):
    srcs, dsts, held, sem = refs[:5], refs[5:10], refs[10:15], refs[15]
    reads = [pltpu.make_async_copy(srcs[n], held[n], sem.at[0, n]) for n in range(5)]
    writes = [pltpu.make_async_copy(held[n], dsts[n], sem.at[1, n]) for n in range(5)]
    for read in reads:
        read.start()
    for read, write in zip(reads, writes):
        read.wait()
        write.start()
    for write in writes:
        write.wait()


def per_device(
    queries,
    keys,
    values,
    query_tangent,
    key_tangent,
    value_tangent,
    query_gain,
    key_gain,
    time_index,
    shard_order,
):
    width = HEADS_DEV * HD
    vm = pl.BlockSpec(memory_space=pltpu.VMEM)
    hbm = pl.BlockSpec(memory_space=pl.ANY)
    sm = pl.BlockSpec(memory_space=pltpu.SMEM)
    dma = pltpu.SemaphoreType.DMA
    big = jax.ShapeDtypeStruct((TOK, width), BF16)
    scratch = [
        pltpu.VMEM((6, TOK, width), BF16),
        pltpu.VMEM((TOK, width), BF16),
        pltpu.VMEM((TOK, width), BF16),
        pltpu.VMEM((TOK, width), BF16),
        pltpu.VMEM((1, GSH), F32),
        pltpu.VMEM((1, GSH), F32),
        pltpu.VMEM((TOK, 128), F32),
        pltpu.VMEM((TOK, 128), F32),
        pltpu.VMEM((8, 128), F32),
        pltpu.VMEM((4, 8, 128), F32),
        pltpu.VMEM((8, 8, 128), F32),
        pltpu.VMEM((TOK, 128), F32),
        pltpu.VMEM((8, width), F32),
        pltpu.VMEM((3, TOK, 256), BF16),
        pltpu.VMEM((3, TOK, 256), BF16),
        pltpu.VMEM((SLOTS, TOK, 256), BF16),
        pltpu.VMEM((2 * SLOTS, TOK, 256), BF16),
        pltpu.VMEM((2 * SLOTS, TOK, 256), BF16),
        pltpu.VMEM((256, SEQ), BF16),
        pltpu.VMEM((128, SEQ), BF16),
        pltpu.VMEM((SEQ, CHUNK), F32),
        pltpu.VMEM((SEQ, CHUNK), BF16),
        pltpu.VMEM((SEQ, ROWS), BF16),
        pltpu.VMEM((SEQ, ROWS), BF16),
        pltpu.VMEM((SLOTS, TOK, HD), BF16),
        pltpu.VMEM((N_CHUNK, HD, CHUNK), F32),
        pltpu.VMEM((N_CHUNK, HD, CHUNK), F32),
        pltpu.VMEM((N_CHUNK, 8, CHUNK), F32),
        pltpu.VMEM((24, 8, 128), F32),
        pltpu.VMEM((ROWS, HD), BF16),
        pltpu.VMEM((SLOTS, TOK, HD), BF16),
        pltpu.VMEM((SLOTS, TOK, HD), BF16),
        pltpu.VMEM((SLOTS, TOK, HD), BF16),
        pltpu.VMEM((2, ROWS, HD), BF16),
        pltpu.VMEM((2, ROWS, HD), BF16),
        pltpu.VMEM((3, TOK, HD), BF16),
        pltpu.VMEM((3, TOK, HD), BF16),
        pltpu.VMEM((3, TOK, HD), BF16),
        pltpu.VMEM((8, 8, 128), F32),
        pltpu.VMEM((4, 8, 128), F32),
        pltpu.VMEM((4, 8, 128), F32),
        pltpu.VMEM((16, 8, 128), F32),
        dma((4,)),
        dma((4,)),
        dma((8,)),
        dma((8,)),
        dma((3, 2)),
        dma((8, 2)),
        dma((3,)),
        dma((8,)),
        dma((3,)),
        dma((8,)),
        dma((8,)),
        dma((8,)),
        dma((8,)),
        dma((8,)),
        dma((24,)),
        dma((24,)),
        dma((3, 8)),
        dma((3, 3)),
        dma((2,)),
        dma((2,)),
        dma((8,)),
        dma((8,)),
        dma((4,)),
        dma((4,)),
        dma((16,)),
        dma((16,)),
        dma((6,)),
        dma((5,)),
    ]
    small = jax.ShapeDtypeStruct((1, GSH), F32)
    outs = pl.pallas_call(
        kernel,
        out_shape=(big, big, big, small, small),
        in_specs=[sm, sm] + [hbm] * 6 + [vm] * 2,
        out_specs=(hbm,) * 5,
        scratch_shapes=scratch,
        compiler_params=pltpu.CompilerParams(
            collective_id=0, has_side_effects=True, vmem_limit_bytes=VMEM_LIMIT
        ),
        name="tangent_attention",
    )(
        shard_order,
        time_index,
        queries,
        keys,
        values,
        query_tangent,
        key_tangent,
        value_tangent,
        query_gain.reshape(1, GSH),
        key_gain.reshape(1, GSH),
    )
    outs = pl.pallas_call(
        finish,
        out_shape=(big, big, big, small, small),
        in_specs=[hbm] * 5,
        out_specs=(hbm,) * 5,
        scratch_shapes=[pltpu.VMEM(a.shape, a.dtype) for a in outs] + [dma((2, 5))],
        compiler_params=pltpu.CompilerParams(vmem_limit_bytes=VMEM_LIMIT),
        name="store_results",
    )(*outs)
    return (outs[0], outs[1], outs[2], outs[3].reshape(GSH), outs[4].reshape(GSH))


def solution(mesh):
    placed = (
        P("ctx", "fsdp"),
        P("ctx", "fsdp"),
        P("ctx", "fsdp"),
        P("ctx", "fsdp"),
        P("ctx", "fsdp"),
        P("ctx", "fsdp"),
        P("fsdp"),
        P("fsdp"),
        P(),
        P("ctx"),
    )
    return jax.shard_map(
        per_device,
        mesh=mesh,
        in_specs=placed,
        out_specs=(P("ctx", "fsdp"), P("ctx", "fsdp"), P("ctx", "fsdp"), P("fsdp"), P("fsdp")),
        check_vma=False,
    )
```

```python
import math

import jax
import jax.numpy as jnp
from jax import lax
from jax.experimental import pallas as pl
from jax.experimental.pallas import tpu as pltpu
from jax.sharding import PartitionSpec as P

MESH = pl.DeviceIdType.MESH
F32 = jnp.float32
BF16 = jnp.bfloat16

HD = 128
TOK = 128
STEPS = 1000
CHANNELS = 3072
HEADS_DEV = 3
N_CTX = 16
N_FSDP = 32
RANKS = 8
SAMPLES = 4
SLOTS = 8
ROWS = SLOTS * TOK
SEQ = 2 * ROWS
GSH = 96
CHUNK = 256
N_CHUNK = ROWS // CHUNK
KTILE = 512
EARLY = 3
VMEM_LIMIT = 63 * 1024 * 1024

eps_norm = 1e-06
loss_scale = 256.0
floor_term = 0.1
ROOT = math.sqrt(HD)
EXP2C = math.log2(math.e) / ROOT

LOC = ((0, 2, 9, 11, 4, 14), (5, 7, 14, 12, 9, 3))

NT = (((1,), (1,)), ((), ()))


def dot(a, b):
    return jnp.dot(a, b, preferred_element_type=F32)


def cols_to_rows(cols):
    lane = lax.broadcasted_iota(jnp.int32, (TOK, 128), 1)
    tile = jnp.zeros((TOK, 128), F32)
    for i, col in enumerate(cols):
        tile = jnp.where(lane == i, col, tile)
    return tile.T[0:8, :]


def rows_to_cols(rows):
    return jnp.concatenate([rows] * 16, axis=0).T


def kernel(
    so_ref,
    ti_ref,
    q_hbm,
    k_hbm,
    v_hbm,
    qt_hbm,
    kt_hbm,
    vt_hbm,
    qg_ref,
    kg_ref,
    dq_hbm,
    dk_hbm,
    dv_hbm,
    qgg_hbm,
    kgg_hbm,
    loaded,
    dq_out,
    dk_out,
    dv_out,
    qgg_out,
    kgg_out,
    cr,
    sr,
    gsend,
    grecv,
    strecv,
    statc,
    msend,
    mrecv,
    mcol,
    cosT,
    sinT,
    gain,
    qraw,
    kraw,
    qq,
    kk,
    vv,
    vT,
    kT,
    s_buf,
    t_buf,
    e_buf,
    ds_buf,
    cn_buf,
    qn_buf,
    oT,
    gT,
    dyq,
    lrow,
    trow,
    erecv,
    resq,
    resk,
    resv,
    xsend,
    xrecv,
    retq,
    retk,
    retv,
    crecv,
    ggsend,
    ggrecv,
    ggsum,
    g_ss,
    g_rs,
    st_ss,
    st_rs,
    m_ss,
    m_rs,
    v_ss,
    v_rs,
    q_ss,
    q_rs,
    k_ss,
    k_rs,
    fk_ss,
    fk_rs,
    fv_ss,
    fv_rs,
    e_ss,
    e_rs,
    r_ss,
    r_rs,
    x_ss,
    x_rs,
    c_ss,
    c_rs,
    gg_ss,
    gg_rs,
    in_sem,
    out_sem,
):
    q_ref, k_ref, v_ref, qt_ref, kt_ref, vt_ref = (loaded.at[n] for n in range(6))
    c = lax.axis_index("ctx")
    f = lax.axis_index("fsdp")
    samp = f // 8
    rank = f % 8
    ylo = (f // 2) % 2
    core = f % 2
    base = f - core
    sib = base + (1 - core)
    half = c % 2
    slot = c // 2

    dests = []
    for h in range(HEADS_DEV):
        a, b = LOC[0][h], LOC[0][3 + h]
        d, e = LOC[1][h], LOC[1][3 + h]
        cd = a + core * (b - a) + ylo * (d - a) + core * ylo * (e - d - b + a)
        fd = base + half
        dests.append((cd, fd, jnp.logical_and(cd == c, fd == f)))

    act = 0
    jj = 0
    for j in range(6):
        hit = jnp.where(c == LOC[0][j] + ylo * (LOC[1][j] - LOC[0][j]), 1, 0)
        act = act + hit
        jj = jj + j * hit
    active = act == 1
    hcore = jj // 3
    hl = jj % 3
    src_f = base + hcore

    def source(t):
        cs = 2 * t + core
        return cs, src_f, jnp.logical_and(cs == c, src_f == f)

    def remote(src, dst, ss, rs, dev):
        return pltpu.make_async_remote_copy(
            src_ref=src, dst_ref=dst, send_sem=ss, recv_sem=rs, device_id=dev, device_id_type=MESH
        )

    def push(src, dst, ss, rs, dev, own):
        @pl.when(own)
        def _():
            pltpu.make_async_copy(src, dst, rs).start()

        @pl.when(jnp.logical_not(own))
        def _():
            remote(src, dst, ss, rs, dev).start()

    def sent(src, dst, ss, rs, dev, own):
        @pl.when(jnp.logical_not(own))
        def _():
            remote(src, dst, ss, rs, dev).wait_send()

    def arrived(dst, rs):
        pltpu.make_async_copy(dst, dst, rs).wait()

    own_rank, shard = f // 4, f % 4
    head_rank = (rank // 4) * 4 + ylo * 2 + hcore
    o_ylo, o_core = (own_rank // 2) % 2, own_rank % 2
    feeds = []
    for w in range(2):
        hit = 0
        for h in range(HEADS_DEV):
            a, b = LOC[0][h], LOC[0][3 + h]
            d, e = LOC[1][h], LOC[1][3 + h]
            at = a + o_core * (b - a) + o_ylo * (d - a) + o_core * o_ylo * (e - d - b + a)
            hit = hit + jnp.where(jnp.logical_and(at == c, shard == h + w), 1, 0)
        feeds.append(hit)
    fed = []
    for s in range(SAMPLES):
        for u in range(2):
            fed.append((2 * s + own_rank // 4) * 4 + o_ylo * 2 + u)

    barrier = pltpu.get_barrier_semaphore()

    def greet(dev, own):
        @pl.when(jnp.logical_not(own))
        def _():
            pl.semaphore_signal(barrier, inc=1, device_id=dev, device_id_type=MESH)

    for i in range(1, RANKS):
        pl.semaphore_signal(
            barrier, inc=1, device_id=(c, samp * 8 + (rank + i) % 8), device_id_type=MESH
        )

    @pl.when(active)
    def _():
        for t in range(SLOTS):
            cs, fs, own = source(t)
            greet((cs, fs), own)
        for w in range(2):
            fo = 4 * head_rank + hl + w
            greet((c, fo), fo == f)

    for s in range(SAMPLES):
        fu = 8 * s + own_rank
        greet((c, fu), fu == f)

    loads = [
        pltpu.make_async_copy(src, loaded.at[n], in_sem.at[n])
        for n, src in enumerate((q_hbm, k_hbm, v_hbm, qt_hbm, kt_hbm, vt_hbm))
    ]
    for load in loads:
        load.start()

    m_id = lax.broadcasted_iota(jnp.int32, (8, 128), 1) % 64
    freq = jnp.full((8, 128), 1.0, F32)
    for bit in range(6):
        factor = 10000.0 ** (-(2.0**bit) / 64.0)
        freq = freq * jnp.where((m_id // (2**bit)) % 2 == 1, factor, 1.0)
    row_id = lax.broadcasted_iota(jnp.int32, (TOK, 128), 0)
    angle = row_id.astype(F32) * freq[0:1, :]
    cr[...] = jnp.cos(angle)
    sr[...] = jnp.sin(angle)
    gsend[...] = jnp.zeros((8, 128), F32)
    gsend[0:1, 0:GSH] = qg_ref[...]
    gsend[1:2, 0:GSH] = kg_ref[...]

    for load in loads:
        load.wait()
    qx = q_ref[...].astype(F32)
    kx = k_ref[...].astype(F32)
    qdx = qt_ref[...].astype(F32)
    kdx = kt_ref[...].astype(F32)

    def rsum(x):
        return jnp.sum(x, axis=1, keepdims=True)

    strecv[rank] = cols_to_rows([rsum(qx * qx), rsum(kx * kx), rsum(qx * qdx), rsum(kx * kdx)])

    own_heads = 0
    for cd, fd, own in dests:
        own_heads = own_heads + jnp.where(own, 1, 0)
    own_shard = jnp.where(own_rank == rank, 1, 0)
    own_fed = 0
    for fd in fed:
        own_fed = own_fed + jnp.where(fd == f, 1, 0)
    feed = feeds[0] + feeds[1]
    pl.semaphore_wait(
        barrier, (RANKS - 1) + (HEADS_DEV - own_heads) + (4 - own_shard) + feed * (8 - own_fed)
    )

    stat_copies = []
    for i in range(1, RANKS):
        peer = samp * 8 + (rank + i) % 8
        stat_copies.append(
            remote(strecv.at[rank], strecv.at[rank], st_ss.at[i], st_rs.at[rank], (c, peer))
        )
    for copy in stat_copies:
        copy.start()
    gain_copies = []
    for n, fd in enumerate(fed):
        gain_copies.append((gsend, grecv.at[feeds[1]], g_ss.at[n], g_rs.at[feeds[1]], (c, fd), fd == f))

    @pl.when(feed == 1)
    def _():
        for args in gain_copies:
            push(*args)

    tile_copies = []
    for pair, dst, ss, rs in (
        ((k_ref, kt_ref), lambda n: kraw.at[slot, n], k_ss, k_rs),
        ((q_ref, qt_ref), lambda n: qraw.at[slot, n], q_ss, q_rs),
        ((v_ref, vt_ref), lambda n: vv.at[slot, :, n * HD : (n + 1) * HD], v_ss, v_rs),
    ):
        for h, (cd, fd, own) in enumerate(dests):
            for n, ref in enumerate(pair):
                src = ref.at[:, h * HD : (h + 1) * HD]
                tile_copies.append((src, dst(n), ss.at[h, n], rs.at[slot, n], (cd, fd), own))
    for args in tile_copies:
        push(*args)

    for i in range(1, RANKS):
        peer = (rank + i) % 8
        arrived(strecv.at[peer], st_rs.at[peer])
    total = strecv[0]
    for i in range(1, RANKS):
        total = total + strecv[i]
    means = total / CHANNELS
    start = jnp.full((8, 128), so_ref[0] * TOK, jnp.int32).astype(F32)
    sub_id = lax.broadcasted_iota(jnp.int32, (8, 128), 0)
    msend[...] = jnp.where(sub_id == 4, start, means)
    meta_copies = []
    for h, (cd, fd, own) in enumerate(dests):
        meta_copies.append((msend, mrecv.at[slot], m_ss.at[h], m_rs.at[slot], (cd, fd), own))
    for args in meta_copies:
        push(*args)
    statc[...] = rows_to_cols(means)

    @pl.when(active)
    def _():
        for t in range(SLOTS):
            arrived(mrecv.at[t], m_rs.at[t])
        for w in range(2):
            arrived(grecv.at[w], g_rs.at[w])
        lane8 = lax.broadcasted_iota(jnp.int32, (8, 128), 1)
        gain[...] = jnp.where(
            lane8 < GSH - 32 * hl,
            pltpu.roll(grecv[0], (128 - 32 * hl) % 128, 1),
            pltpu.roll(grecv[1], GSH - 32 * hl, 1),
        )
        starts = jnp.concatenate([mrecv[t][4:5, :] for t in range(SLOTS)], axis=0)
        cb = jnp.cos(starts * freq)
        sb = jnp.sin(starts * freq)
        sign = jnp.where(lax.broadcasted_iota(jnp.int32, (TOK, 128), 1) < 64, -1.0, 1.0)

        def turn(x, t):
            return x * cosT[t] + pltpu.roll(x, 64, 1) * sinT[t]

        def turn_back(x, t):
            return x * cosT[t] - pltpu.roll(x, 64, 1) * sinT[t]

        def inv_of(t, i):
            return lax.rsqrt(mcol[t, :, i : i + 1] + eps_norm)

        def normed(raw, t, i):
            x = raw[t, 0].astype(F32)
            dx = raw[t, 1].astype(F32)
            inv = inv_of(t, i)
            grow = gain[i : i + 1, :]
            cross = mcol[t, :, i + 2 : i + 3]
            y = x * inv * grow
            yt = (dx * inv - x * (inv * inv * inv) * cross) * grow
            return turn(y, t).astype(BF16), turn(yt, t).astype(BF16)

        for t in range(SLOTS):
            mcol[t] = rows_to_cols(mrecv[t])
            cosT[t] = cb[t : t + 1] * cr[...] - sb[t : t + 1] * sr[...]
            sinT[t] = sign * (sb[t : t + 1] * cr[...] + cb[t : t + 1] * sr[...])
        for t in range(SLOTS):
            for n in range(2):
                arrived(kraw.at[t, n], k_rs.at[t, n])
            y, yt = normed(kraw, t, 1)
            kk[t, :, 0:HD] = y
            kk[t, :, HD : 2 * HD] = yt
            remote(kk.at[t], kk.at[SLOTS + t], fk_ss.at[t], fk_rs.at[t], (c, sib)).start()
        for t in range(SLOTS):
            for n in range(2):
                arrived(qraw.at[t, n], q_rs.at[t, n])
            y, yt = normed(qraw, t, 0)
            qq[t, :, 0:HD] = yt
            qq[t, :, HD : 2 * HD] = y
        for t in range(SLOTS):
            remote(kk.at[t], kk.at[SLOTS + t], fk_ss.at[t], fk_rs.at[t], (c, sib)).wait()

        t_val = jnp.full((8, 128), ti_ref[samp], jnp.int32).astype(F32)
        t_ang = (0.5 * math.pi) * (t_val + 0.5) / STEPS
        sin_a = jnp.sin(t_ang)[0:1, :]
        cos_a = jnp.cos(t_ang)[0:1, :]
        c_out = jnp.concatenate([sin_a * cos_a] * 2, axis=1)
        c_tan = jnp.concatenate([cos_a * cos_a] * 2, axis=1)

        per = KTILE // TOK

        def weigh(rc, carry):
            qb = qq[pl.ds(rc * 2, 2)].reshape(CHUNK, 2 * HD)
            peak = jnp.full((1, CHUNK), -jnp.inf, F32)
            for kt in range(SEQ // KTILE):
                kb = kk[kt * per : (kt + 1) * per, :, 0:HD].reshape(KTILE, HD)
                sc = lax.dot_general(kb, qb[:, HD : 2 * HD], NT, preferred_element_type=F32)
                s_buf[kt * KTILE : (kt + 1) * KTILE, :] = sc
                peak = jnp.maximum(peak, jnp.max(sc, axis=0, keepdims=True))
            shift = peak * EXP2C
            lsum = jnp.zeros((1, CHUNK), F32)
            tilt = jnp.zeros((1, CHUNK), F32)
            cols = pl.ds(pl.multiple_of(rc * CHUNK, CHUNK), CHUNK)
            for kt in range(SEQ // KTILE):
                rows = slice(kt * KTILE, (kt + 1) * KTILE)
                kb = kk[kt * per : (kt + 1) * per].reshape(KTILE, 2 * HD)
                up = lax.dot_general(kb, qb, NT, preferred_element_type=F32)
                ex = jnp.exp2(s_buf[rows, :] * EXP2C - shift)
                ti = ex * up
                lsum = lsum + jnp.sum(ex, axis=0, keepdims=True)
                tilt = tilt + jnp.sum(ti, axis=0, keepdims=True)
                e_buf[rows, cols] = ex.astype(BF16)
                t_buf[rows, cols] = ti.astype(BF16)
            linv = 1.0 / lsum
            lrow[rc] = jnp.broadcast_to(linv, (8, CHUNK))
            trow[rc] = jnp.broadcast_to(tilt * (1.0 / ROOT) * linv, (8, CHUNK))
            return carry

        lax.fori_loop(0, EARLY, weigh, 0)
        for t in range(SLOTS):
            arrived(vv.at[t, :, 0:HD], v_rs.at[t, 0])
            arrived(vv.at[t, :, HD : 2 * HD], v_rs.at[t, 1])
            remote(vv.at[t], vv.at[SLOTS + t], fv_ss.at[t], fv_rs.at[t], (c, sib)).start()
        lax.fori_loop(EARLY, N_CHUNK, weigh, 0)
        for t in range(SLOTS):
            vT[:, t * TOK : (t + 1) * TOK] = vv[t].T
        for t in range(SLOTS):
            rows = slice((SLOTS + t) * TOK, (SLOTS + t + 1) * TOK)
            remote(vv.at[t], vv.at[SLOTS + t], fv_ss.at[t], fv_rs.at[t], (c, sib)).wait()
            vT[:, rows] = vv[SLOTS + t].T

        def combine(rc, carry):
            cols = pl.ds(pl.multiple_of(rc * CHUNK, CHUNK), CHUNK)
            ov = dot(vT[...], e_buf[:, cols])
            tv = dot(vT[0:HD, :], t_buf[:, cols])
            linv = lrow[rc][0:1, :]
            out = ov[0:HD, :] * linv
            out_t = (ov[HD : 2 * HD, :] + tv * (1.0 / ROOT)) * linv - trow[rc][0:1, :] * out
            oT[rc] = out
            gT[rc] = c_out * out + c_tan * out_t
            return carry

        lax.fori_loop(0, N_CHUNK, combine, 0)

        energy = []
        for rc in range(N_CHUNK):
            g = gT[rc]
            e = jnp.sum(g * g, axis=0, keepdims=True)
            energy += [e[:, 0:128], e[:, 128:256]]
        mine = (rank // 2) * 6 + jj
        erecv[mine] = jnp.concatenate(energy, axis=0)
        for plane in range(4):
            for j in range(6):
                idx = plane * 6 + j
                fp = 8 * samp + plane * 2 + core

                @pl.when(mine != idx)
                def _(idx=idx, cp=LOC[plane % 2][j], fp=fp):
                    remote(
                        erecv.at[mine], erecv.at[mine], e_ss.at[idx], e_rs.at[mine], (cp, fp)
                    ).start()

        for t in range(2 * SLOTS):
            kT[:, t * TOK : (t + 1) * TOK] = kk[t, :, 0:HD].T

        def back(rc, carry):
            cols = pl.ds(pl.multiple_of(rc * CHUNK, CHUNK), CHUNK)
            cnT = (gT[rc] * (lrow[rc][0:1, :] * (1.0 / ROOT))).astype(BF16)
            drift = jnp.sum(cnT.astype(F32) * oT[rc], axis=0, keepdims=True)
            for kt in range(SEQ // KTILE):
                rows = slice(kt * KTILE, (kt + 1) * KTILE)
                vb = vv[kt * per : (kt + 1) * per, :, 0:HD].reshape(KTILE, HD)
                dp = dot(vb, cnT)
                ds_buf[rows, cols] = (e_buf[rows, cols].astype(F32) * (dp - drift)).astype(BF16)
            oT[rc] = dot(kT[...], ds_buf[:, cols])
            return carry

        lax.fori_loop(0, N_CHUNK, back, 0)
        for t in range(SLOTS):
            dyq[t] = turn_back(oT[t // 2, :, (t % 2) * TOK : (t % 2 + 1) * TOK].T, t)

        for idx in range(24):

            @pl.when(mine != idx)
            def _(idx=idx):
                arrived(erecv.at[idx], e_rs.at[idx])

        esum = erecv[0]
        for idx in range(1, 24):
            esum = esum + erecv[idx]
        scale = loss_scale / (jnp.sqrt(esum / CHANNELS) + floor_term)
        scale_c = rows_to_cols(scale)
        for t in range(SLOTS):
            qn_buf[t * TOK : (t + 1) * TOK, :] = (
                qq[t, :, HD : 2 * HD].astype(F32) * scale_c[:, t : t + 1]
            ).astype(BF16)
        qn = qn_buf[...]

        def finished(dy, t, i, raw):
            inv = inv_of(t, i)
            part = jnp.sum(dy * raw[t, 0].astype(F32) * inv, axis=0, keepdims=True)
            return (dy * inv * gain[i : i + 1, :]).astype(BF16), part

        ggq = jnp.zeros((1, HD), F32)
        for t in range(SLOTS):
            cs, fs, own = source(t)
            resq[t], part = finished(dyq[t] * scale_c[:, t : t + 1], t, 0, qraw)
            ggq = ggq + part
            push(resq.at[t], retq.at[hl], r_ss.at[0, t], r_rs.at[0, hl], (cs, fs), own)

        xsend[0] = dot(ds_buf[ROWS:SEQ, :], qn).astype(BF16)
        xk = remote(xsend.at[0], xrecv.at[0], x_ss.at[0], x_rs.at[0], (c, sib))
        xk.start()
        for rc in range(N_CHUNK):
            row = jnp.concatenate([scale[2 * rc : 2 * rc + 1], scale[2 * rc + 1 : 2 * rc + 2]], axis=1)
            cn = gT[rc] * (lrow[rc][0:1, :] * row * (1.0 / ROOT))
            cn_buf[2 * rc : 2 * rc + 2] = cn.T.astype(BF16).reshape(2, TOK, HD)
        cn_all = cn_buf[...].reshape(ROWS, HD)
        xsend[1] = dot(e_buf[ROWS:SEQ, :], cn_all).astype(BF16)
        xv = remote(xsend.at[1], xrecv.at[1], x_ss.at[1], x_rs.at[1], (c, sib))
        xv.start()

        dk = dot(ds_buf[0:ROWS, :], qn)
        xk.wait_recv()
        ggk = jnp.zeros((1, HD), F32)
        for t in range(SLOTS):
            cs, fs, own = source(t)
            rows = slice(t * TOK, (t + 1) * TOK)
            dkt = dk[rows, :] + xrecv[0, rows, :].astype(F32)
            resk[t], part = finished(turn_back(dkt, t), t, 1, kraw)
            ggk = ggk + part
            push(resk.at[t], retk.at[hl], r_ss.at[1, t], r_rs.at[1, hl], (cs, fs), own)
        ggsend[...] = jnp.where(sub_id == 0, ggq, ggk)
        member = samp * 2 + core
        gg_copies = []
        for i in range(N_CTX):
            for w in range(2):
                fo = 4 * head_rank + hl + w
                own = fo == f if i == 0 else fo < 0
                gg_copies.append(
                    (
                        ggsend,
                        ggrecv.at[w, member],
                        gg_ss.at[i, w],
                        gg_rs.at[w, member],
                        ((c + i) % N_CTX, fo),
                        own,
                    )
                )
        for n, args in enumerate(gg_copies):
            if n < 2:
                push(*args)
            else:
                remote(*args[:5]).start()
        dv = dot(e_buf[0:ROWS, :], cn_all)
        xv.wait_recv()
        for t in range(SLOTS):
            cs, fs, own = source(t)
            rows = slice(t * TOK, (t + 1) * TOK)
            resv[t] = ((dv[rows, :] + xrecv[1, rows, :].astype(F32)) * ROOT).astype(BF16)
            push(resv.at[t], retv.at[hl], r_ss.at[2, t], r_rs.at[2, hl], (cs, fs), own)

        xk.wait_send()
        xv.wait_send()
        for n, args in enumerate(gg_copies):
            if n < 2:
                sent(*args)
            else:
                remote(*args[:5]).wait_send()
        for t in range(SLOTS):
            cs, fs, own = source(t)
            sent(resq.at[t], retq.at[hl], r_ss.at[0, t], r_rs.at[0, hl], (cs, fs), own)
            sent(resk.at[t], retk.at[hl], r_ss.at[1, t], r_rs.at[1, hl], (cs, fs), own)
            sent(resv.at[t], retv.at[hl], r_ss.at[2, t], r_rs.at[2, hl], (cs, fs), own)
        for plane in range(4):
            for j in range(6):
                idx = plane * 6 + j
                fp = 8 * samp + plane * 2 + core

                @pl.when(mine != idx)
                def _(idx=idx, cp=LOC[plane % 2][j], fp=fp):
                    remote(
                        erecv.at[mine], erecv.at[mine], e_ss.at[idx], e_rs.at[mine], (cp, fp)
                    ).wait_send()

    crosses = []
    for x_ref, ret, tensor in ((q_ref, retq, 0), (k_ref, retk, 1)):
        part = jnp.zeros((TOK, HD), F32)
        for h in range(HEADS_DEV):
            arrived(ret.at[h], r_rs.at[tensor, h])
            part = part + ret[h].astype(F32) * x_ref[:, h * HD : (h + 1) * HD].astype(F32)
        crosses.append(rsum(part))
    crecv[rank] = cols_to_rows(crosses)
    cross_copies = []
    for i in range(1, RANKS):
        peer = samp * 8 + (rank + i) % 8
        cross_copies.append(
            remote(crecv.at[rank], crecv.at[rank], c_ss.at[i], c_rs.at[rank], (c, peer))
        )
    for copy in cross_copies:
        copy.start()

    stores = [
        pltpu.make_async_copy(src, dst, out_sem.at[n])
        for n, (src, dst) in enumerate(
            (
                (dq_out, dq_hbm),
                (dk_out, dk_hbm),
                (dv_out, dv_hbm),
                (qgg_out, qgg_hbm),
                (kgg_out, kgg_hbm),
            )
        )
    ]
    for h in range(HEADS_DEV):
        arrived(retv.at[h], r_rs.at[2, h])
        dv_out[:, h * HD : (h + 1) * HD] = retv[h]
    stores[2].start()

    for i in range(1, RANKS):
        peer = (rank + i) % 8
        arrived(crecv.at[peer], c_rs.at[peer])
    ctot = crecv[0]
    for i in range(1, RANKS):
        ctot = ctot + crecv[i]
    cmean = rows_to_cols(ctot) / CHANNELS
    for i, (x_ref, ret, out) in enumerate(((q_ref, retq, dq_out), (k_ref, retk, dk_out))):
        pull = cmean[:, i : i + 1] / (statc[:, i : i + 1] + eps_norm)
        for h in range(HEADS_DEV):
            cols = slice(h * HD, (h + 1) * HD)
            out[:, cols] = (ret[h].astype(F32) - x_ref[:, cols].astype(F32) * pull).astype(BF16)
        stores[i].start()

    for w in range(2):
        some = shard != 3 if w == 0 else shard != 0

        @pl.when(some)
        def _(w=w):
            for n in range(8):
                arrived(ggrecv.at[w, n], gg_rs.at[w, n])
            acc = ggrecv[w, 0]
            for n in range(1, 8):
                acc = acc + ggrecv[w, n]
            ggsum[w] = pltpu.roll(acc, 32 * shard, 1)

        @pl.when(jnp.logical_not(some))
        def _(w=w):
            ggsum[w] = jnp.zeros((8, 128), F32)

    glane = lax.broadcasted_iota(jnp.int32, (8, 128), 1)
    gg = jnp.where(glane < 32 * shard, ggsum[1], ggsum[0])
    qgg_out[...] = gg[0:1, 0:GSH]
    kgg_out[...] = gg[1:2, 0:GSH]
    stores[3].start()
    stores[4].start()

    for copy in stat_copies + cross_copies:
        copy.wait_send()
    for args in tile_copies + meta_copies:
        sent(*args)

    @pl.when(feed == 1)
    def _():
        for args in gain_copies:
            sent(*args)

    for store in stores:
        store.wait()


def finish(*refs):
    srcs, dsts, held, sem = refs[:5], refs[5:10], refs[10:15], refs[15]
    reads = [pltpu.make_async_copy(srcs[n], held[n], sem.at[0, n]) for n in range(5)]
    writes = [pltpu.make_async_copy(held[n], dsts[n], sem.at[1, n]) for n in range(5)]
    for read in reads:
        read.start()
    for read, write in zip(reads, writes):
        read.wait()
        write.start()
    for write in writes:
        write.wait()


def per_device(
    queries,
    keys,
    values,
    query_tangent,
    key_tangent,
    value_tangent,
    query_gain,
    key_gain,
    time_index,
    shard_order,
):
    width = HEADS_DEV * HD
    vm = pl.BlockSpec(memory_space=pltpu.VMEM)
    hbm = pl.BlockSpec(memory_space=pl.ANY)
    sm = pl.BlockSpec(memory_space=pltpu.SMEM)
    dma = pltpu.SemaphoreType.DMA
    big = jax.ShapeDtypeStruct((TOK, width), BF16)
    scratch = [
        pltpu.VMEM((6, TOK, width), BF16),
        pltpu.VMEM((TOK, width), BF16),
        pltpu.VMEM((TOK, width), BF16),
        pltpu.VMEM((TOK, width), BF16),
        pltpu.VMEM((1, GSH), F32),
        pltpu.VMEM((1, GSH), F32),
        pltpu.VMEM((TOK, 128), F32),
        pltpu.VMEM((TOK, 128), F32),
        pltpu.VMEM((8, 128), F32),
        pltpu.VMEM((2, 8, 128), F32),
        pltpu.VMEM((8, 8, 128), F32),
        pltpu.VMEM((TOK, 128), F32),
        pltpu.VMEM((8, 128), F32),
        pltpu.VMEM((SLOTS, 8, 128), F32),
        pltpu.VMEM((SLOTS, TOK, 128), F32),
        pltpu.VMEM((SLOTS, TOK, 128), F32),
        pltpu.VMEM((SLOTS, TOK, 128), F32),
        pltpu.VMEM((8, 128), F32),
        pltpu.VMEM((SLOTS, 2, TOK, HD), BF16),
        pltpu.VMEM((SLOTS, 2, TOK, HD), BF16),
        pltpu.VMEM((SLOTS, TOK, 256), BF16),
        pltpu.VMEM((2 * SLOTS, TOK, 256), BF16),
        pltpu.VMEM((2 * SLOTS, TOK, 256), BF16),
        pltpu.VMEM((256, SEQ), BF16),
        pltpu.VMEM((128, SEQ), BF16),
        pltpu.VMEM((SEQ, CHUNK), F32),
        pltpu.VMEM((SEQ, ROWS), BF16),
        pltpu.VMEM((SEQ, ROWS), BF16),
        pltpu.VMEM((SEQ, ROWS), BF16),
        pltpu.VMEM((SLOTS, TOK, HD), BF16),
        pltpu.VMEM((ROWS, HD), BF16),
        pltpu.VMEM((N_CHUNK, HD, CHUNK), F32),
        pltpu.VMEM((N_CHUNK, HD, CHUNK), F32),
        pltpu.VMEM((SLOTS, TOK, HD), F32),
        pltpu.VMEM((N_CHUNK, 8, CHUNK), F32),
        pltpu.VMEM((N_CHUNK, 8, CHUNK), F32),
        pltpu.VMEM((24, 8, 128), F32),
        pltpu.VMEM((SLOTS, TOK, HD), BF16),
        pltpu.VMEM((SLOTS, TOK, HD), BF16),
        pltpu.VMEM((SLOTS, TOK, HD), BF16),
        pltpu.VMEM((2, ROWS, HD), BF16),
        pltpu.VMEM((2, ROWS, HD), BF16),
        pltpu.VMEM((3, TOK, HD), BF16),
        pltpu.VMEM((3, TOK, HD), BF16),
        pltpu.VMEM((3, TOK, HD), BF16),
        pltpu.VMEM((8, 8, 128), F32),
        pltpu.VMEM((8, 128), F32),
        pltpu.VMEM((2, 8, 8, 128), F32),
        pltpu.VMEM((2, 8, 128), F32),
        dma((8,)),
        dma((2,)),
        dma((8,)),
        dma((8,)),
        dma((3,)),
        dma((8,)),
        dma((3, 2)),
        dma((8, 2)),
        dma((3, 2)),
        dma((8, 2)),
        dma((3, 2)),
        dma((8, 2)),
        dma((8,)),
        dma((8,)),
        dma((8,)),
        dma((8,)),
        dma((24,)),
        dma((24,)),
        dma((3, 8)),
        dma((3, 3)),
        dma((2,)),
        dma((2,)),
        dma((8,)),
        dma((8,)),
        dma((16, 2)),
        dma((2, 8)),
        dma((6,)),
        dma((5,)),
    ]
    small = jax.ShapeDtypeStruct((1, GSH), F32)
    outs = pl.pallas_call(
        kernel,
        out_shape=(big, big, big, small, small),
        in_specs=[sm, sm] + [hbm] * 6 + [vm] * 2,
        out_specs=(hbm,) * 5,
        scratch_shapes=scratch,
        compiler_params=pltpu.CompilerParams(
            collective_id=0, has_side_effects=True, vmem_limit_bytes=VMEM_LIMIT
        ),
        name="tangent_attention",
    )(
        shard_order,
        time_index,
        queries,
        keys,
        values,
        query_tangent,
        key_tangent,
        value_tangent,
        query_gain.reshape(1, GSH),
        key_gain.reshape(1, GSH),
    )
    outs = pl.pallas_call(
        finish,
        out_shape=(big, big, big, small, small),
        in_specs=[hbm] * 5,
        out_specs=(hbm,) * 5,
        scratch_shapes=[pltpu.VMEM(a.shape, a.dtype) for a in outs] + [dma((2, 5))],
        compiler_params=pltpu.CompilerParams(vmem_limit_bytes=VMEM_LIMIT),
        name="store_results",
    )(*outs)
    return (outs[0], outs[1], outs[2], outs[3].reshape(GSH), outs[4].reshape(GSH))


def solution(mesh):
    placed = (
        P("ctx", "fsdp"),
        P("ctx", "fsdp"),
        P("ctx", "fsdp"),
        P("ctx", "fsdp"),
        P("ctx", "fsdp"),
        P("ctx", "fsdp"),
        P("fsdp"),
        P("fsdp"),
        P(),
        P("ctx"),
    )
    return jax.shard_map(
        per_device,
        mesh=mesh,
        in_specs=placed,
        out_specs=(P("ctx", "fsdp"), P("ctx", "fsdp"), P("ctx", "fsdp"), P("fsdp"), P("fsdp")),
        check_vma=False,
    )
```

```python
import math

import jax
import jax.numpy as jnp
from jax import lax
from jax.experimental import pallas as pl
from jax.experimental.pallas import tpu as pltpu
from jax.sharding import PartitionSpec as P

MESH = pl.DeviceIdType.MESH
F32 = jnp.float32
BF16 = jnp.bfloat16

HD = 128
TOK = 128
STEPS = 1000
CHANNELS = 3072
HEADS_DEV = 3
N_CTX = 16
N_FSDP = 32
RANKS = 8
SAMPLES = 4
SLOTS = 8
ROWS = SLOTS * TOK
SEQ = 2 * ROWS
GSH = 96
CHUNK = 256
N_CHUNK = ROWS // CHUNK
KTILE = 512
EARLY = 3
VMEM_LIMIT = 63 * 1024 * 1024

eps_norm = 1e-06
loss_scale = 256.0
floor_term = 0.1
ROOT = math.sqrt(HD)
EXP2C = math.log2(math.e) / ROOT

LOC = ((1, 3, 10, 8, 5, 15), (6, 4, 15, 13, 10, 0))

NT = (((1,), (1,)), ((), ()))


def dot(a, b):
    return jnp.dot(a, b, preferred_element_type=F32)


def cols_to_rows(cols):
    lane = lax.broadcasted_iota(jnp.int32, (TOK, 128), 1)
    tile = jnp.zeros((TOK, 128), F32)
    for i, col in enumerate(cols):
        tile = jnp.where(lane == i, col, tile)
    return tile.T[0:8, :]


def rows_to_cols(rows):
    return jnp.concatenate([rows] * 16, axis=0).T


def kernel(
    so_ref,
    ti_ref,
    q_hbm,
    k_hbm,
    v_hbm,
    qt_hbm,
    kt_hbm,
    vt_hbm,
    qg_ref,
    kg_ref,
    dq_hbm,
    dk_hbm,
    dv_hbm,
    qgg_hbm,
    kgg_hbm,
    loaded,
    dq_out,
    dk_out,
    dv_out,
    qgg_out,
    kgg_out,
    cr,
    sr,
    gsend,
    grecv,
    strecv,
    statc,
    msend,
    mrecv,
    mcol,
    cosT,
    sinT,
    gain,
    qraw,
    kraw,
    qq,
    kk,
    vv,
    vT,
    kT,
    s_buf,
    t_buf,
    e_buf,
    ds_buf,
    cn_buf,
    qn_buf,
    oT,
    gT,
    dyq,
    lrow,
    trow,
    erecv,
    resq,
    resk,
    resv,
    xsend,
    xrecv,
    retq,
    retk,
    retv,
    crecv,
    ggsend,
    ggrecv,
    ffsend,
    ffrecv,
    csend,
    cpart,
    g_ss,
    g_rs,
    st_ss,
    st_rs,
    m_ss,
    m_rs,
    v_ss,
    v_rs,
    q_ss,
    q_rs,
    k_ss,
    k_rs,
    fk_ss,
    fk_rs,
    fv_ss,
    fv_rs,
    e_ss,
    e_rs,
    r_ss,
    r_rs,
    x_ss,
    x_rs,
    c_ss,
    c_rs,
    gg_ss,
    gg_rs,
    ff_ss,
    ff_rs,
    p_ss,
    p_rs,
    in_sem,
    out_sem,
):
    q_ref, k_ref, v_ref, qt_ref, kt_ref, vt_ref = (loaded.at[n] for n in range(6))
    c = lax.axis_index("ctx")
    f = lax.axis_index("fsdp")
    samp = f // 8
    rank = f % 8
    ylo = (f // 2) % 2
    core = f % 2
    base = f - core
    sib = base + (1 - core)
    half = c % 2
    slot = c // 2

    dests = []
    for h in range(HEADS_DEV):
        a, b = LOC[0][h], LOC[0][3 + h]
        d, e = LOC[1][h], LOC[1][3 + h]
        cd = a + core * (b - a) + ylo * (d - a) + core * ylo * (e - d - b + a)
        fd = base + half
        dests.append((cd, fd, jnp.logical_and(cd == c, fd == f)))

    act = 0
    jj = 0
    for j in range(6):
        hit = jnp.where(c == LOC[0][j] + ylo * (LOC[1][j] - LOC[0][j]), 1, 0)
        act = act + hit
        jj = jj + j * hit
    active = act == 1
    hcore = jj // 3
    hl = jj % 3
    src_f = base + hcore

    def source(t):
        cs = 2 * t + core
        return cs, src_f, jnp.logical_and(cs == c, src_f == f)

    def remote(src, dst, ss, rs, dev):
        return pltpu.make_async_remote_copy(
            src_ref=src, dst_ref=dst, send_sem=ss, recv_sem=rs, device_id=dev, device_id_type=MESH
        )

    def push(src, dst, ss, rs, dev, own):
        @pl.when(own)
        def _():
            pltpu.make_async_copy(src, dst, rs).start()

        @pl.when(jnp.logical_not(own))
        def _():
            remote(src, dst, ss, rs, dev).start()

    def sent(src, dst, ss, rs, dev, own):
        @pl.when(jnp.logical_not(own))
        def _():
            remote(src, dst, ss, rs, dev).wait_send()

    def arrived(dst, rs):
        pltpu.make_async_copy(dst, dst, rs).wait()

    own_rank, shard = f // 4, f % 4
    head_rank = (rank // 4) * 4 + ylo * 2 + hcore
    o_ylo, o_core = (own_rank // 2) % 2, own_rank % 2
    feeds = []
    for w in range(2):
        hit = 0
        for h in range(HEADS_DEV):
            a, b = LOC[0][h], LOC[0][3 + h]
            d, e = LOC[1][h], LOC[1][3 + h]
            at = a + o_core * (b - a) + o_ylo * (d - a) + o_core * o_ylo * (e - d - b + a)
            hit = hit + jnp.where(jnp.logical_and(at == c, shard == h + w), 1, 0)
        feeds.append(hit)
    fed = []
    for s in range(SAMPLES):
        for u in range(2):
            fed.append((2 * s + own_rank // 4) * 4 + o_ylo * 2 + u)

    barrier = pltpu.get_barrier_semaphore()

    def greet(dev, own):
        @pl.when(jnp.logical_not(own))
        def _():
            pl.semaphore_signal(barrier, inc=1, device_id=dev, device_id_type=MESH)

    for i in range(1, RANKS):
        pl.semaphore_signal(
            barrier, inc=1, device_id=(c, samp * 8 + (rank + i) % 8), device_id_type=MESH
        )

    @pl.when(active)
    def _():
        for t in range(SLOTS):
            cs, fs, own = source(t)
            greet((cs, fs), own)
        for w in range(2):
            fo = 4 * head_rank + hl + w
            greet((c, fo), fo == f)

    loads = [
        pltpu.make_async_copy(src, loaded.at[n], in_sem.at[n])
        for n, src in enumerate((q_hbm, k_hbm, v_hbm, qt_hbm, kt_hbm, vt_hbm))
    ]
    for load in loads:
        load.start()

    m_id = lax.broadcasted_iota(jnp.int32, (8, 128), 1) % 64
    freq = jnp.full((8, 128), 1.0, F32)
    for bit in range(6):
        factor = 10000.0 ** (-(2.0**bit) / 64.0)
        freq = freq * jnp.where((m_id // (2**bit)) % 2 == 1, factor, 1.0)
    row_id = lax.broadcasted_iota(jnp.int32, (TOK, 128), 0)
    angle = row_id.astype(F32) * freq[0:1, :]
    cr[...] = jnp.cos(angle)
    sr[...] = jnp.sin(angle)
    gsend[...] = jnp.zeros((8, 128), F32)
    gsend[0:1, 0:GSH] = qg_ref[...]
    gsend[1:2, 0:GSH] = kg_ref[...]

    for load in loads:
        load.wait()
    qx = q_ref[...].astype(F32)
    kx = k_ref[...].astype(F32)
    qdx = qt_ref[...].astype(F32)
    kdx = kt_ref[...].astype(F32)

    def rsum(x):
        return jnp.sum(x, axis=1, keepdims=True)

    strecv[rank] = cols_to_rows([rsum(qx * qx), rsum(kx * kx), rsum(qx * qdx), rsum(kx * kdx)])

    own_heads = 0
    for cd, fd, own in dests:
        own_heads = own_heads + jnp.where(own, 1, 0)
    own_fed = 0
    for fd in fed:
        own_fed = own_fed + jnp.where(fd == f, 1, 0)
    feed = feeds[0] + feeds[1]
    pl.semaphore_wait(
        barrier, (RANKS - 1) + (HEADS_DEV - own_heads) + feed * (8 - own_fed)
    )

    stat_copies = []
    for i in range(1, RANKS):
        peer = samp * 8 + (rank + i) % 8
        stat_copies.append(
            remote(strecv.at[rank], strecv.at[rank], st_ss.at[i], st_rs.at[rank], (c, peer))
        )
    for copy in stat_copies:
        copy.start()
    gain_copies = []
    for n, fd in enumerate(fed):
        gain_copies.append((gsend, grecv.at[feeds[1]], g_ss.at[n], g_rs.at[feeds[1]], (c, fd), fd == f))

    @pl.when(feed == 1)
    def _():
        for args in gain_copies:
            push(*args)

    tile_copies = []
    for pair, dst, ss, rs in (
        ((k_ref, kt_ref), lambda n: kraw.at[slot, n], k_ss, k_rs),
        ((q_ref, qt_ref), lambda n: qraw.at[slot, n], q_ss, q_rs),
        ((v_ref, vt_ref), lambda n: vv.at[slot, :, n * HD : (n + 1) * HD], v_ss, v_rs),
    ):
        for h, (cd, fd, own) in enumerate(dests):
            for n, ref in enumerate(pair):
                src = ref.at[:, h * HD : (h + 1) * HD]
                tile_copies.append((src, dst(n), ss.at[h, n], rs.at[slot, n], (cd, fd), own))
    for args in tile_copies:
        push(*args)

    for i in range(1, RANKS):
        peer = (rank + i) % 8
        arrived(strecv.at[peer], st_rs.at[peer])
    total = strecv[0]
    for i in range(1, RANKS):
        total = total + strecv[i]
    means = total / CHANNELS
    start = jnp.full((8, 128), so_ref[0] * TOK, jnp.int32).astype(F32)
    sub_id = lax.broadcasted_iota(jnp.int32, (8, 128), 0)
    msend[...] = jnp.where(sub_id == 4, start, means)
    meta_copies = []
    for h, (cd, fd, own) in enumerate(dests):
        meta_copies.append((msend, mrecv.at[slot], m_ss.at[h], m_rs.at[slot], (cd, fd), own))
    for args in meta_copies:
        push(*args)
    statc[...] = rows_to_cols(means)

    mine = (rank // 2) * 6 + jj
    gg_copies = []
    for w in range(2):
        fo = 4 * head_rank + hl + w
        dst = ggrecv.at[samp * 2 + core]
        gg_copies.append((ggsend, dst, gg_ss.at[w], gg_rs.at[samp * 2 + core], (c, fo), fo == f))

    @pl.when(active)
    def _():
        for t in range(SLOTS):
            arrived(mrecv.at[t], m_rs.at[t])
        for w in range(2):
            arrived(grecv.at[w], g_rs.at[w])
        lane8 = lax.broadcasted_iota(jnp.int32, (8, 128), 1)
        gain[...] = jnp.where(
            lane8 < GSH - 32 * hl,
            pltpu.roll(grecv[0], (128 - 32 * hl) % 128, 1),
            pltpu.roll(grecv[1], GSH - 32 * hl, 1),
        )
        starts = jnp.concatenate([mrecv[t][4:5, :] for t in range(SLOTS)], axis=0)
        cb = jnp.cos(starts * freq)
        sb = jnp.sin(starts * freq)
        sign = jnp.where(lax.broadcasted_iota(jnp.int32, (TOK, 128), 1) < 64, -1.0, 1.0)

        def turn(x, t):
            return x * cosT[t] + pltpu.roll(x, 64, 1) * sinT[t]

        def turn_back(x, t):
            return x * cosT[t] - pltpu.roll(x, 64, 1) * sinT[t]

        def inv_of(t, i):
            return lax.rsqrt(mcol[t, :, i : i + 1] + eps_norm)

        def normed(raw, t, i):
            x = raw[t, 0].astype(F32)
            dx = raw[t, 1].astype(F32)
            inv = inv_of(t, i)
            grow = gain[i : i + 1, :]
            cross = mcol[t, :, i + 2 : i + 3]
            y = x * inv * grow
            yt = (dx * inv - x * (inv * inv * inv) * cross) * grow
            return turn(y, t).astype(BF16), turn(yt, t).astype(BF16)

        for t in range(SLOTS):
            mcol[t] = rows_to_cols(mrecv[t])
            cosT[t] = cb[t : t + 1] * cr[...] - sb[t : t + 1] * sr[...]
            sinT[t] = sign * (sb[t : t + 1] * cr[...] + cb[t : t + 1] * sr[...])
        for t in range(SLOTS):
            for n in range(2):
                arrived(kraw.at[t, n], k_rs.at[t, n])
            y, yt = normed(kraw, t, 1)
            kk[t, :, 0:HD] = y
            kk[t, :, HD : 2 * HD] = yt
            remote(kk.at[t], kk.at[SLOTS + t], fk_ss.at[t], fk_rs.at[t], (c, sib)).start()
        for t in range(SLOTS):
            for n in range(2):
                arrived(qraw.at[t, n], q_rs.at[t, n])
            y, yt = normed(qraw, t, 0)
            qq[t, :, 0:HD] = yt
            qq[t, :, HD : 2 * HD] = y
        for t in range(SLOTS):
            remote(kk.at[t], kk.at[SLOTS + t], fk_ss.at[t], fk_rs.at[t], (c, sib)).wait()

        t_val = jnp.full((8, 128), ti_ref[samp], jnp.int32).astype(F32)
        t_ang = (0.5 * math.pi) * (t_val + 0.5) / STEPS
        sin_a = jnp.sin(t_ang)[0:1, :]
        cos_a = jnp.cos(t_ang)[0:1, :]
        c_out = jnp.concatenate([sin_a * cos_a] * 2, axis=1)
        c_tan = jnp.concatenate([cos_a * cos_a] * 2, axis=1)

        per = KTILE // TOK

        def weigh(rc, carry):
            qb = qq[pl.ds(rc * 2, 2)].reshape(CHUNK, 2 * HD)
            peak = jnp.full((1, CHUNK), -jnp.inf, F32)
            for kt in range(SEQ // KTILE):
                kb = kk[kt * per : (kt + 1) * per, :, 0:HD].reshape(KTILE, HD)
                sc = lax.dot_general(kb, qb[:, HD : 2 * HD], NT, preferred_element_type=F32)
                s_buf[kt * KTILE : (kt + 1) * KTILE, :] = sc
                peak = jnp.maximum(peak, jnp.max(sc, axis=0, keepdims=True))
            shift = peak * EXP2C
            lsum = jnp.zeros((1, CHUNK), F32)
            tilt = jnp.zeros((1, CHUNK), F32)
            cols = pl.ds(pl.multiple_of(rc * CHUNK, CHUNK), CHUNK)
            for kt in range(SEQ // KTILE):
                rows = slice(kt * KTILE, (kt + 1) * KTILE)
                kb = kk[kt * per : (kt + 1) * per].reshape(KTILE, 2 * HD)
                up = lax.dot_general(kb, qb, NT, preferred_element_type=F32)
                ex = jnp.exp2(s_buf[rows, :] * EXP2C - shift)
                ti = ex * up
                lsum = lsum + jnp.sum(ex, axis=0, keepdims=True)
                tilt = tilt + jnp.sum(ti, axis=0, keepdims=True)
                e_buf[rows, cols] = ex.astype(BF16)
                t_buf[rows, cols] = ti.astype(BF16)
            linv = 1.0 / lsum
            lrow[rc] = jnp.broadcast_to(linv, (8, CHUNK))
            trow[rc] = jnp.broadcast_to(tilt * (1.0 / ROOT) * linv, (8, CHUNK))
            return carry

        lax.fori_loop(0, EARLY, weigh, 0)
        for t in range(SLOTS):
            arrived(vv.at[t, :, 0:HD], v_rs.at[t, 0])
            arrived(vv.at[t, :, HD : 2 * HD], v_rs.at[t, 1])
            remote(vv.at[t], vv.at[SLOTS + t], fv_ss.at[t], fv_rs.at[t], (c, sib)).start()
        lax.fori_loop(EARLY, N_CHUNK, weigh, 0)
        for t in range(SLOTS):
            vT[:, t * TOK : (t + 1) * TOK] = vv[t].T
        for t in range(SLOTS):
            rows = slice((SLOTS + t) * TOK, (SLOTS + t + 1) * TOK)
            remote(vv.at[t], vv.at[SLOTS + t], fv_ss.at[t], fv_rs.at[t], (c, sib)).wait()
            vT[:, rows] = vv[SLOTS + t].T

        def combine(rc, carry):
            cols = pl.ds(pl.multiple_of(rc * CHUNK, CHUNK), CHUNK)
            ov = dot(vT[...], e_buf[:, cols])
            tv = dot(vT[0:HD, :], t_buf[:, cols])
            linv = lrow[rc][0:1, :]
            out = ov[0:HD, :] * linv
            out_t = (ov[HD : 2 * HD, :] + tv * (1.0 / ROOT)) * linv - trow[rc][0:1, :] * out
            oT[rc] = out
            gT[rc] = c_out * out + c_tan * out_t
            return carry

        lax.fori_loop(0, N_CHUNK, combine, 0)

        energy = []
        for rc in range(N_CHUNK):
            g = gT[rc]
            e = jnp.sum(g * g, axis=0, keepdims=True)
            energy += [e[:, 0:128], e[:, 128:256]]
        erecv[mine] = jnp.concatenate(energy, axis=0)
        for plane in range(4):
            for j in range(6):
                idx = plane * 6 + j
                fp = 8 * samp + plane * 2 + core

                @pl.when(mine != idx)
                def _(idx=idx, cp=LOC[plane % 2][j], fp=fp):
                    remote(
                        erecv.at[mine], erecv.at[mine], e_ss.at[idx], e_rs.at[mine], (cp, fp)
                    ).start()

        for t in range(2 * SLOTS):
            kT[:, t * TOK : (t + 1) * TOK] = kk[t, :, 0:HD].T

        def back(rc, carry):
            cols = pl.ds(pl.multiple_of(rc * CHUNK, CHUNK), CHUNK)
            cnT = (gT[rc] * (lrow[rc][0:1, :] * (1.0 / ROOT))).astype(BF16)
            drift = jnp.sum(cnT.astype(F32) * oT[rc], axis=0, keepdims=True)
            for kt in range(SEQ // KTILE):
                rows = slice(kt * KTILE, (kt + 1) * KTILE)
                vb = vv[kt * per : (kt + 1) * per, :, 0:HD].reshape(KTILE, HD)
                dp = dot(vb, cnT)
                ds_buf[rows, cols] = (e_buf[rows, cols].astype(F32) * (dp - drift)).astype(BF16)
            oT[rc] = dot(kT[...], ds_buf[:, cols])
            return carry

        lax.fori_loop(0, N_CHUNK, back, 0)
        for t in range(SLOTS):
            dyq[t] = turn_back(oT[t // 2, :, (t % 2) * TOK : (t % 2 + 1) * TOK].T, t)

        for idx in range(24):

            @pl.when(mine != idx)
            def _(idx=idx):
                arrived(erecv.at[idx], e_rs.at[idx])

        esum = erecv[0]
        for idx in range(1, 24):
            esum = esum + erecv[idx]
        scale = loss_scale / (jnp.sqrt(esum / CHANNELS) + floor_term)
        scale_c = rows_to_cols(scale)
        for t in range(SLOTS):
            qn_buf[t * TOK : (t + 1) * TOK, :] = (
                qq[t, :, HD : 2 * HD].astype(F32) * scale_c[:, t : t + 1]
            ).astype(BF16)
        qn = qn_buf[...]

        def finished(dy, t, i, raw):
            x = raw[t, 0].astype(F32)
            scaled = dy * inv_of(t, i)
            grad = scaled * gain[i : i + 1, :]
            part = jnp.sum(scaled * x, axis=0, keepdims=True)
            return grad.astype(BF16), part, rsum(grad * x)

        ggq = jnp.zeros((1, HD), F32)
        crosses = []
        for t in range(SLOTS):
            cs, fs, own = source(t)
            resq[t], part, cross = finished(dyq[t] * scale_c[:, t : t + 1], t, 0, qraw)
            ggq = ggq + part
            crosses.append(cross)
            push(resq.at[t], retq.at[hl], r_ss.at[0, t], r_rs.at[0, hl], (cs, fs), own)

        xsend[0] = dot(ds_buf[ROWS:SEQ, :], qn).astype(BF16)
        xk = remote(xsend.at[0], xrecv.at[0], x_ss.at[0], x_rs.at[0], (c, sib))
        xk.start()
        for rc in range(N_CHUNK):
            row = jnp.concatenate([scale[2 * rc : 2 * rc + 1], scale[2 * rc + 1 : 2 * rc + 2]], axis=1)
            cn = gT[rc] * (lrow[rc][0:1, :] * row * (1.0 / ROOT))
            cn_buf[2 * rc : 2 * rc + 2] = cn.T.astype(BF16).reshape(2, TOK, HD)
        cn_all = cn_buf[...].reshape(ROWS, HD)
        xsend[1] = dot(e_buf[ROWS:SEQ, :], cn_all).astype(BF16)
        xv = remote(xsend.at[1], xrecv.at[1], x_ss.at[1], x_rs.at[1], (c, sib))
        xv.start()

        dk = dot(ds_buf[0:ROWS, :], qn)
        xk.wait_recv()
        ggk = jnp.zeros((1, HD), F32)
        for t in range(SLOTS):
            rows = slice(t * TOK, (t + 1) * TOK)
            dkt = dk[rows, :] + xrecv[0, rows, :].astype(F32)
            resk[t], part, cross = finished(turn_back(dkt, t), t, 1, kraw)
            ggk = ggk + part
            crosses.append(cross)
        lane_id = lax.broadcasted_iota(jnp.int32, (TOK, 128), 1)
        ctile = jnp.zeros((TOK, 128), F32)
        for n, cross in enumerate(crosses):
            ctile = jnp.where(lane_id == n, cross, ctile)
        ctile = ctile.T
        for t in range(SLOTS):
            cs, fs, own = source(t)
            csend[t] = jnp.where(
                sub_id == 0, ctile[t : t + 1, :], ctile[SLOTS + t : SLOTS + t + 1, :]
            )
            push(csend.at[t], cpart.at[hl], p_ss.at[t], p_rs.at[hl], (cs, fs), own)
        for t in range(SLOTS):
            cs, fs, own = source(t)
            push(resk.at[t], retk.at[hl], r_ss.at[1, t], r_rs.at[1, hl], (cs, fs), own)
        ggsend[...] = jnp.where(sub_id == 0, ggq, ggk)
        for args in gg_copies:
            push(*args)
        dv = dot(e_buf[0:ROWS, :], cn_all)
        xv.wait_recv()
        for t in range(SLOTS):
            cs, fs, own = source(t)
            rows = slice(t * TOK, (t + 1) * TOK)
            resv[t] = ((dv[rows, :] + xrecv[1, rows, :].astype(F32)) * ROOT).astype(BF16)
            push(resv.at[t], retv.at[hl], r_ss.at[2, t], r_rs.at[2, hl], (cs, fs), own)

    for h in range(HEADS_DEV):
        arrived(cpart.at[h], p_rs.at[h])
    crecv[rank] = cpart[0] + cpart[1] + cpart[2]
    cross_copies = []
    for i in range(1, RANKS):
        peer = samp * 8 + (rank + i) % 8
        cross_copies.append(
            remote(crecv.at[rank], crecv.at[rank], c_ss.at[i], c_rs.at[rank], (c, peer))
        )
    for copy in cross_copies:
        copy.start()

    ff_copies = []
    for i in range(N_CTX):
        ff_copies.append(
            (
                ffsend,
                ffrecv.at[feeds[1]],
                ff_ss.at[i],
                ff_rs.at[feeds[1]],
                ((c + i) % N_CTX, f),
            )
        )

    @pl.when(feed == 1)
    def _():
        for n in range(8):
            arrived(ggrecv.at[n], gg_rs.at[n])
        acc = ggrecv[0]
        for n in range(1, 8):
            acc = acc + ggrecv[n]
        ffsend[...] = pltpu.roll(acc, 32 * shard, 1)
        pltpu.make_async_copy(ffsend, ffrecv.at[feeds[1]], ff_rs.at[feeds[1]]).start()
        for args in ff_copies[1:]:
            remote(*args).start()

    stores = [
        pltpu.make_async_copy(src, dst, out_sem.at[n])
        for n, (src, dst) in enumerate(
            (
                (dq_out, dq_hbm),
                (dk_out, dk_hbm),
                (dv_out, dv_hbm),
                (qgg_out, qgg_hbm),
                (kgg_out, kgg_hbm),
            )
        )
    ]
    for h in range(HEADS_DEV):
        arrived(retq.at[h], r_rs.at[0, h])
        arrived(retk.at[h], r_rs.at[1, h])
    for i in range(1, RANKS):
        peer = (rank + i) % 8
        arrived(crecv.at[peer], c_rs.at[peer])
    ctot = crecv[0]
    for i in range(1, RANKS):
        ctot = ctot + crecv[i]
    cmean = rows_to_cols(ctot) / CHANNELS
    for i, (x_ref, ret, out) in enumerate(((q_ref, retq, dq_out), (k_ref, retk, dk_out))):
        pull = cmean[:, i : i + 1] / (statc[:, i : i + 1] + eps_norm)
        for h in range(HEADS_DEV):
            cols = slice(h * HD, (h + 1) * HD)
            out[:, cols] = (ret[h].astype(F32) - x_ref[:, cols].astype(F32) * pull).astype(BF16)
        stores[i].start()

    for h in range(HEADS_DEV):
        arrived(retv.at[h], r_rs.at[2, h])
        dv_out[:, h * HD : (h + 1) * HD] = retv[h]
    stores[2].start()

    for w in range(2):
        some = shard != 3 if w == 0 else shard != 0

        @pl.when(some)
        def _(w=w):
            arrived(ffrecv.at[w], ff_rs.at[w])

        @pl.when(jnp.logical_not(some))
        def _(w=w):
            ffrecv[w] = jnp.zeros((8, 128), F32)

    glane = lax.broadcasted_iota(jnp.int32, (8, 128), 1)
    gg = jnp.where(glane < 32 * shard, ffrecv[1], ffrecv[0])
    qgg_out[...] = gg[0:1, 0:GSH]
    kgg_out[...] = gg[1:2, 0:GSH]
    stores[3].start()
    stores[4].start()

    for copy in stat_copies + cross_copies:
        copy.wait_send()
    for args in tile_copies + meta_copies:
        sent(*args)

    @pl.when(feed == 1)
    def _():
        for args in gain_copies:
            sent(*args)
        for args in ff_copies[1:]:
            remote(*args).wait_send()

    @pl.when(active)
    def _():
        for n in range(2):
            remote(xsend.at[n], xrecv.at[n], x_ss.at[n], x_rs.at[n], (c, sib)).wait_send()
        for args in gg_copies:
            sent(*args)
        for t in range(SLOTS):
            cs, fs, own = source(t)
            sent(csend.at[t], cpart.at[hl], p_ss.at[t], p_rs.at[hl], (cs, fs), own)
            sent(resq.at[t], retq.at[hl], r_ss.at[0, t], r_rs.at[0, hl], (cs, fs), own)
            sent(resk.at[t], retk.at[hl], r_ss.at[1, t], r_rs.at[1, hl], (cs, fs), own)
            sent(resv.at[t], retv.at[hl], r_ss.at[2, t], r_rs.at[2, hl], (cs, fs), own)
        for plane in range(4):
            for j in range(6):
                idx = plane * 6 + j
                fp = 8 * samp + plane * 2 + core

                @pl.when(mine != idx)
                def _(idx=idx, cp=LOC[plane % 2][j], fp=fp):
                    remote(
                        erecv.at[mine], erecv.at[mine], e_ss.at[idx], e_rs.at[mine], (cp, fp)
                    ).wait_send()

    for store in stores:
        store.wait()


def finish(*refs):
    srcs, dsts, held, sem = refs[:5], refs[5:10], refs[10:15], refs[15]
    reads = [pltpu.make_async_copy(srcs[n], held[n], sem.at[0, n]) for n in range(5)]
    writes = [pltpu.make_async_copy(held[n], dsts[n], sem.at[1, n]) for n in range(5)]
    for read in reads:
        read.start()
    for read, write in zip(reads, writes):
        read.wait()
        write.start()
    for write in writes:
        write.wait()


def per_device(
    queries,
    keys,
    values,
    query_tangent,
    key_tangent,
    value_tangent,
    query_gain,
    key_gain,
    time_index,
    shard_order,
):
    width = HEADS_DEV * HD
    vm = pl.BlockSpec(memory_space=pltpu.VMEM)
    hbm = pl.BlockSpec(memory_space=pl.ANY)
    sm = pl.BlockSpec(memory_space=pltpu.SMEM)
    dma = pltpu.SemaphoreType.DMA
    big = jax.ShapeDtypeStruct((TOK, width), BF16)
    scratch = [
        pltpu.VMEM((6, TOK, width), BF16),
        pltpu.VMEM((TOK, width), BF16),
        pltpu.VMEM((TOK, width), BF16),
        pltpu.VMEM((TOK, width), BF16),
        pltpu.VMEM((1, GSH), F32),
        pltpu.VMEM((1, GSH), F32),
        pltpu.VMEM((TOK, 128), F32),
        pltpu.VMEM((TOK, 128), F32),
        pltpu.VMEM((8, 128), F32),
        pltpu.VMEM((2, 8, 128), F32),
        pltpu.VMEM((8, 8, 128), F32),
        pltpu.VMEM((TOK, 128), F32),
        pltpu.VMEM((8, 128), F32),
        pltpu.VMEM((SLOTS, 8, 128), F32),
        pltpu.VMEM((SLOTS, TOK, 128), F32),
        pltpu.VMEM((SLOTS, TOK, 128), F32),
        pltpu.VMEM((SLOTS, TOK, 128), F32),
        pltpu.VMEM((8, 128), F32),
        pltpu.VMEM((SLOTS, 2, TOK, HD), BF16),
        pltpu.VMEM((SLOTS, 2, TOK, HD), BF16),
        pltpu.VMEM((SLOTS, TOK, 256), BF16),
        pltpu.VMEM((2 * SLOTS, TOK, 256), BF16),
        pltpu.VMEM((2 * SLOTS, TOK, 256), BF16),
        pltpu.VMEM((256, SEQ), BF16),
        pltpu.VMEM((128, SEQ), BF16),
        pltpu.VMEM((SEQ, CHUNK), F32),
        pltpu.VMEM((SEQ, ROWS), BF16),
        pltpu.VMEM((SEQ, ROWS), BF16),
        pltpu.VMEM((SEQ, ROWS), BF16),
        pltpu.VMEM((SLOTS, TOK, HD), BF16),
        pltpu.VMEM((ROWS, HD), BF16),
        pltpu.VMEM((N_CHUNK, HD, CHUNK), F32),
        pltpu.VMEM((N_CHUNK, HD, CHUNK), F32),
        pltpu.VMEM((SLOTS, TOK, HD), F32),
        pltpu.VMEM((N_CHUNK, 8, CHUNK), F32),
        pltpu.VMEM((N_CHUNK, 8, CHUNK), F32),
        pltpu.VMEM((24, 8, 128), F32),
        pltpu.VMEM((SLOTS, TOK, HD), BF16),
        pltpu.VMEM((SLOTS, TOK, HD), BF16),
        pltpu.VMEM((SLOTS, TOK, HD), BF16),
        pltpu.VMEM((2, ROWS, HD), BF16),
        pltpu.VMEM((2, ROWS, HD), BF16),
        pltpu.VMEM((3, TOK, HD), BF16),
        pltpu.VMEM((3, TOK, HD), BF16),
        pltpu.VMEM((3, TOK, HD), BF16),
        pltpu.VMEM((8, 8, 128), F32),
        pltpu.VMEM((8, 128), F32),
        pltpu.VMEM((8, 8, 128), F32),
        pltpu.VMEM((8, 128), F32),
        pltpu.VMEM((2, 8, 128), F32),
        pltpu.VMEM((SLOTS, 8, 128), F32),
        pltpu.VMEM((3, 8, 128), F32),
        dma((8,)),
        dma((2,)),
        dma((8,)),
        dma((8,)),
        dma((3,)),
        dma((8,)),
        dma((3, 2)),
        dma((8, 2)),
        dma((3, 2)),
        dma((8, 2)),
        dma((3, 2)),
        dma((8, 2)),
        dma((8,)),
        dma((8,)),
        dma((8,)),
        dma((8,)),
        dma((24,)),
        dma((24,)),
        dma((3, 8)),
        dma((3, 3)),
        dma((2,)),
        dma((2,)),
        dma((8,)),
        dma((8,)),
        dma((2,)),
        dma((8,)),
        dma((16,)),
        dma((2,)),
        dma((8,)),
        dma((3,)),
        dma((6,)),
        dma((5,)),
    ]
    small = jax.ShapeDtypeStruct((1, GSH), F32)
    outs = pl.pallas_call(
        kernel,
        out_shape=(big, big, big, small, small),
        in_specs=[sm, sm] + [hbm] * 6 + [vm] * 2,
        out_specs=(hbm,) * 5,
        scratch_shapes=scratch,
        compiler_params=pltpu.CompilerParams(
            collective_id=0, has_side_effects=True, vmem_limit_bytes=VMEM_LIMIT
        ),
        name="tangent_attention",
    )(
        shard_order,
        time_index,
        queries,
        keys,
        values,
        query_tangent,
        key_tangent,
        value_tangent,
        query_gain.reshape(1, GSH),
        key_gain.reshape(1, GSH),
    )
    outs = pl.pallas_call(
        finish,
        out_shape=(big, big, big, small, small),
        in_specs=[hbm] * 5,
        out_specs=(hbm,) * 5,
        scratch_shapes=[pltpu.VMEM(a.shape, a.dtype) for a in outs] + [dma((2, 5))],
        compiler_params=pltpu.CompilerParams(vmem_limit_bytes=VMEM_LIMIT),
        name="store_results",
    )(*outs)
    return (outs[0], outs[1], outs[2], outs[3].reshape(GSH), outs[4].reshape(GSH))


def solution(mesh):
    placed = (
        P("ctx", "fsdp"),
        P("ctx", "fsdp"),
        P("ctx", "fsdp"),
        P("ctx", "fsdp"),
        P("ctx", "fsdp"),
        P("ctx", "fsdp"),
        P("fsdp"),
        P("fsdp"),
        P(),
        P("ctx"),
    )
    return jax.shard_map(
        per_device,
        mesh=mesh,
        in_specs=placed,
        out_specs=(P("ctx", "fsdp"), P("ctx", "fsdp"), P("ctx", "fsdp"), P("fsdp"), P("fsdp")),
        check_vma=False,
    )
```

```python
import math

import jax
import jax.numpy as jnp
from jax import lax
from jax.experimental import pallas as pl
from jax.experimental.pallas import tpu as pltpu
from jax.sharding import PartitionSpec as P

MESH = pl.DeviceIdType.MESH
F32 = jnp.float32
BF16 = jnp.bfloat16

HD = 128
TOK = 128
STEPS = 1000
CHANNELS = 3072
HEADS_DEV = 3
N_CTX = 16
N_FSDP = 32
RANKS = 8
SAMPLES = 4
SLOTS = 8
ROWS = SLOTS * TOK
SEQ = 2 * ROWS
GSH = 96
CHUNK = 256
N_CHUNK = ROWS // CHUNK
KTILE = 512
EARLY = 3
VMEM_LIMIT = 63 * 1024 * 1024

eps_norm = 1e-06
loss_scale = 256.0
floor_term = 0.1
ROOT = math.sqrt(HD)
EXP2C = math.log2(math.e) / ROOT

LOC = ((1, 3, 10, 8, 5, 15), (6, 4, 15, 13, 10, 0))

NT = (((1,), (1,)), ((), ()))


def dot(a, b):
    return jnp.dot(a, b, preferred_element_type=F32)


def cols_to_rows(cols):
    lane = lax.broadcasted_iota(jnp.int32, (TOK, 128), 1)
    tile = jnp.zeros((TOK, 128), F32)
    for i, col in enumerate(cols):
        tile = jnp.where(lane == i, col, tile)
    return tile.T[0:8, :]


def rows_to_cols(rows):
    return jnp.concatenate([rows] * 16, axis=0).T


def kernel(
    so_ref,
    ti_ref,
    q_hbm,
    k_hbm,
    v_hbm,
    qt_hbm,
    kt_hbm,
    vt_hbm,
    qg_ref,
    kg_ref,
    dq_hbm,
    dk_hbm,
    dv_hbm,
    qgg_hbm,
    kgg_hbm,
    loaded,
    dq_out,
    dk_out,
    dv_out,
    qgg_out,
    kgg_out,
    cr,
    sr,
    gsend,
    grecv,
    strecv,
    statc,
    msend,
    mrecv,
    mcol,
    cosT,
    sinT,
    gain,
    qraw,
    kraw,
    qq,
    kk,
    vv,
    vT,
    kT,
    s_buf,
    t_buf,
    e_buf,
    ds_buf,
    cn_buf,
    qn_buf,
    oT,
    gT,
    dyq,
    lrow,
    trow,
    erecv,
    resq,
    resk,
    resv,
    xsend,
    xrecv,
    retq,
    retk,
    retv,
    crecv,
    ggsend,
    ggrecv,
    ffsend,
    ffrecv,
    csend,
    cpart,
    g_ss,
    g_rs,
    st_ss,
    st_rs,
    m_ss,
    m_rs,
    v_ss,
    v_rs,
    q_ss,
    q_rs,
    k_ss,
    k_rs,
    fk_ss,
    fk_rs,
    fv_ss,
    fv_rs,
    e_ss,
    e_rs,
    r_ss,
    r_rs,
    x_ss,
    x_rs,
    c_ss,
    c_rs,
    gg_ss,
    gg_rs,
    ff_ss,
    ff_rs,
    p_ss,
    p_rs,
    in_sem,
    out_sem,
):
    q_ref, k_ref, v_ref, qt_ref, kt_ref, vt_ref = (loaded.at[n] for n in range(6))
    c = lax.axis_index("ctx")
    f = lax.axis_index("fsdp")
    samp = f // 8
    rank = f % 8
    ylo = (f // 2) % 2
    core = f % 2
    base = f - core
    sib = base + (1 - core)
    half = c % 2
    slot = c // 2

    dests = []
    for h in range(HEADS_DEV):
        a, b = LOC[0][h], LOC[0][3 + h]
        d, e = LOC[1][h], LOC[1][3 + h]
        cd = a + core * (b - a) + ylo * (d - a) + core * ylo * (e - d - b + a)
        fd = base + half
        dests.append((cd, fd, jnp.logical_and(cd == c, fd == f)))

    act = 0
    jj = 0
    for j in range(6):
        hit = jnp.where(c == LOC[0][j] + ylo * (LOC[1][j] - LOC[0][j]), 1, 0)
        act = act + hit
        jj = jj + j * hit
    active = act == 1
    hcore = jj // 3
    hl = jj % 3
    src_f = base + hcore

    def source(t):
        cs = 2 * t + core
        return cs, src_f, jnp.logical_and(cs == c, src_f == f)

    def remote(src, dst, ss, rs, dev):
        return pltpu.make_async_remote_copy(
            src_ref=src, dst_ref=dst, send_sem=ss, recv_sem=rs, device_id=dev, device_id_type=MESH
        )

    def push(src, dst, ss, rs, dev, own):
        @pl.when(own)
        def _():
            pltpu.make_async_copy(src, dst, rs).start()

        @pl.when(jnp.logical_not(own))
        def _():
            remote(src, dst, ss, rs, dev).start()

    def sent(src, dst, ss, rs, dev, own):
        @pl.when(jnp.logical_not(own))
        def _():
            remote(src, dst, ss, rs, dev).wait_send()

    def arrived(dst, rs):
        pltpu.make_async_copy(dst, dst, rs).wait()

    own_rank, shard = f // 4, f % 4
    head_rank = (rank // 4) * 4 + ylo * 2 + hcore
    o_ylo, o_core = (own_rank // 2) % 2, own_rank % 2
    feeds = []
    for w in range(2):
        hit = 0
        for h in range(HEADS_DEV):
            a, b = LOC[0][h], LOC[0][3 + h]
            d, e = LOC[1][h], LOC[1][3 + h]
            at = a + o_core * (b - a) + o_ylo * (d - a) + o_core * o_ylo * (e - d - b + a)
            hit = hit + jnp.where(jnp.logical_and(at == c, shard == h + w), 1, 0)
        feeds.append(hit)
    fed = []
    for s in range(SAMPLES):
        for u in range(2):
            fed.append((2 * s + own_rank // 4) * 4 + o_ylo * 2 + u)

    barrier = pltpu.get_barrier_semaphore()

    def greet(dev, own):
        @pl.when(jnp.logical_not(own))
        def _():
            pl.semaphore_signal(barrier, inc=1, device_id=dev, device_id_type=MESH)

    for i in range(1, RANKS):
        pl.semaphore_signal(
            barrier, inc=1, device_id=(c, samp * 8 + (rank + i) % 8), device_id_type=MESH
        )

    @pl.when(active)
    def _():
        for t in range(SLOTS):
            cs, fs, own = source(t)
            greet((cs, fs), own)
        for w in range(2):
            fo = 4 * head_rank + hl + w
            greet((c, fo), fo == f)

    loads = [
        pltpu.make_async_copy(src, loaded.at[n], in_sem.at[n])
        for n, src in enumerate((q_hbm, k_hbm, v_hbm, qt_hbm, kt_hbm, vt_hbm))
    ]
    for load in loads:
        load.start()

    m_id = lax.broadcasted_iota(jnp.int32, (8, 128), 1) % 64
    freq = jnp.full((8, 128), 1.0, F32)
    for bit in range(6):
        factor = 10000.0 ** (-(2.0**bit) / 64.0)
        freq = freq * jnp.where((m_id // (2**bit)) % 2 == 1, factor, 1.0)
    row_id = lax.broadcasted_iota(jnp.int32, (TOK, 128), 0)
    angle = row_id.astype(F32) * freq[0:1, :]
    cr[...] = jnp.cos(angle)
    sr[...] = jnp.sin(angle)
    gsend[...] = jnp.zeros((8, 128), F32)
    gsend[0:1, 0:GSH] = qg_ref[...]
    gsend[1:2, 0:GSH] = kg_ref[...]

    for load in loads:
        load.wait()
    qx = q_ref[...].astype(F32)
    kx = k_ref[...].astype(F32)
    qdx = qt_ref[...].astype(F32)
    kdx = kt_ref[...].astype(F32)

    def rsum(x):
        return jnp.sum(x, axis=1, keepdims=True)

    strecv[rank] = cols_to_rows([rsum(qx * qx), rsum(kx * kx), rsum(qx * qdx), rsum(kx * kdx)])

    own_heads = 0
    for cd, fd, own in dests:
        own_heads = own_heads + jnp.where(own, 1, 0)
    own_fed = 0
    for fd in fed:
        own_fed = own_fed + jnp.where(fd == f, 1, 0)
    feed = feeds[0] + feeds[1]
    pl.semaphore_wait(
        barrier, (RANKS - 1) + (HEADS_DEV - own_heads) + feed * (8 - own_fed)
    )

    stat_copies = []
    for i in range(1, RANKS):
        peer = samp * 8 + (rank + i) % 8
        stat_copies.append(
            remote(strecv.at[rank], strecv.at[rank], st_ss.at[i], st_rs.at[rank], (c, peer))
        )
    for copy in stat_copies:
        copy.start()
    gain_copies = []
    for n, fd in enumerate(fed):
        gain_copies.append((gsend, grecv.at[feeds[1]], g_ss.at[n], g_rs.at[feeds[1]], (c, fd), fd == f))

    @pl.when(feed == 1)
    def _():
        for args in gain_copies:
            push(*args)

    tile_copies = []
    for pair, dst, ss, rs in (
        ((k_ref, kt_ref), lambda n: kraw.at[slot, n], k_ss, k_rs),
        ((q_ref, qt_ref), lambda n: qraw.at[slot, n], q_ss, q_rs),
        ((v_ref, vt_ref), lambda n: vv.at[slot, :, n * HD : (n + 1) * HD], v_ss, v_rs),
    ):
        for h, (cd, fd, own) in enumerate(dests):
            for n, ref in enumerate(pair):
                src = ref.at[:, h * HD : (h + 1) * HD]
                tile_copies.append((src, dst(n), ss.at[h, n], rs.at[slot, n], (cd, fd), own))
    ahead = 4 * HEADS_DEV
    for args in tile_copies[:ahead]:
        push(*args)

    for i in range(1, RANKS):
        peer = (rank + i) % 8
        arrived(strecv.at[peer], st_rs.at[peer])
    total = strecv[0]
    for i in range(1, RANKS):
        total = total + strecv[i]
    means = total / CHANNELS
    start = jnp.full((8, 128), so_ref[0] * TOK, jnp.int32).astype(F32)
    sub_id = lax.broadcasted_iota(jnp.int32, (8, 128), 0)
    msend[...] = jnp.where(sub_id == 4, start, means)
    meta_copies = []
    for h, (cd, fd, own) in enumerate(dests):
        meta_copies.append((msend, mrecv.at[slot], m_ss.at[h], m_rs.at[slot], (cd, fd), own))
    for args in meta_copies + tile_copies[ahead:]:
        push(*args)
    statc[...] = rows_to_cols(means)

    mine = (rank // 2) * 6 + jj
    gg_copies = []
    for w in range(2):
        fo = 4 * head_rank + hl + w
        dst = ggrecv.at[samp * 2 + core]
        gg_copies.append((ggsend, dst, gg_ss.at[w], gg_rs.at[samp * 2 + core], (c, fo), fo == f))

    @pl.when(active)
    def _():
        for w in range(2):
            arrived(grecv.at[w], g_rs.at[w])
        lane8 = lax.broadcasted_iota(jnp.int32, (8, 128), 1)
        gain[...] = jnp.where(
            lane8 < GSH - 32 * hl,
            pltpu.roll(grecv[0], (128 - 32 * hl) % 128, 1),
            pltpu.roll(grecv[1], GSH - 32 * hl, 1),
        )
        sign = jnp.where(lax.broadcasted_iota(jnp.int32, (TOK, 128), 1) < 64, -1.0, 1.0)

        def turn(x, t):
            return x * cosT[t] + pltpu.roll(x, 64, 1) * sinT[t]

        def turn_back(x, t):
            return x * cosT[t] - pltpu.roll(x, 64, 1) * sinT[t]

        def inv_of(t, i):
            return lax.rsqrt(mcol[t, :, i : i + 1] + eps_norm)

        def normed(raw, t, i):
            x = raw[t, 0].astype(F32)
            dx = raw[t, 1].astype(F32)
            inv = inv_of(t, i)
            grow = gain[i : i + 1, :]
            cross = mcol[t, :, i + 2 : i + 3]
            y = x * inv * grow
            yt = (dx * inv - x * (inv * inv * inv) * cross) * grow
            return turn(y, t).astype(BF16), turn(yt, t).astype(BF16)

        def take_keys(t):
            arrived(mrecv.at[t], m_rs.at[t])
            at = mrecv[t][4:5, :] * freq
            cb = jnp.cos(at)[0:1, :]
            sb = jnp.sin(at)[0:1, :]
            mcol[t] = rows_to_cols(mrecv[t])
            cosT[t] = cb * cr[...] - sb * sr[...]
            sinT[t] = sign * (sb * cr[...] + cb * sr[...])
            for n in range(2):
                arrived(kraw.at[t, n], k_rs.at[t, n])
            y, yt = normed(kraw, t, 1)
            kk[t, :, 0:HD] = y
            kk[t, :, HD : 2 * HD] = yt
            remote(kk.at[t], kk.at[SLOTS + t], fk_ss.at[t], fk_rs.at[t], (c, sib)).start()

        def take_queries(t):
            for n in range(2):
                arrived(qraw.at[t, n], q_rs.at[t, n])
            y, yt = normed(qraw, t, 0)
            qq[t, :, 0:HD] = yt
            qq[t, :, HD : 2 * HD] = y

        for t in range(SLOTS - 1, 0, -1):
            take_keys(t)
        for t in range(SLOTS - 1, 0, -1):
            take_queries(t)
        take_keys(0)
        take_queries(0)
        for t in range(SLOTS):
            remote(kk.at[t], kk.at[SLOTS + t], fk_ss.at[t], fk_rs.at[t], (c, sib)).wait()

        t_val = jnp.full((8, 128), ti_ref[samp], jnp.int32).astype(F32)
        t_ang = (0.5 * math.pi) * (t_val + 0.5) / STEPS
        sin_a = jnp.sin(t_ang)[0:1, :]
        cos_a = jnp.cos(t_ang)[0:1, :]
        c_out = jnp.concatenate([sin_a * cos_a] * 2, axis=1)
        c_tan = jnp.concatenate([cos_a * cos_a] * 2, axis=1)

        per = KTILE // TOK

        def weigh(rc, carry):
            qb = qq[pl.ds(rc * 2, 2)].reshape(CHUNK, 2 * HD)
            peak = jnp.full((1, CHUNK), -jnp.inf, F32)
            for kt in range(SEQ // KTILE):
                kb = kk[kt * per : (kt + 1) * per, :, 0:HD].reshape(KTILE, HD)
                sc = lax.dot_general(kb, qb[:, HD : 2 * HD], NT, preferred_element_type=F32)
                s_buf[kt * KTILE : (kt + 1) * KTILE, :] = sc
                peak = jnp.maximum(peak, jnp.max(sc, axis=0, keepdims=True))
            shift = peak * EXP2C
            lsum = jnp.zeros((1, CHUNK), F32)
            tilt = jnp.zeros((1, CHUNK), F32)
            cols = pl.ds(pl.multiple_of(rc * CHUNK, CHUNK), CHUNK)
            for kt in range(SEQ // KTILE):
                rows = slice(kt * KTILE, (kt + 1) * KTILE)
                kb = kk[kt * per : (kt + 1) * per].reshape(KTILE, 2 * HD)
                up = lax.dot_general(kb, qb, NT, preferred_element_type=F32)
                ex = jnp.exp2(s_buf[rows, :] * EXP2C - shift)
                ti = ex * up
                lsum = lsum + jnp.sum(ex, axis=0, keepdims=True)
                tilt = tilt + jnp.sum(ti, axis=0, keepdims=True)
                e_buf[rows, cols] = ex.astype(BF16)
                t_buf[rows, cols] = ti.astype(BF16)
            linv = 1.0 / lsum
            lrow[rc] = jnp.broadcast_to(linv, (8, CHUNK))
            trow[rc] = jnp.broadcast_to(tilt * (1.0 / ROOT) * linv, (8, CHUNK))
            return carry

        lax.fori_loop(0, EARLY, weigh, 0)
        for t in range(SLOTS):
            arrived(vv.at[t, :, 0:HD], v_rs.at[t, 0])
            arrived(vv.at[t, :, HD : 2 * HD], v_rs.at[t, 1])
            remote(vv.at[t], vv.at[SLOTS + t], fv_ss.at[t], fv_rs.at[t], (c, sib)).start()
        lax.fori_loop(EARLY, N_CHUNK, weigh, 0)
        for t in range(SLOTS):
            vT[:, t * TOK : (t + 1) * TOK] = vv[t].T
        for t in range(SLOTS):
            rows = slice((SLOTS + t) * TOK, (SLOTS + t + 1) * TOK)
            remote(vv.at[t], vv.at[SLOTS + t], fv_ss.at[t], fv_rs.at[t], (c, sib)).wait()
            vT[:, rows] = vv[SLOTS + t].T

        def combine(rc, carry):
            cols = pl.ds(pl.multiple_of(rc * CHUNK, CHUNK), CHUNK)
            ov = dot(vT[...], e_buf[:, cols])
            tv = dot(vT[0:HD, :], t_buf[:, cols])
            linv = lrow[rc][0:1, :]
            out = ov[0:HD, :] * linv
            out_t = (ov[HD : 2 * HD, :] + tv * (1.0 / ROOT)) * linv - trow[rc][0:1, :] * out
            oT[rc] = out
            gT[rc] = c_out * out + c_tan * out_t
            return carry

        lax.fori_loop(0, N_CHUNK, combine, 0)

        energy = []
        for rc in range(N_CHUNK):
            g = gT[rc]
            e = jnp.sum(g * g, axis=0, keepdims=True)
            energy += [e[:, 0:128], e[:, 128:256]]
        erecv[mine] = jnp.concatenate(energy, axis=0)
        for plane in range(4):
            for j in range(6):
                idx = plane * 6 + j
                fp = 8 * samp + plane * 2 + core

                @pl.when(mine != idx)
                def _(idx=idx, cp=LOC[plane % 2][j], fp=fp):
                    remote(
                        erecv.at[mine], erecv.at[mine], e_ss.at[idx], e_rs.at[mine], (cp, fp)
                    ).start()

        for t in range(2 * SLOTS):
            kT[:, t * TOK : (t + 1) * TOK] = kk[t, :, 0:HD].T

        def back(rc, carry):
            cols = pl.ds(pl.multiple_of(rc * CHUNK, CHUNK), CHUNK)
            cnT = (gT[rc] * (lrow[rc][0:1, :] * (1.0 / ROOT))).astype(BF16)
            drift = jnp.sum(cnT.astype(F32) * oT[rc], axis=0, keepdims=True)
            for kt in range(SEQ // KTILE):
                rows = slice(kt * KTILE, (kt + 1) * KTILE)
                vb = vv[kt * per : (kt + 1) * per, :, 0:HD].reshape(KTILE, HD)
                dp = dot(vb, cnT)
                ds_buf[rows, cols] = (e_buf[rows, cols].astype(F32) * (dp - drift)).astype(BF16)
            oT[rc] = dot(kT[...], ds_buf[:, cols])
            return carry

        lax.fori_loop(0, N_CHUNK, back, 0)
        for t in range(SLOTS):
            dyq[t] = turn_back(oT[t // 2, :, (t % 2) * TOK : (t % 2 + 1) * TOK].T, t)

        for idx in range(24):

            @pl.when(mine != idx)
            def _(idx=idx):
                arrived(erecv.at[idx], e_rs.at[idx])

        esum = erecv[0]
        for idx in range(1, 24):
            esum = esum + erecv[idx]
        scale = loss_scale / (jnp.sqrt(esum / CHANNELS) + floor_term)
        scale_c = rows_to_cols(scale)
        for t in range(SLOTS):
            qn_buf[t * TOK : (t + 1) * TOK, :] = (
                qq[t, :, HD : 2 * HD].astype(F32) * scale_c[:, t : t + 1]
            ).astype(BF16)
        qn = qn_buf[...]

        def finished(dy, t, i, raw):
            x = raw[t, 0].astype(F32)
            scaled = dy * inv_of(t, i)
            grad = scaled * gain[i : i + 1, :]
            part = jnp.sum(scaled * x, axis=0, keepdims=True)
            return grad.astype(BF16), part, rsum(grad * x)

        ggq = jnp.zeros((1, HD), F32)
        crosses = []
        for t in range(SLOTS):
            cs, fs, own = source(t)
            resq[t], part, cross = finished(dyq[t] * scale_c[:, t : t + 1], t, 0, qraw)
            ggq = ggq + part
            crosses.append(cross)
            push(resq.at[t], retq.at[hl], r_ss.at[0, t], r_rs.at[0, hl], (cs, fs), own)

        xsend[0] = dot(ds_buf[ROWS:SEQ, :], qn).astype(BF16)
        xk = remote(xsend.at[0], xrecv.at[0], x_ss.at[0], x_rs.at[0], (c, sib))
        xk.start()
        for rc in range(N_CHUNK):
            row = jnp.concatenate([scale[2 * rc : 2 * rc + 1], scale[2 * rc + 1 : 2 * rc + 2]], axis=1)
            cn = gT[rc] * (lrow[rc][0:1, :] * row * (1.0 / ROOT))
            cn_buf[2 * rc : 2 * rc + 2] = cn.T.astype(BF16).reshape(2, TOK, HD)
        cn_all = cn_buf[...].reshape(ROWS, HD)
        xsend[1] = dot(e_buf[ROWS:SEQ, :], cn_all).astype(BF16)
        xv = remote(xsend.at[1], xrecv.at[1], x_ss.at[1], x_rs.at[1], (c, sib))
        xv.start()

        dk = dot(ds_buf[0:ROWS, :], qn)
        xk.wait_recv()
        ggk = jnp.zeros((1, HD), F32)
        for t in range(SLOTS):
            rows = slice(t * TOK, (t + 1) * TOK)
            dkt = dk[rows, :] + xrecv[0, rows, :].astype(F32)
            resk[t], part, cross = finished(turn_back(dkt, t), t, 1, kraw)
            ggk = ggk + part
            crosses.append(cross)
        ggsend[...] = jnp.where(sub_id == 0, ggq, ggk)
        for args in gg_copies:
            push(*args)
        lane_id = lax.broadcasted_iota(jnp.int32, (TOK, 128), 1)
        ctile = jnp.zeros((TOK, 128), F32)
        for n, cross in enumerate(crosses):
            ctile = jnp.where(lane_id == n, cross, ctile)
        ctile = ctile.T
        for t in range(SLOTS):
            cs, fs, own = source(t)
            csend[t] = jnp.where(
                sub_id == 0, ctile[t : t + 1, :], ctile[SLOTS + t : SLOTS + t + 1, :]
            )
            push(csend.at[t], cpart.at[hl], p_ss.at[t], p_rs.at[hl], (cs, fs), own)
        for t in range(SLOTS):
            cs, fs, own = source(t)
            push(resk.at[t], retk.at[hl], r_ss.at[1, t], r_rs.at[1, hl], (cs, fs), own)
        dv = dot(e_buf[0:ROWS, :], cn_all)
        xv.wait_recv()
        for t in range(SLOTS):
            cs, fs, own = source(t)
            rows = slice(t * TOK, (t + 1) * TOK)
            resv[t] = ((dv[rows, :] + xrecv[1, rows, :].astype(F32)) * ROOT).astype(BF16)
            push(resv.at[t], retv.at[hl], r_ss.at[2, t], r_rs.at[2, hl], (cs, fs), own)

    for h in range(HEADS_DEV):
        arrived(cpart.at[h], p_rs.at[h])
    crecv[rank] = cpart[0] + cpart[1] + cpart[2]
    cross_copies = []
    for i in range(1, RANKS):
        peer = samp * 8 + (rank + i) % 8
        cross_copies.append(
            remote(crecv.at[rank], crecv.at[rank], c_ss.at[i], c_rs.at[rank], (c, peer))
        )
    for copy in cross_copies:
        copy.start()

    ff_copies = []
    for i in range(N_CTX):
        ff_copies.append(
            (
                ffsend,
                ffrecv.at[feeds[1]],
                ff_ss.at[i],
                ff_rs.at[feeds[1]],
                ((c + i) % N_CTX, f),
            )
        )

    @pl.when(feed == 1)
    def _():
        for n in range(8):
            arrived(ggrecv.at[n], gg_rs.at[n])
        acc = ggrecv[0]
        for n in range(1, 8):
            acc = acc + ggrecv[n]
        ffsend[...] = pltpu.roll(acc, 32 * shard, 1)
        pltpu.make_async_copy(ffsend, ffrecv.at[feeds[1]], ff_rs.at[feeds[1]]).start()
        for args in ff_copies[1:]:
            remote(*args).start()

    stores = [
        pltpu.make_async_copy(src, dst, out_sem.at[n])
        for n, (src, dst) in enumerate(
            (
                (dq_out, dq_hbm),
                (dk_out, dk_hbm),
                (dv_out, dv_hbm),
                (qgg_out, qgg_hbm),
                (kgg_out, kgg_hbm),
            )
        )
    ]
    for h in range(HEADS_DEV):
        arrived(retq.at[h], r_rs.at[0, h])
        arrived(retk.at[h], r_rs.at[1, h])
    for i in range(1, RANKS):
        peer = (rank + i) % 8
        arrived(crecv.at[peer], c_rs.at[peer])
    ctot = crecv[0]
    for i in range(1, RANKS):
        ctot = ctot + crecv[i]
    cmean = rows_to_cols(ctot) / CHANNELS
    for i, (x_ref, ret, out) in enumerate(((q_ref, retq, dq_out), (k_ref, retk, dk_out))):
        pull = cmean[:, i : i + 1] / (statc[:, i : i + 1] + eps_norm)
        for h in range(HEADS_DEV):
            cols = slice(h * HD, (h + 1) * HD)
            out[:, cols] = (ret[h].astype(F32) - x_ref[:, cols].astype(F32) * pull).astype(BF16)
        stores[i].start()

    for h in range(HEADS_DEV):
        arrived(retv.at[h], r_rs.at[2, h])
        dv_out[:, h * HD : (h + 1) * HD] = retv[h]
    stores[2].start()

    for w in range(2):
        some = shard != 3 if w == 0 else shard != 0

        @pl.when(some)
        def _(w=w):
            arrived(ffrecv.at[w], ff_rs.at[w])

        @pl.when(jnp.logical_not(some))
        def _(w=w):
            ffrecv[w] = jnp.zeros((8, 128), F32)

    glane = lax.broadcasted_iota(jnp.int32, (8, 128), 1)
    gg = jnp.where(glane < 32 * shard, ffrecv[1], ffrecv[0])
    qgg_out[...] = gg[0:1, 0:GSH]
    kgg_out[...] = gg[1:2, 0:GSH]
    stores[3].start()
    stores[4].start()

    for copy in stat_copies + cross_copies:
        copy.wait_send()
    for args in tile_copies + meta_copies:
        sent(*args)

    @pl.when(feed == 1)
    def _():
        for args in gain_copies:
            sent(*args)
        for args in ff_copies[1:]:
            remote(*args).wait_send()

    @pl.when(active)
    def _():
        for n in range(2):
            remote(xsend.at[n], xrecv.at[n], x_ss.at[n], x_rs.at[n], (c, sib)).wait_send()
        for args in gg_copies:
            sent(*args)
        for t in range(SLOTS):
            cs, fs, own = source(t)
            sent(csend.at[t], cpart.at[hl], p_ss.at[t], p_rs.at[hl], (cs, fs), own)
            sent(resq.at[t], retq.at[hl], r_ss.at[0, t], r_rs.at[0, hl], (cs, fs), own)
            sent(resk.at[t], retk.at[hl], r_ss.at[1, t], r_rs.at[1, hl], (cs, fs), own)
            sent(resv.at[t], retv.at[hl], r_ss.at[2, t], r_rs.at[2, hl], (cs, fs), own)
        for plane in range(4):
            for j in range(6):
                idx = plane * 6 + j
                fp = 8 * samp + plane * 2 + core

                @pl.when(mine != idx)
                def _(idx=idx, cp=LOC[plane % 2][j], fp=fp):
                    remote(
                        erecv.at[mine], erecv.at[mine], e_ss.at[idx], e_rs.at[mine], (cp, fp)
                    ).wait_send()

    for store in stores:
        store.wait()


def finish(*refs):
    srcs, dsts, held, sem = refs[:5], refs[5:10], refs[10:15], refs[15]
    reads = [pltpu.make_async_copy(srcs[n], held[n], sem.at[0, n]) for n in range(5)]
    writes = [pltpu.make_async_copy(held[n], dsts[n], sem.at[1, n]) for n in range(5)]
    for read in reads:
        read.start()
    for read, write in zip(reads, writes):
        read.wait()
        write.start()
    for write in writes:
        write.wait()


def per_device(
    queries,
    keys,
    values,
    query_tangent,
    key_tangent,
    value_tangent,
    query_gain,
    key_gain,
    time_index,
    shard_order,
):
    width = HEADS_DEV * HD
    vm = pl.BlockSpec(memory_space=pltpu.VMEM)
    hbm = pl.BlockSpec(memory_space=pl.ANY)
    sm = pl.BlockSpec(memory_space=pltpu.SMEM)
    dma = pltpu.SemaphoreType.DMA
    big = jax.ShapeDtypeStruct((TOK, width), BF16)
    scratch = [
        pltpu.VMEM((6, TOK, width), BF16),
        pltpu.VMEM((TOK, width), BF16),
        pltpu.VMEM((TOK, width), BF16),
        pltpu.VMEM((TOK, width), BF16),
        pltpu.VMEM((1, GSH), F32),
        pltpu.VMEM((1, GSH), F32),
        pltpu.VMEM((TOK, 128), F32),
        pltpu.VMEM((TOK, 128), F32),
        pltpu.VMEM((8, 128), F32),
        pltpu.VMEM((2, 8, 128), F32),
        pltpu.VMEM((8, 8, 128), F32),
        pltpu.VMEM((TOK, 128), F32),
        pltpu.VMEM((8, 128), F32),
        pltpu.VMEM((SLOTS, 8, 128), F32),
        pltpu.VMEM((SLOTS, TOK, 128), F32),
        pltpu.VMEM((SLOTS, TOK, 128), F32),
        pltpu.VMEM((SLOTS, TOK, 128), F32),
        pltpu.VMEM((8, 128), F32),
        pltpu.VMEM((SLOTS, 2, TOK, HD), BF16),
        pltpu.VMEM((SLOTS, 2, TOK, HD), BF16),
        pltpu.VMEM((SLOTS, TOK, 256), BF16),
        pltpu.VMEM((2 * SLOTS, TOK, 256), BF16),
        pltpu.VMEM((2 * SLOTS, TOK, 256), BF16),
        pltpu.VMEM((256, SEQ), BF16),
        pltpu.VMEM((128, SEQ), BF16),
        pltpu.VMEM((SEQ, CHUNK), F32),
        pltpu.VMEM((SEQ, ROWS), BF16),
        pltpu.VMEM((SEQ, ROWS), BF16),
        pltpu.VMEM((SEQ, ROWS), BF16),
        pltpu.VMEM((SLOTS, TOK, HD), BF16),
        pltpu.VMEM((ROWS, HD), BF16),
        pltpu.VMEM((N_CHUNK, HD, CHUNK), F32),
        pltpu.VMEM((N_CHUNK, HD, CHUNK), F32),
        pltpu.VMEM((SLOTS, TOK, HD), F32),
        pltpu.VMEM((N_CHUNK, 8, CHUNK), F32),
        pltpu.VMEM((N_CHUNK, 8, CHUNK), F32),
        pltpu.VMEM((24, 8, 128), F32),
        pltpu.VMEM((SLOTS, TOK, HD), BF16),
        pltpu.VMEM((SLOTS, TOK, HD), BF16),
        pltpu.VMEM((SLOTS, TOK, HD), BF16),
        pltpu.VMEM((2, ROWS, HD), BF16),
        pltpu.VMEM((2, ROWS, HD), BF16),
        pltpu.VMEM((3, TOK, HD), BF16),
        pltpu.VMEM((3, TOK, HD), BF16),
        pltpu.VMEM((3, TOK, HD), BF16),
        pltpu.VMEM((8, 8, 128), F32),
        pltpu.VMEM((8, 128), F32),
        pltpu.VMEM((8, 8, 128), F32),
        pltpu.VMEM((8, 128), F32),
        pltpu.VMEM((2, 8, 128), F32),
        pltpu.VMEM((SLOTS, 8, 128), F32),
        pltpu.VMEM((3, 8, 128), F32),
        dma((8,)),
        dma((2,)),
        dma((8,)),
        dma((8,)),
        dma((3,)),
        dma((8,)),
        dma((3, 2)),
        dma((8, 2)),
        dma((3, 2)),
        dma((8, 2)),
        dma((3, 2)),
        dma((8, 2)),
        dma((8,)),
        dma((8,)),
        dma((8,)),
        dma((8,)),
        dma((24,)),
        dma((24,)),
        dma((3, 8)),
        dma((3, 3)),
        dma((2,)),
        dma((2,)),
        dma((8,)),
        dma((8,)),
        dma((2,)),
        dma((8,)),
        dma((16,)),
        dma((2,)),
        dma((8,)),
        dma((3,)),
        dma((6,)),
        dma((5,)),
    ]
    small = jax.ShapeDtypeStruct((1, GSH), F32)
    outs = pl.pallas_call(
        kernel,
        out_shape=(big, big, big, small, small),
        in_specs=[sm, sm] + [hbm] * 6 + [vm] * 2,
        out_specs=(hbm,) * 5,
        scratch_shapes=scratch,
        compiler_params=pltpu.CompilerParams(
            collective_id=0, has_side_effects=True, vmem_limit_bytes=VMEM_LIMIT
        ),
        name="tangent_attention",
    )(
        shard_order,
        time_index,
        queries,
        keys,
        values,
        query_tangent,
        key_tangent,
        value_tangent,
        query_gain.reshape(1, GSH),
        key_gain.reshape(1, GSH),
    )
    outs = pl.pallas_call(
        finish,
        out_shape=(big, big, big, small, small),
        in_specs=[hbm] * 5,
        out_specs=(hbm,) * 5,
        scratch_shapes=[pltpu.VMEM(a.shape, a.dtype) for a in outs] + [dma((2, 5))],
        compiler_params=pltpu.CompilerParams(vmem_limit_bytes=VMEM_LIMIT),
        name="store_results",
    )(*outs)
    return (outs[0], outs[1], outs[2], outs[3].reshape(GSH), outs[4].reshape(GSH))


def solution(mesh):
    placed = (
        P("ctx", "fsdp"),
        P("ctx", "fsdp"),
        P("ctx", "fsdp"),
        P("ctx", "fsdp"),
        P("ctx", "fsdp"),
        P("ctx", "fsdp"),
        P("fsdp"),
        P("fsdp"),
        P(),
        P("ctx"),
    )
    return jax.shard_map(
        per_device,
        mesh=mesh,
        in_specs=placed,
        out_specs=(P("ctx", "fsdp"), P("ctx", "fsdp"), P("ctx", "fsdp"), P("fsdp"), P("fsdp")),
        check_vma=False,
    )
```

```python
import math

import jax
import jax.numpy as jnp
from jax import lax
from jax.experimental import pallas as pl
from jax.experimental.pallas import tpu as pltpu
from jax.sharding import PartitionSpec as P

MESH = pl.DeviceIdType.MESH
F32 = jnp.float32
BF16 = jnp.bfloat16

HD = 128
TOK = 128
STEPS = 1000
CHANNELS = 3072
HEADS_DEV = 3
N_CTX = 16
N_FSDP = 32
RANKS = 8
SAMPLES = 4
SLOTS = 8
ROWS = SLOTS * TOK
SEQ = 2 * ROWS
GSH = 96
CHUNK = 256
N_CHUNK = ROWS // CHUNK
KTILE = 512
EARLY = 3
VMEM_LIMIT = 63 * 1024 * 1024

eps_norm = 1e-06
loss_scale = 256.0
floor_term = 0.1
ROOT = math.sqrt(HD)
EXP2C = math.log2(math.e) / ROOT

LOC = ((1, 3, 10, 8, 5, 15), (6, 4, 15, 13, 10, 0))

NT = (((1,), (1,)), ((), ()))


def dot(a, b):
    return jnp.dot(a, b, preferred_element_type=F32)


def cols_to_rows(cols):
    lane = lax.broadcasted_iota(jnp.int32, (TOK, 128), 1)
    tile = jnp.zeros((TOK, 128), F32)
    for i, col in enumerate(cols):
        tile = jnp.where(lane == i, col, tile)
    return tile.T[0:8, :]


def rows_to_cols(rows):
    return jnp.concatenate([rows] * 16, axis=0).T


def kernel(
    so_ref,
    ti_ref,
    q_hbm,
    k_hbm,
    v_hbm,
    qt_hbm,
    kt_hbm,
    vt_hbm,
    qg_ref,
    kg_ref,
    dq_hbm,
    dk_hbm,
    dv_hbm,
    qgg_hbm,
    kgg_hbm,
    loaded,
    dq_out,
    dk_out,
    dv_out,
    qgg_out,
    kgg_out,
    cr,
    sr,
    gsend,
    grecv,
    strecv,
    statc,
    msend,
    mrecv,
    mcol,
    cosT,
    sinT,
    gain,
    qraw,
    kraw,
    qq,
    kk,
    vv,
    vT,
    kT,
    s_buf,
    t_buf,
    e_buf,
    ds_buf,
    cn_buf,
    qn_buf,
    oT,
    gT,
    dyq,
    lrow,
    trow,
    erecv,
    resq,
    resk,
    resv,
    xsend,
    xrecv,
    retq,
    retk,
    retv,
    crecv,
    ggsend,
    ggrecv,
    ffsend,
    ffrecv,
    csend,
    cpart,
    g_ss,
    g_rs,
    st_ss,
    st_rs,
    m_ss,
    m_rs,
    v_ss,
    v_rs,
    q_ss,
    q_rs,
    k_ss,
    k_rs,
    fk_ss,
    fk_rs,
    fv_ss,
    fv_rs,
    e_ss,
    e_rs,
    r_ss,
    r_rs,
    x_ss,
    x_rs,
    c_ss,
    c_rs,
    gg_ss,
    gg_rs,
    ff_ss,
    ff_rs,
    p_ss,
    p_rs,
    in_sem,
    out_sem,
):
    q_ref, k_ref, v_ref, qt_ref, kt_ref, vt_ref = (loaded.at[n] for n in range(6))
    c = lax.axis_index("ctx")
    f = lax.axis_index("fsdp")
    samp = f // 8
    rank = f % 8
    ylo = (f // 2) % 2
    core = f % 2
    base = f - core
    sib = base + (1 - core)
    half = c % 2
    slot = c // 2

    dests = []
    for h in range(HEADS_DEV):
        a, b = LOC[0][h], LOC[0][3 + h]
        d, e = LOC[1][h], LOC[1][3 + h]
        cd = a + core * (b - a) + ylo * (d - a) + core * ylo * (e - d - b + a)
        fd = base + half
        dests.append((cd, fd, jnp.logical_and(cd == c, fd == f)))

    act = 0
    jj = 0
    for j in range(6):
        hit = jnp.where(c == LOC[0][j] + ylo * (LOC[1][j] - LOC[0][j]), 1, 0)
        act = act + hit
        jj = jj + j * hit
    active = act == 1
    hcore = jj // 3
    hl = jj % 3
    src_f = base + hcore

    def source(t):
        cs = 2 * t + core
        return cs, src_f, jnp.logical_and(cs == c, src_f == f)

    def remote(src, dst, ss, rs, dev):
        return pltpu.make_async_remote_copy(
            src_ref=src, dst_ref=dst, send_sem=ss, recv_sem=rs, device_id=dev, device_id_type=MESH
        )

    def push(src, dst, ss, rs, dev, own):
        @pl.when(own)
        def _():
            pltpu.make_async_copy(src, dst, rs).start()

        @pl.when(jnp.logical_not(own))
        def _():
            remote(src, dst, ss, rs, dev).start()

    def sent(src, dst, ss, rs, dev, own):
        @pl.when(jnp.logical_not(own))
        def _():
            remote(src, dst, ss, rs, dev).wait_send()

    def arrived(dst, rs):
        pltpu.make_async_copy(dst, dst, rs).wait()

    own_rank, shard = f // 4, f % 4
    head_rank = (rank // 4) * 4 + ylo * 2 + hcore
    o_ylo, o_core = (own_rank // 2) % 2, own_rank % 2
    feeds = []
    for w in range(2):
        hit = 0
        for h in range(HEADS_DEV):
            a, b = LOC[0][h], LOC[0][3 + h]
            d, e = LOC[1][h], LOC[1][3 + h]
            at = a + o_core * (b - a) + o_ylo * (d - a) + o_core * o_ylo * (e - d - b + a)
            hit = hit + jnp.where(jnp.logical_and(at == c, shard == h + w), 1, 0)
        feeds.append(hit)
    fed = []
    for s in range(SAMPLES):
        for u in range(2):
            fed.append((2 * s + own_rank // 4) * 4 + o_ylo * 2 + u)

    barrier = pltpu.get_barrier_semaphore()

    def greet(dev, own):
        @pl.when(jnp.logical_not(own))
        def _():
            pl.semaphore_signal(barrier, inc=1, device_id=dev, device_id_type=MESH)

    for i in range(1, RANKS):
        pl.semaphore_signal(
            barrier, inc=1, device_id=(c, samp * 8 + (rank + i) % 8), device_id_type=MESH
        )

    @pl.when(active)
    def _():
        for t in range(SLOTS):
            cs, fs, own = source(t)
            greet((cs, fs), own)
        for w in range(2):
            fo = 4 * head_rank + hl + w
            greet((c, fo), fo == f)

    loads = [
        pltpu.make_async_copy(src, loaded.at[n], in_sem.at[n])
        for n, src in enumerate((q_hbm, k_hbm, v_hbm, qt_hbm, kt_hbm, vt_hbm))
    ]
    for load in loads:
        load.start()

    m_id = lax.broadcasted_iota(jnp.int32, (8, 128), 1) % 64
    freq = jnp.full((8, 128), 1.0, F32)
    for bit in range(6):
        factor = 10000.0 ** (-(2.0**bit) / 64.0)
        freq = freq * jnp.where((m_id // (2**bit)) % 2 == 1, factor, 1.0)
    row_id = lax.broadcasted_iota(jnp.int32, (TOK, 128), 0)
    angle = row_id.astype(F32) * freq[0:1, :]
    cr[...] = jnp.cos(angle)
    sr[...] = jnp.sin(angle)
    gsend[...] = jnp.zeros((8, 128), F32)
    gsend[0:1, 0:GSH] = qg_ref[...]
    gsend[1:2, 0:GSH] = kg_ref[...]

    for load in loads:
        load.wait()
    qx = q_ref[...].astype(F32)
    kx = k_ref[...].astype(F32)
    qdx = qt_ref[...].astype(F32)
    kdx = kt_ref[...].astype(F32)

    def rsum(x):
        return jnp.sum(x, axis=1, keepdims=True)

    strecv[rank] = cols_to_rows([rsum(qx * qx), rsum(kx * kx), rsum(qx * qdx), rsum(kx * kdx)])

    own_heads = 0
    for cd, fd, own in dests:
        own_heads = own_heads + jnp.where(own, 1, 0)
    own_fed = 0
    for fd in fed:
        own_fed = own_fed + jnp.where(fd == f, 1, 0)
    feed = feeds[0] + feeds[1]
    pl.semaphore_wait(
        barrier, (RANKS - 1) + (HEADS_DEV - own_heads) + feed * (8 - own_fed)
    )

    stat_copies = []
    for i in range(1, RANKS):
        peer = samp * 8 + (rank + i) % 8
        stat_copies.append(
            remote(strecv.at[rank], strecv.at[rank], st_ss.at[i], st_rs.at[rank], (c, peer))
        )
    for copy in stat_copies:
        copy.start()
    gain_copies = []
    for n, fd in enumerate(fed):
        gain_copies.append((gsend, grecv.at[feeds[1]], g_ss.at[n], g_rs.at[feeds[1]], (c, fd), fd == f))

    @pl.when(feed == 1)
    def _():
        for args in gain_copies:
            push(*args)

    tile_copies = []
    for pair, dst, ss, rs in (
        ((k_ref, kt_ref), lambda n: kraw.at[slot, n], k_ss, k_rs),
        ((q_ref, qt_ref), lambda n: qraw.at[slot, n], q_ss, q_rs),
        ((v_ref, vt_ref), lambda n: vv.at[slot, :, n * HD : (n + 1) * HD], v_ss, v_rs),
    ):
        for h, (cd, fd, own) in enumerate(dests):
            for n, ref in enumerate(pair):
                src = ref.at[:, h * HD : (h + 1) * HD]
                tile_copies.append((src, dst(n), ss.at[h, n], rs.at[slot, n], (cd, fd), own))
    ahead = 4 * HEADS_DEV
    for args in tile_copies[:ahead]:
        push(*args)

    for i in range(1, RANKS):
        peer = (rank + i) % 8
        arrived(strecv.at[peer], st_rs.at[peer])
    total = strecv[0]
    for i in range(1, RANKS):
        total = total + strecv[i]
    means = total / CHANNELS
    start = jnp.full((8, 128), so_ref[0] * TOK, jnp.int32).astype(F32)
    sub_id = lax.broadcasted_iota(jnp.int32, (8, 128), 0)
    msend[...] = jnp.where(sub_id == 4, start, means)
    meta_copies = []
    for h, (cd, fd, own) in enumerate(dests):
        meta_copies.append((msend, mrecv.at[slot], m_ss.at[h], m_rs.at[slot], (cd, fd), own))
    for args in meta_copies + tile_copies[ahead:]:
        push(*args)
    statc[...] = rows_to_cols(means)

    mine = (rank // 2) * 6 + jj
    gg_copies = []
    for w in range(2):
        fo = 4 * head_rank + hl + w
        dst = ggrecv.at[samp * 2 + core]
        gg_copies.append((ggsend, dst, gg_ss.at[w], gg_rs.at[samp * 2 + core], (c, fo), fo == f))

    @pl.when(active)
    def _():
        for w in range(2):
            arrived(grecv.at[w], g_rs.at[w])
        lane8 = lax.broadcasted_iota(jnp.int32, (8, 128), 1)
        gain[...] = jnp.where(
            lane8 < GSH - 32 * hl,
            pltpu.roll(grecv[0], (128 - 32 * hl) % 128, 1),
            pltpu.roll(grecv[1], GSH - 32 * hl, 1),
        )
        sign = jnp.where(lax.broadcasted_iota(jnp.int32, (TOK, 128), 1) < 64, -1.0, 1.0)

        def turn(x, t):
            return x * cosT[t] + pltpu.roll(x, 64, 1) * sinT[t]

        def turn_back(x, t):
            return x * cosT[t] - pltpu.roll(x, 64, 1) * sinT[t]

        def inv_of(t, i):
            return lax.rsqrt(mcol[t, :, i : i + 1] + eps_norm)

        def normed(raw, t, i):
            x = raw[t, 0].astype(F32)
            dx = raw[t, 1].astype(F32)
            inv = inv_of(t, i)
            grow = gain[i : i + 1, :]
            cross = mcol[t, :, i + 2 : i + 3]
            y = x * inv * grow
            yt = (dx * inv - x * (inv * inv * inv) * cross) * grow
            return turn(y, t).astype(BF16), turn(yt, t).astype(BF16)

        def take_keys(t):
            arrived(mrecv.at[t], m_rs.at[t])
            at = mrecv[t][4:5, :] * freq
            cb = jnp.cos(at)[0:1, :]
            sb = jnp.sin(at)[0:1, :]
            mcol[t] = rows_to_cols(mrecv[t])
            cosT[t] = cb * cr[...] - sb * sr[...]
            sinT[t] = sign * (sb * cr[...] + cb * sr[...])
            for n in range(2):
                arrived(kraw.at[t, n], k_rs.at[t, n])
            y, yt = normed(kraw, t, 1)
            kk[t, :, 0:HD] = y
            kk[t, :, HD : 2 * HD] = yt
            remote(kk.at[t], kk.at[SLOTS + t], fk_ss.at[t], fk_rs.at[t], (c, sib)).start()

        def take_queries(t):
            for n in range(2):
                arrived(qraw.at[t, n], q_rs.at[t, n])
            y, yt = normed(qraw, t, 0)
            qq[t, :, 0:HD] = yt
            qq[t, :, HD : 2 * HD] = y

        for t in range(SLOTS - 1, 0, -1):
            take_keys(t)
        for t in range(SLOTS - 1, 0, -1):
            take_queries(t)
        take_keys(0)
        take_queries(0)
        for t in range(SLOTS):
            remote(kk.at[t], kk.at[SLOTS + t], fk_ss.at[t], fk_rs.at[t], (c, sib)).wait()

        t_val = jnp.full((8, 128), ti_ref[samp], jnp.int32).astype(F32)
        t_ang = (0.5 * math.pi) * (t_val + 0.5) / STEPS
        sin_a = jnp.sin(t_ang)[0:1, :]
        cos_a = jnp.cos(t_ang)[0:1, :]
        c_out = jnp.concatenate([sin_a * cos_a] * 2, axis=1)
        c_tan = jnp.concatenate([cos_a * cos_a] * 2, axis=1)

        per = KTILE // TOK

        def weigh(rc, carry):
            qb = qq[pl.ds(rc * 2, 2)].reshape(CHUNK, 2 * HD)
            peak = jnp.full((1, CHUNK), -jnp.inf, F32)
            for kt in range(SEQ // KTILE):
                kb = kk[kt * per : (kt + 1) * per, :, 0:HD].reshape(KTILE, HD)
                sc = lax.dot_general(kb, qb[:, HD : 2 * HD], NT, preferred_element_type=F32)
                s_buf[kt * KTILE : (kt + 1) * KTILE, :] = sc
                peak = jnp.maximum(peak, jnp.max(sc, axis=0, keepdims=True))
            shift = peak * EXP2C
            lsum = jnp.zeros((1, CHUNK), F32)
            tilt = jnp.zeros((1, CHUNK), F32)
            cols = pl.ds(pl.multiple_of(rc * CHUNK, CHUNK), CHUNK)
            for kt in range(SEQ // KTILE):
                rows = slice(kt * KTILE, (kt + 1) * KTILE)
                kb = kk[kt * per : (kt + 1) * per].reshape(KTILE, 2 * HD)
                up = lax.dot_general(kb, qb, NT, preferred_element_type=F32)
                ex = jnp.exp2(s_buf[rows, :] * EXP2C - shift)
                ti = ex * up
                lsum = lsum + jnp.sum(ex, axis=0, keepdims=True)
                tilt = tilt + jnp.sum(ti, axis=0, keepdims=True)
                e_buf[rows, cols] = ex.astype(BF16)
                t_buf[rows, cols] = ti.astype(BF16)
            linv = 1.0 / lsum
            lrow[rc] = jnp.broadcast_to(linv, (8, CHUNK))
            trow[rc] = jnp.broadcast_to(tilt * (1.0 / ROOT) * linv, (8, CHUNK))
            return carry

        lax.fori_loop(0, EARLY, weigh, 0)
        for t in range(SLOTS):
            arrived(vv.at[t, :, 0:HD], v_rs.at[t, 0])
            arrived(vv.at[t, :, HD : 2 * HD], v_rs.at[t, 1])
            remote(vv.at[t], vv.at[SLOTS + t], fv_ss.at[t], fv_rs.at[t], (c, sib)).start()
        lax.fori_loop(EARLY, N_CHUNK, weigh, 0)
        for t in range(SLOTS):
            vT[:, t * TOK : (t + 1) * TOK] = vv[t].T
        for t in range(SLOTS):
            rows = slice((SLOTS + t) * TOK, (SLOTS + t + 1) * TOK)
            remote(vv.at[t], vv.at[SLOTS + t], fv_ss.at[t], fv_rs.at[t], (c, sib)).wait()
            vT[:, rows] = vv[SLOTS + t].T

        def combine(rc, carry):
            cols = pl.ds(pl.multiple_of(rc * CHUNK, CHUNK), CHUNK)
            ov = dot(vT[...], e_buf[:, cols])
            tv = dot(vT[0:HD, :], t_buf[:, cols])
            linv = lrow[rc][0:1, :]
            out = ov[0:HD, :] * linv
            out_t = (ov[HD : 2 * HD, :] + tv * (1.0 / ROOT)) * linv - trow[rc][0:1, :] * out
            oT[rc] = out
            gT[rc] = c_out * out + c_tan * out_t
            return carry

        lax.fori_loop(0, N_CHUNK, combine, 0)

        energy = []
        for rc in range(N_CHUNK):
            g = gT[rc]
            e = jnp.sum(g * g, axis=0, keepdims=True)
            energy += [e[:, 0:128], e[:, 128:256]]
        erecv[mine] = jnp.concatenate(energy, axis=0)
        for plane in range(4):
            for j in range(6):
                idx = plane * 6 + j
                fp = 8 * samp + plane * 2 + core

                @pl.when(mine != idx)
                def _(idx=idx, cp=LOC[plane % 2][j], fp=fp):
                    remote(
                        erecv.at[mine], erecv.at[mine], e_ss.at[idx], e_rs.at[mine], (cp, fp)
                    ).start()

        for t in range(2 * SLOTS):
            kT[:, t * TOK : (t + 1) * TOK] = kk[t, :, 0:HD].T

        def back(rc, carry):
            cols = pl.ds(pl.multiple_of(rc * CHUNK, CHUNK), CHUNK)
            cnT = (gT[rc] * (lrow[rc][0:1, :] * (1.0 / ROOT))).astype(BF16)
            drift = jnp.sum(cnT.astype(F32) * oT[rc], axis=0, keepdims=True)
            for kt in range(SEQ // KTILE):
                rows = slice(kt * KTILE, (kt + 1) * KTILE)
                vb = vv[kt * per : (kt + 1) * per, :, 0:HD].reshape(KTILE, HD)
                dp = dot(vb, cnT)
                ds_buf[rows, cols] = (e_buf[rows, cols].astype(F32) * (dp - drift)).astype(BF16)
            oT[rc] = dot(kT[...], ds_buf[:, cols])
            return carry

        lax.fori_loop(0, N_CHUNK, back, 0)
        for t in range(SLOTS):
            dyq[t] = turn_back(oT[t // 2, :, (t % 2) * TOK : (t % 2 + 1) * TOK].T, t)

        for idx in range(24):

            @pl.when(mine != idx)
            def _(idx=idx):
                arrived(erecv.at[idx], e_rs.at[idx])

        esum = erecv[0]
        for idx in range(1, 24):
            esum = esum + erecv[idx]
        scale = loss_scale / (jnp.sqrt(esum / CHANNELS) + floor_term)
        scale_c = rows_to_cols(scale)
        for t in range(SLOTS):
            qn_buf[t * TOK : (t + 1) * TOK, :] = (
                qq[t, :, HD : 2 * HD].astype(F32) * scale_c[:, t : t + 1]
            ).astype(BF16)
        qn = qn_buf[...]

        def finished(dy, t, i, raw):
            x = raw[t, 0].astype(F32)
            scaled = dy * inv_of(t, i)
            grad = scaled * gain[i : i + 1, :]
            part = jnp.sum(scaled * x, axis=0, keepdims=True)
            return grad.astype(BF16), part, rsum(grad * x)

        ggq = jnp.zeros((1, HD), F32)
        crosses = []
        for t in range(SLOTS):
            cs, fs, own = source(t)
            resq[t], part, cross = finished(dyq[t] * scale_c[:, t : t + 1], t, 0, qraw)
            ggq = ggq + part
            crosses.append(cross)
            push(resq.at[t], retq.at[hl], r_ss.at[0, t], r_rs.at[0, hl], (cs, fs), own)

        xsend[0] = dot(ds_buf[ROWS:SEQ, :], qn).astype(BF16)
        xk = remote(xsend.at[0], xrecv.at[0], x_ss.at[0], x_rs.at[0], (c, sib))
        xk.start()
        for rc in range(N_CHUNK):
            row = jnp.concatenate([scale[2 * rc : 2 * rc + 1], scale[2 * rc + 1 : 2 * rc + 2]], axis=1)
            cn = gT[rc] * (lrow[rc][0:1, :] * row * (1.0 / ROOT))
            cn_buf[2 * rc : 2 * rc + 2] = cn.T.astype(BF16).reshape(2, TOK, HD)
        cn_all = cn_buf[...].reshape(ROWS, HD)
        xsend[1] = dot(e_buf[ROWS:SEQ, :], cn_all).astype(BF16)
        xv = remote(xsend.at[1], xrecv.at[1], x_ss.at[1], x_rs.at[1], (c, sib))
        xv.start()

        dk = dot(ds_buf[0:ROWS, :], qn)
        xk.wait_recv()
        ggk = jnp.zeros((1, HD), F32)
        for t in range(SLOTS):
            rows = slice(t * TOK, (t + 1) * TOK)
            dkt = dk[rows, :] + xrecv[0, rows, :].astype(F32)
            resk[t], part, cross = finished(turn_back(dkt, t), t, 1, kraw)
            ggk = ggk + part
            crosses.append(cross)
        ggsend[...] = jnp.where(sub_id == 0, ggq, ggk)
        for args in gg_copies:
            push(*args)
        lane_id = lax.broadcasted_iota(jnp.int32, (TOK, 128), 1)
        ctile = jnp.zeros((TOK, 128), F32)
        for n, cross in enumerate(crosses):
            ctile = jnp.where(lane_id == n, cross, ctile)
        ctile = ctile.T
        for t in range(SLOTS):
            cs, fs, own = source(t)
            csend[t] = jnp.where(
                sub_id == 0, ctile[t : t + 1, :], ctile[SLOTS + t : SLOTS + t + 1, :]
            )
            push(csend.at[t], cpart.at[hl], p_ss.at[t], p_rs.at[hl], (cs, fs), own)
        for t in range(SLOTS):
            cs, fs, own = source(t)
            push(resk.at[t], retk.at[hl], r_ss.at[1, t], r_rs.at[1, hl], (cs, fs), own)
        dv = dot(e_buf[0:ROWS, :], cn_all)
        xv.wait_recv()
        for t in range(SLOTS):
            cs, fs, own = source(t)
            rows = slice(t * TOK, (t + 1) * TOK)
            resv[t] = ((dv[rows, :] + xrecv[1, rows, :].astype(F32)) * ROOT).astype(BF16)
            push(resv.at[t], retv.at[hl], r_ss.at[2, t], r_rs.at[2, hl], (cs, fs), own)

    ff_copies = []
    for i in range(N_CTX):
        ff_copies.append(
            (
                ffsend,
                ffrecv.at[feeds[1]],
                ff_ss.at[i],
                ff_rs.at[feeds[1]],
                ((c + i) % N_CTX, f),
            )
        )

    @pl.when(feed == 1)
    def _():
        for n in range(8):
            arrived(ggrecv.at[n], gg_rs.at[n])
        acc = ggrecv[0]
        for n in range(1, 8):
            acc = acc + ggrecv[n]
        ffsend[...] = pltpu.roll(acc, 32 * shard, 1)
        pltpu.make_async_copy(ffsend, ffrecv.at[feeds[1]], ff_rs.at[feeds[1]]).start()
        for args in ff_copies[1:]:
            remote(*args).start()

    for h in range(HEADS_DEV):
        arrived(cpart.at[h], p_rs.at[h])
    crecv[rank] = cpart[0] + cpart[1] + cpart[2]
    cross_copies = []
    for i in range(1, RANKS):
        peer = samp * 8 + (rank + i) % 8
        cross_copies.append(
            remote(crecv.at[rank], crecv.at[rank], c_ss.at[i], c_rs.at[rank], (c, peer))
        )
    for copy in cross_copies:
        copy.start()

    stores = [
        pltpu.make_async_copy(src, dst, out_sem.at[n])
        for n, (src, dst) in enumerate(
            (
                (dq_out, dq_hbm),
                (dk_out, dk_hbm),
                (dv_out, dv_hbm),
                (qgg_out, qgg_hbm),
                (kgg_out, kgg_hbm),
            )
        )
    ]
    for h in range(HEADS_DEV):
        arrived(retq.at[h], r_rs.at[0, h])
        arrived(retk.at[h], r_rs.at[1, h])
    for i in range(1, RANKS):
        peer = (rank + i) % 8
        arrived(crecv.at[peer], c_rs.at[peer])
    ctot = crecv[0]
    for i in range(1, RANKS):
        ctot = ctot + crecv[i]
    cmean = rows_to_cols(ctot) / CHANNELS
    for i, (x_ref, ret, out) in enumerate(((q_ref, retq, dq_out), (k_ref, retk, dk_out))):
        pull = cmean[:, i : i + 1] / (statc[:, i : i + 1] + eps_norm)
        for h in range(HEADS_DEV):
            cols = slice(h * HD, (h + 1) * HD)
            out[:, cols] = (ret[h].astype(F32) - x_ref[:, cols].astype(F32) * pull).astype(BF16)
        stores[i].start()

    for h in range(HEADS_DEV):
        arrived(retv.at[h], r_rs.at[2, h])
        dv_out[:, h * HD : (h + 1) * HD] = retv[h]
    stores[2].start()

    for w in range(2):
        some = shard != 3 if w == 0 else shard != 0

        @pl.when(some)
        def _(w=w):
            arrived(ffrecv.at[w], ff_rs.at[w])

        @pl.when(jnp.logical_not(some))
        def _(w=w):
            ffrecv[w] = jnp.zeros((8, 128), F32)

    glane = lax.broadcasted_iota(jnp.int32, (8, 128), 1)
    gg = jnp.where(glane < 32 * shard, ffrecv[1], ffrecv[0])
    qgg_out[...] = gg[0:1, 0:GSH]
    kgg_out[...] = gg[1:2, 0:GSH]
    stores[3].start()
    stores[4].start()

    for copy in stat_copies + cross_copies:
        copy.wait_send()
    for args in tile_copies + meta_copies:
        sent(*args)

    @pl.when(feed == 1)
    def _():
        for args in gain_copies:
            sent(*args)
        for args in ff_copies[1:]:
            remote(*args).wait_send()

    @pl.when(active)
    def _():
        for n in range(2):
            remote(xsend.at[n], xrecv.at[n], x_ss.at[n], x_rs.at[n], (c, sib)).wait_send()
        for args in gg_copies:
            sent(*args)
        for t in range(SLOTS):
            cs, fs, own = source(t)
            sent(csend.at[t], cpart.at[hl], p_ss.at[t], p_rs.at[hl], (cs, fs), own)
            sent(resq.at[t], retq.at[hl], r_ss.at[0, t], r_rs.at[0, hl], (cs, fs), own)
            sent(resk.at[t], retk.at[hl], r_ss.at[1, t], r_rs.at[1, hl], (cs, fs), own)
            sent(resv.at[t], retv.at[hl], r_ss.at[2, t], r_rs.at[2, hl], (cs, fs), own)
        for plane in range(4):
            for j in range(6):
                idx = plane * 6 + j
                fp = 8 * samp + plane * 2 + core

                @pl.when(mine != idx)
                def _(idx=idx, cp=LOC[plane % 2][j], fp=fp):
                    remote(
                        erecv.at[mine], erecv.at[mine], e_ss.at[idx], e_rs.at[mine], (cp, fp)
                    ).wait_send()

    for store in stores:
        store.wait()


def finish(*refs):
    srcs, dsts, held, sem = refs[:5], refs[5:10], refs[10:15], refs[15]
    reads = [pltpu.make_async_copy(srcs[n], held[n], sem.at[0, n]) for n in range(5)]
    writes = [pltpu.make_async_copy(held[n], dsts[n], sem.at[1, n]) for n in range(5)]
    for read in reads:
        read.start()
    for read, write in zip(reads, writes):
        read.wait()
        write.start()
    for write in writes:
        write.wait()


def per_device(
    queries,
    keys,
    values,
    query_tangent,
    key_tangent,
    value_tangent,
    query_gain,
    key_gain,
    time_index,
    shard_order,
):
    width = HEADS_DEV * HD
    vm = pl.BlockSpec(memory_space=pltpu.VMEM)
    hbm = pl.BlockSpec(memory_space=pl.ANY)
    sm = pl.BlockSpec(memory_space=pltpu.SMEM)
    dma = pltpu.SemaphoreType.DMA
    big = jax.ShapeDtypeStruct((TOK, width), BF16)
    scratch = [
        pltpu.VMEM((6, TOK, width), BF16),
        pltpu.VMEM((TOK, width), BF16),
        pltpu.VMEM((TOK, width), BF16),
        pltpu.VMEM((TOK, width), BF16),
        pltpu.VMEM((1, GSH), F32),
        pltpu.VMEM((1, GSH), F32),
        pltpu.VMEM((TOK, 128), F32),
        pltpu.VMEM((TOK, 128), F32),
        pltpu.VMEM((8, 128), F32),
        pltpu.VMEM((2, 8, 128), F32),
        pltpu.VMEM((8, 8, 128), F32),
        pltpu.VMEM((TOK, 128), F32),
        pltpu.VMEM((8, 128), F32),
        pltpu.VMEM((SLOTS, 8, 128), F32),
        pltpu.VMEM((SLOTS, TOK, 128), F32),
        pltpu.VMEM((SLOTS, TOK, 128), F32),
        pltpu.VMEM((SLOTS, TOK, 128), F32),
        pltpu.VMEM((8, 128), F32),
        pltpu.VMEM((SLOTS, 2, TOK, HD), BF16),
        pltpu.VMEM((SLOTS, 2, TOK, HD), BF16),
        pltpu.VMEM((SLOTS, TOK, 256), BF16),
        pltpu.VMEM((2 * SLOTS, TOK, 256), BF16),
        pltpu.VMEM((2 * SLOTS, TOK, 256), BF16),
        pltpu.VMEM((256, SEQ), BF16),
        pltpu.VMEM((128, SEQ), BF16),
        pltpu.VMEM((SEQ, CHUNK), F32),
        pltpu.VMEM((SEQ, ROWS), BF16),
        pltpu.VMEM((SEQ, ROWS), BF16),
        pltpu.VMEM((SEQ, ROWS), BF16),
        pltpu.VMEM((SLOTS, TOK, HD), BF16),
        pltpu.VMEM((ROWS, HD), BF16),
        pltpu.VMEM((N_CHUNK, HD, CHUNK), F32),
        pltpu.VMEM((N_CHUNK, HD, CHUNK), F32),
        pltpu.VMEM((SLOTS, TOK, HD), F32),
        pltpu.VMEM((N_CHUNK, 8, CHUNK), F32),
        pltpu.VMEM((N_CHUNK, 8, CHUNK), F32),
        pltpu.VMEM((24, 8, 128), F32),
        pltpu.VMEM((SLOTS, TOK, HD), BF16),
        pltpu.VMEM((SLOTS, TOK, HD), BF16),
        pltpu.VMEM((SLOTS, TOK, HD), BF16),
        pltpu.VMEM((2, ROWS, HD), BF16),
        pltpu.VMEM((2, ROWS, HD), BF16),
        pltpu.VMEM((3, TOK, HD), BF16),
        pltpu.VMEM((3, TOK, HD), BF16),
        pltpu.VMEM((3, TOK, HD), BF16),
        pltpu.VMEM((8, 8, 128), F32),
        pltpu.VMEM((8, 128), F32),
        pltpu.VMEM((8, 8, 128), F32),
        pltpu.VMEM((8, 128), F32),
        pltpu.VMEM((2, 8, 128), F32),
        pltpu.VMEM((SLOTS, 8, 128), F32),
        pltpu.VMEM((3, 8, 128), F32),
        dma((8,)),
        dma((2,)),
        dma((8,)),
        dma((8,)),
        dma((3,)),
        dma((8,)),
        dma((3, 2)),
        dma((8, 2)),
        dma((3, 2)),
        dma((8, 2)),
        dma((3, 2)),
        dma((8, 2)),
        dma((8,)),
        dma((8,)),
        dma((8,)),
        dma((8,)),
        dma((24,)),
        dma((24,)),
        dma((3, 8)),
        dma((3, 3)),
        dma((2,)),
        dma((2,)),
        dma((8,)),
        dma((8,)),
        dma((2,)),
        dma((8,)),
        dma((16,)),
        dma((2,)),
        dma((8,)),
        dma((3,)),
        dma((6,)),
        dma((5,)),
    ]
    small = jax.ShapeDtypeStruct((1, GSH), F32)
    outs = pl.pallas_call(
        kernel,
        out_shape=(big, big, big, small, small),
        in_specs=[sm, sm] + [hbm] * 6 + [vm] * 2,
        out_specs=(hbm,) * 5,
        scratch_shapes=scratch,
        compiler_params=pltpu.CompilerParams(
            collective_id=0, has_side_effects=True, vmem_limit_bytes=VMEM_LIMIT
        ),
        name="tangent_attention",
    )(
        shard_order,
        time_index,
        queries,
        keys,
        values,
        query_tangent,
        key_tangent,
        value_tangent,
        query_gain.reshape(1, GSH),
        key_gain.reshape(1, GSH),
    )
    outs = pl.pallas_call(
        finish,
        out_shape=(big, big, big, small, small),
        in_specs=[hbm] * 5,
        out_specs=(hbm,) * 5,
        scratch_shapes=[pltpu.VMEM(a.shape, a.dtype) for a in outs] + [dma((2, 5))],
        compiler_params=pltpu.CompilerParams(vmem_limit_bytes=VMEM_LIMIT),
        name="store_results",
    )(*outs)
    return (outs[0], outs[1], outs[2], outs[3].reshape(GSH), outs[4].reshape(GSH))


def solution(mesh):
    placed = (
        P("ctx", "fsdp"),
        P("ctx", "fsdp"),
        P("ctx", "fsdp"),
        P("ctx", "fsdp"),
        P("ctx", "fsdp"),
        P("ctx", "fsdp"),
        P("fsdp"),
        P("fsdp"),
        P(),
        P("ctx"),
    )
    return jax.shard_map(
        per_device,
        mesh=mesh,
        in_specs=placed,
        out_specs=(P("ctx", "fsdp"), P("ctx", "fsdp"), P("ctx", "fsdp"), P("fsdp"), P("fsdp")),
        check_vma=False,
    )
```
